128 devices in a mesh: ctx: 16 (over z_lo, y, core), fsdp: 8 (over z_hi, x).
Axes of the slice: x: 4, y: 4, z: 4 (z_hi: 2, z_lo: 2; z = z_hi * 2 + z_lo), core: 2. Of those that a mesh axis runs over, the one named last changes fastest.
Arguments:
- layer_input: bfloat16 [6144, 2048], P('ctx', 'fsdp'), may hold values from -6 to 6
- norm_gain: bfloat16 [2048], P('fsdp'), may hold values from 0.5 to 1.5
- norm_bias: bfloat16 [2048], P('fsdp'), may hold values from -1.75 to 1.75
- query_weight: bfloat16 [2048, 2048], P(None, 'fsdp'), may hold values from -0.125 to 0.125
- query_bias: bfloat16 [2048], P('fsdp'), may hold values from -1.75 to 1.75
- key_weight: bfloat16 [2048, 2048], P(None, 'fsdp'), may hold values from -0.125 to 0.125
- key_bias: bfloat16 [2048], P('fsdp'), may hold values from -1.75 to 1.75
- value_weight: bfloat16 [2048, 2048], P(None, 'fsdp'), may hold values from -0.125 to 0.125
- value_bias: bfloat16 [2048], P('fsdp'), may hold values from -0.3125 to 0.3125
- out_weight: bfloat16 [2048, 2048], P('fsdp'), may hold values from -2 to 2
- out_bias: bfloat16 [2048], P('fsdp'), may hold values from -3.5 to 3.5
- inner_weight: bfloat16 [2048, 8192], P(None, 'fsdp'), may hold values from -0.125 to 0.125
- inner_bias: bfloat16 [8192], P('fsdp'), may hold values from -1.75 to 1.75
- outer_weight: bfloat16 [8192, 2048], P('fsdp'), may hold values from -0.0625 to 0.0625
- outer_bias: bfloat16 [2048], P('fsdp'), may hold values from -3.5 to 3.5
- output_grad: bfloat16 [6144, 2048], P('ctx', 'fsdp'), may hold values from -6 to 6
- group_order: int32 [32], replicated, may hold values from 0 to 31, as said below
- sequence_ids: int32 [6144], replicated, may hold values from 0 to 4, as said below
Outputs:
- layer_output: bfloat16 [6144, 2048], P('ctx', 'fsdp')
- input_grad: float32 [6144, 2048], P('ctx', 'fsdp')
- norm_gain_grad: float32 [2048], P('fsdp')
- norm_bias_grad: float32 [2048], P('fsdp')
- query_weight_grad: float32 [2048, 2048], P(None, 'fsdp')
- query_bias_grad: float32 [2048], P('fsdp')
- key_weight_grad: float32 [2048, 2048], P(None, 'fsdp')
- key_bias_grad: float32 [2048], P('fsdp')
- value_weight_grad: float32 [2048, 2048], P(None, 'fsdp')
- value_bias_grad: float32 [2048], P('fsdp')
- out_weight_grad: float32 [2048, 2048], P('fsdp')
- out_bias_grad: float32 [2048], P('fsdp')
- inner_weight_grad: float32 [2048, 8192], P(None, 'fsdp')
- inner_bias_grad: float32 [8192], P('fsdp')
- outer_weight_grad: float32 [8192, 2048], P('fsdp')
- outer_bias_grad: float32 [2048], P('fsdp')
The draws below stay inside these ranges and needn't reach their ends.
Inputs may be any that keep to these rules, and one draw needn't show every extreme that they name: `group_order`: slots 2 i and 2 i + 1 hold groups c and 31 - c for some c; every group is held once. `sequence_ids`: never falls along the positions; document 0 covers at least the first 3072 positions.
All inputs are finite; a program needn't handle non-finite values.
Results may differ from the reference program's by a relative error of at most 0.04.
Values may be sent and summed in bfloat16 or wider, within the bound.
A program may use at most 192 MiB of HBM per device.

```python
import math
from functools import partial
import jax
import jax.numpy as jnp
from jax import lax

D = 2048
HEADS = 32
HEAD_DIM = 64
ROT = 32
FF = 8192
GROUP = 192
GROUPS = 32
SEQ_LEN = 6144


def draw_group_order(key, part):
    key = jax.random.fold_in(key, 11)
    key_pairs, key_flips = jax.random.split(key)
    pair_count = GROUPS // 2
    pair_order = jax.random.permutation(key_pairs, pair_count).astype(jnp.int32)
    flip_bits = jax.random.randint(key_flips, (pair_count,), 0, 2)
    low_side = pair_order
    high_side = GROUPS - 1 - pair_order
    first_slot = jnp.where(flip_bits == 1, high_side, low_side)
    second_slot = jnp.where(flip_bits == 1, low_side, high_side)
    return jnp.stack([first_slot, second_slot], axis=1).reshape(GROUPS).astype(jnp.int32)


def draw_sequence_ids(key, part):
    key = jax.random.fold_in(key, 23)
    key_first, key_rest = jax.random.split(key)
    first_cut = jax.random.randint(key_first, (1,), SEQ_LEN // 2, 3 * SEQ_LEN // 4)
    later_cuts = jax.random.randint(key_rest, (3,), first_cut + 1, SEQ_LEN)
    all_cuts = jnp.concatenate([first_cut, later_cuts])
    position = jnp.arange(SEQ_LEN, dtype=jnp.int32)
    return jnp.sum((position[:, None] >= all_cuts[None, :]).astype(jnp.int32), axis=1).astype(jnp.int32)


def shard_levels(rng, dims, cuts, smallest, largest):
    loudness, own = 1.0, jax.random.fold_in(rng, 6)
    for dim, parts in cuts:
        draws = jnp.exp(jax.random.uniform(jax.random.fold_in(own, dim), (parts,), jnp.float32, smallest / len(cuts), largest / len(cuts)))
        loudness = loudness * jnp.repeat(draws, dims[dim] // parts).reshape([-1 if axis == dim else 1 for axis in range(len(dims))])
    return loudness


def normal_values(key, extent, scale, limit, cuts=(), kind=jnp.bfloat16):
    drawn = scale * jax.random.normal(key, extent, jnp.float32)
    if cuts:
        drawn = drawn * shard_levels(key, extent, cuts, -0.22, 0.18)
    return jnp.clip(drawn, -limit, limit).astype(kind)


def setup_inputs(seed: int = 0) -> dict:
    splits = jax.random.split(jax.random.key(seed), 19)
    layer_input = normal_values(splits[0], (SEQ_LEN, D), 1.0, 6.0, ((0, 16), (1, 8)))
    norm_gain = jnp.clip(1.0 + 0.1 * jax.random.normal(splits[1], (D,), jnp.float32), 0.5, 1.5).astype(jnp.bfloat16)
    norm_bias = normal_values(splits[2], (D,), 0.3, 1.75, ((0, 8),))
    query_weight = normal_values(splits[3], (D, D), D ** -0.5, 0.125, ((1, 8),))
    query_bias = normal_values(splits[4], (D,), 0.3, 1.75, ((0, 8),))
    key_weight = normal_values(splits[5], (D, D), D ** -0.5, 0.125, ((1, 8),))
    key_bias = normal_values(splits[6], (D,), 0.3, 1.75, ((0, 8),))
    value_weight = normal_values(splits[7], (D, D), D ** -0.5, 0.125, ((1, 8),))
    value_bias = normal_values(splits[8], (D,), 0.05, 0.3125, ((0, 8),))
    out_weight = normal_values(splits[9], (D, D), (max(1, D * 32 // SEQ_LEN)) ** -0.5, 2.0, ((0, 8),))
    out_bias = normal_values(splits[10], (D,), 0.6, 3.5, ((0, 8),))
    inner_weight = normal_values(splits[11], (D, FF), D ** -0.5, 0.125, ((1, 8),))
    inner_bias = normal_values(splits[12], (FF,), 0.3, 1.75, ((0, 8),))
    outer_weight = normal_values(splits[13], (FF, D), FF ** -0.5, 0.0625, ((0, 8),))
    outer_bias = normal_values(splits[14], (D,), 0.6, 3.5, ((0, 8),))
    output_grad = normal_values(splits[15], (SEQ_LEN, D), 1.0, 6.0, ((0, 16), (1, 8)))
    group_order = draw_group_order(jax.random.fold_in(splits[18], 71), 0)
    sequence_ids = draw_sequence_ids(jax.random.fold_in(splits[18], 71), 0)
    return {"layer_input": layer_input, "norm_gain": norm_gain, "norm_bias": norm_bias, "query_weight": query_weight, "query_bias": query_bias, "key_weight": key_weight, "key_bias": key_bias, "value_weight": value_weight, "value_bias": value_bias, "out_weight": out_weight, "out_bias": out_bias, "inner_weight": inner_weight, "inner_bias": inner_bias, "outer_weight": outer_weight, "outer_bias": outer_bias, "output_grad": output_grad, "group_order": group_order, "sequence_ids": sequence_ids}


EPS = 1e-05
HIGH = lax.Precision.HIGHEST

@jax.custom_vjp
def low(v):
    return lax.optimization_barrier(v.astype(jnp.bfloat16)).astype(jnp.float32)

@jax.custom_vjp
def low_back(v):
    return v

def low_keep(v):
    return (low(v), None)

def low_pass(kept, grad):
    return (grad,)

def back_keep(v):
    return (v, None)

def back_low(kept, grad):
    return (low(grad),)
low.defvjp(low_keep, low_pass)
low_back.defvjp(back_keep, back_low)

def rotary(values, position, sign):
    half_rot = ROT // 2
    freqs = 10000.0 ** (-(jnp.arange(half_rot, dtype=jnp.float32) * 2.0 / ROT))
    angles = position.astype(jnp.float32)[:, None] * freqs[None, :]
    cosine = jnp.cos(angles)[:, None, :]
    sine = sign * jnp.sin(angles)[:, None, :]
    first_half = values[..., :half_rot]
    second_half = values[..., half_rot:ROT]
    return jnp.concatenate([first_half * cosine - second_half * sine, second_half * cosine + first_half * sine, values[..., ROT:]], axis=-1)

def head_attention(items, position, document):
    queries, keys, values = items
    block_rows = math.gcd(SEQ_LEN, 512)
    block_count = SEQ_LEN // block_rows
    scale = HEAD_DIM ** (-0.5)

    @jax.checkpoint
    def one_block(block_items):
        query_block, query_pos, query_doc = block_items
        scores = low_back(jnp.dot(query_block, keys.T, precision=HIGH) * scale)
        allowed = (position[None, :] <= query_pos[:, None]) & (document[None, :] == query_doc[:, None])
        scores = jnp.where(allowed, scores, -1e+30)
        row_max = lax.optimization_barrier(jnp.max(scores, axis=-1, keepdims=True))
        weights = jnp.exp(scores - row_max)
        probs = weights / lax.optimization_barrier(jnp.sum(weights, axis=-1, keepdims=True))
        return jnp.dot(low(probs), values, precision=HIGH)
    result = lax.map(one_block, (queries.reshape(block_count, block_rows, HEAD_DIM), position.reshape(block_count, block_rows), document.reshape(block_count, block_rows)))
    return result.reshape(SEQ_LEN, HEAD_DIM)

def reference(layer_input, norm_gain, norm_bias, query_weight, query_bias, key_weight, key_bias, value_weight, value_bias, out_weight, out_bias, inner_weight, inner_bias, outer_weight, outer_bias, output_grad, group_order, sequence_ids):
    storage = jnp.arange(SEQ_LEN, dtype=jnp.int32)
    position = (group_order[storage // GROUP] * GROUP + storage % GROUP).astype(jnp.int32)
    document = sequence_ids[position]
    heads_shape = (SEQ_LEN, HEADS, HEAD_DIM)

    def forward(inputs, gain_vec, shift_vec, query_mat, query_vec, key_mat, key_vec, value_mat, value_vec, out_mat, out_vec, inner_mat, inner_vec, outer_mat, outer_vec):
        row_mean = lax.optimization_barrier(jnp.mean(inputs, axis=-1, keepdims=True))
        centered = inputs - row_mean
        variance = lax.optimization_barrier(jnp.mean(centered * centered, axis=-1, keepdims=True))
        normed = low(centered * lax.rsqrt(variance + EPS) * gain_vec + shift_vec)

        def project(matrix, vector):
            return jnp.dot(normed, matrix, precision=HIGH) + vector
        queries = low(rotary(low_back(project(query_mat, query_vec)).reshape(heads_shape), position, 1.0))
        keys = low(rotary(low_back(project(key_mat, key_vec)).reshape(heads_shape), position, 1.0))
        values = low(low_back(project(value_mat, value_vec))).reshape(heads_shape)
        per_head = jax.checkpoint(partial(head_attention, position=position, document=document))
        attended = lax.map(per_head, (queries.transpose(1, 0, 2), keys.transpose(1, 0, 2), values.transpose(1, 0, 2)))
        attended = attended.transpose(1, 0, 2).reshape(SEQ_LEN, D)
        attn_branch = jnp.dot(low(low_back(attended)), out_mat, precision=HIGH) + out_vec
        inner = low_back(project(inner_mat, inner_vec))
        activated = low(jax.nn.gelu(inner, approximate=True))
        return inputs + attn_branch + jnp.dot(activated, outer_mat, precision=HIGH) + outer_vec
    params = tuple((array.astype(jnp.float32) for array in (layer_input, norm_gain, norm_bias, query_weight, query_bias, key_weight, key_bias, value_weight, value_bias, out_weight, out_bias, inner_weight, inner_bias, outer_weight, outer_bias)))
    output, pull_back = jax.vjp(forward, *params)
    grads = pull_back(output_grad.astype(jnp.float32))
    return (output.astype(jnp.bfloat16), grads[0], grads[1], grads[2], grads[3], grads[4], grads[5], grads[6], grads[7], grads[8], grads[9], grads[10], grads[11], grads[12], grads[13], grads[14])
```

```python
from functools import partial

import jax
import jax.numpy as jnp
from jax import lax
from jax.experimental import pallas as pl
from jax.experimental.pallas import tpu as pltpu
from jax.sharding import PartitionSpec as P

HEAD_DIM = 64
ROT = 32
GROUP = 192
GROUPS = 32
SEQ_LEN = 6144
DOCS = 5
EPS = 1e-05
MASKED = -1e30
FLOOR = -1e29
MESH = pl.DeviceIdType.MESH
BF16 = jnp.bfloat16
F32 = jnp.float32
ANY = pl.BlockSpec(memory_space=pl.ANY)
VMEM = pl.BlockSpec(memory_space=pltpu.VMEM)
SMEM = pl.BlockSpec(memory_space=pltpu.SMEM)
MIB = 2**20


class Group:
    def __init__(self, axis):
        ctx, fsdp = lax.axis_index("ctx"), lax.axis_index("fsdp")
        self.axis, self.ctx, self.fsdp = axis, ctx, fsdp
        self.core = lax.rem(ctx, 2)
        self.me = lax.div(ctx, 2) if axis == "ctx" else fsdp
        self.ring, self.pair = lax.rem(self.me, 4), lax.div(self.me, 4)

    def member(self, step, flip):
        pair = 1 - self.pair if flip else self.pair
        return pair * 4 + lax.rem(self.ring + (step + 4), 4)

    def device(self, step, flip):
        member = self.member(step, flip)
        if self.axis == "ctx":
            return (member * 2 + self.core, self.fsdp)
        return (self.ctx, member)

    def neighbours(self):
        return [self.device(1, 0), self.device(-1, 0), self.device(0, 1)]


def other_core(group):
    return (group.ctx + 1 - 2 * group.core, group.fsdp)


def barrier(devices):
    semaphore = pltpu.get_barrier_semaphore()
    for device in devices:
        pl.semaphore_signal(semaphore, inc=1, device_id=device, device_id_type=MESH)
    pl.semaphore_wait(semaphore, len(devices))


def remote(source, target, sems, slot, device):
    return pltpu.make_async_remote_copy(
        src_ref=source,
        dst_ref=target,
        send_sem=sems[0].at[slot],
        recv_sem=sems[1].at[slot],
        device_id=device,
        device_id_type=MESH,
    )


GATHER = (
    (1, 0, (0, 0), 0, 2, None),
    (-1, 0, (0, 0), 0, 2, None),
    (0, 1, (0, 0), 2, 4, None),
    (1, 0, (0, 0), 2, 4, None),
    (-1, 0, (0, 0), 2, 4, None),
    (0, 1, (0, 0), 0, 2, None),
    (1, 0, (-1, 0), 0, 1, 0),
    (-1, 0, (1, 0), 1, 2, 1),
    (0, 1, (-1, 0), 0, 2, 0),
    (0, 1, (1, 0), 0, 2, 1),
    (0, 1, (2, 0), 0, 1, 6),
    (0, 1, (2, 0), 1, 2, 7),
    (1, 0, (0, 1), 2, 4, 2),
    (-1, 0, (0, 1), 2, 4, 2),
    (1, 0, (-1, 0), 2, 3, 3),
    (-1, 0, (1, 0), 3, 4, 4),
    (1, 0, (-1, 1), 2, 3, 12),
    (-1, 0, (1, 1), 3, 4, 13),
)
GATHER_ORDER = (0, 1, 2, 3, 4, 6, 7, 12, 13, 5, 8, 9, 10, 11, 14, 15, 16, 17)
GATHER_SLOTS = len(GATHER)


def gather(group, view, sems, arrived=None):
    started = []

    def start(slot):
        step, flip, block, a, b, _ = GATHER[slot]
        ref = view(group.member(*block), a, b)
        copy = remote(ref, ref, sems, slot, group.device(step, flip))
        copy.start()
        started.append(copy)

    for slot, row in enumerate(GATHER):
        if row[5] is None:
            start(slot)
    if arrived:
        arrived(group.member(0, 0), 0, 4)
    for slot in GATHER_ORDER:
        step, flip, block, a, b, _ = GATHER[slot]
        yield
        member = group.member(block[0] - step, block[1] ^ flip)
        ref = view(member, a, b)
        remote(ref, ref, sems, slot, group.device(step, flip)).wait_recv()
        for later, row in enumerate(GATHER):
            if row[5] == slot:
                start(later)
        if arrived:
            arrived(member, a, b)
    for copy in started:
        copy.wait_send()


SCATTER_SLOTS = 23
HOLD = 7


def add_into(target, *sources):
    total = target[...].astype(F32)
    for source in sources:
        total = total + source[...].astype(F32)
    target[...] = total.astype(target.dtype)


def scatter(group, part, quarters, hold, result, sems):
    started = []

    def start(slot, source, step, flip, k, a, b):
        copy = remote(source, quarters(hold.at[k], a, b), sems, slot, group.device(step, flip))
        copy.start()
        started.append(copy)

    def wait(slot, k, a, b):
        ref = quarters(hold.at[k], a, b)
        remote(ref, ref, sems, slot, group.device(0, 1)).wait_recv()

    def held(k, a, b):
        return quarters(hold.at[k], a, b)

    start(0, part(2, 1, 0, 2), 0, 1, 0, 0, 2)
    start(10, part(2, 1, 2, 3), 1, 0, 0, 2, 3)
    start(11, part(2, 1, 3, 4), -1, 0, 0, 3, 4)
    start(1, part(1, 1, 0, 2), 0, 1, 1, 0, 2)
    start(2, part(-1, 1, 0, 2), 0, 1, 2, 0, 2)
    start(16, part(2, 0, 2, 3), 1, 0, 3, 2, 3)
    start(17, part(2, 0, 3, 4), -1, 0, 3, 3, 4)
    start(12, part(1, 1, 3, 4), 1, 0, 1, 3, 4)
    start(13, part(-1, 1, 2, 3), -1, 0, 2, 2, 3)
    start(18, part(1, 0, 3, 4), 1, 0, 4, 3, 4)
    start(19, part(-1, 0, 2, 3), -1, 0, 5, 2, 3)
    start(3, part(0, 1, 0, 2), 0, 1, 3, 0, 2)
    yield
    wait(0, 0, 0, 2)
    add_into(held(0, 0, 2), part(2, 0, 0, 2))
    start(4, held(0, 0, 1), 1, 0, 4, 0, 1)
    start(5, held(0, 1, 2), -1, 0, 4, 1, 2)
    yield
    wait(10, 0, 2, 3)
    add_into(held(0, 2, 3), part(1, 1, 2, 3))
    start(14, held(0, 2, 3), 1, 0, 1, 2, 3)
    wait(11, 0, 3, 4)
    add_into(held(0, 3, 4), part(-1, 1, 3, 4))
    start(15, held(0, 3, 4), -1, 0, 2, 3, 4)
    yield
    wait(1, 1, 0, 2)
    add_into(held(1, 0, 2), part(1, 0, 0, 2))
    start(6, held(1, 1, 2), 1, 0, 5, 1, 2)
    wait(2, 2, 0, 2)
    add_into(held(2, 0, 2), part(-1, 0, 0, 2))
    start(8, held(2, 0, 1), -1, 0, 6, 0, 1)
    yield
    wait(16, 3, 2, 3)
    add_into(held(3, 2, 3), part(1, 0, 2, 3))
    start(20, held(3, 2, 3), 1, 0, 4, 2, 3)
    wait(17, 3, 3, 4)
    add_into(held(3, 3, 4), part(-1, 0, 3, 4))
    start(21, held(3, 3, 4), -1, 0, 5, 3, 4)
    yield
    wait(4, 4, 0, 1)
    add_into(held(1, 0, 1), held(4, 0, 1))
    start(7, held(1, 0, 1), 1, 0, 5, 0, 1)
    wait(5, 4, 1, 2)
    add_into(held(2, 1, 2), held(4, 1, 2))
    start(9, held(2, 1, 2), -1, 0, 6, 1, 2)
    yield
    wait(12, 1, 3, 4)
    wait(14, 1, 2, 3)
    wait(13, 2, 2, 3)
    wait(15, 2, 3, 4)
    add_into(held(1, 2, 4), held(2, 2, 4), part(0, 1, 2, 4))
    start(22, held(1, 2, 4), 0, 1, 6, 2, 4)
    yield
    wait(3, 3, 0, 2)
    wait(6, 5, 1, 2)
    wait(8, 6, 0, 1)
    wait(7, 5, 0, 1)
    wait(9, 6, 1, 2)
    result(0, 2, [part(0, 0, 0, 2), held(3, 0, 2), held(5, 0, 2), held(6, 0, 2)])
    yield
    wait(18, 4, 3, 4)
    wait(20, 4, 2, 3)
    wait(19, 5, 2, 3)
    wait(21, 5, 3, 4)
    wait(22, 6, 2, 4)
    result(2, 4, [part(0, 0, 2, 4), held(4, 2, 4), held(5, 2, 4), held(6, 2, 4)])
    for copy in started:
        copy.wait_send()


def total_of(refs):
    total = refs[0][...].astype(F32)
    for ref in refs[1:]:
        total = total + ref[...].astype(F32)
    return total


def drain(*programs):
    programs = list(programs)
    while programs:
        programs = [p for p in programs if next(p, "end") != "end"]


def pairs(count):
    return [pltpu.SemaphoreType.DMA((count,)), pltpu.SemaphoreType.DMA((count,))]


def params(collective_id, mib):
    return pltpu.CompilerParams(
        collective_id=collective_id, has_side_effects=True, vmem_limit_bytes=mib * MIB
    )


ROW_CUTS = (0, 96, 192, 288, 400)


def gather_rows_kernel(x_ref, dy_ref, x_out, dy_out, xs, xr, ds, dr, cs, cr, local):
    group = Group("fsdp")
    core = group.core
    width = x_ref.shape[1]
    partner = other_core(group)

    def x_view(member, a, b):
        columns = pl.ds(pl.multiple_of(member * width, width), width)
        return x_out.at[core, pl.ds(ROW_CUTS[a], ROW_CUTS[b] - ROW_CUTS[a]), columns]

    def dy_view(member, a, b):
        columns = pl.ds(pl.multiple_of(member * width, width), width)
        return dy_out.at[core, pl.ds(96 * a, 96 * (b - a)), columns]

    copies = [
        pltpu.make_async_copy(x_ref, x_view(group.me, 0, 4), local.at[0]),
        pltpu.make_async_copy(dy_ref, dy_view(group.me, 0, 4), local.at[1]),
    ]
    for copy in copies:
        copy.start()
    barrier(group.neighbours() + [partner])
    for copy in copies:
        copy.wait()
    drain(gather(group, x_view, (xs, xr)), gather(group, dy_view, (ds, dr)))
    last = [
        remote(x_out.at[core], x_out.at[core], (cs, cr), 0, partner),
        remote(dy_out.at[core], dy_out.at[core], (cs, cr), 1, partner),
    ]
    for copy in last:
        copy.start()
    for copy in last:
        copy.wait()


def gather_rows(x, dy):
    return pl.pallas_call(
        gather_rows_kernel,
        out_shape=[
            jax.ShapeDtypeStruct((2, x.shape[0], 2048), BF16),
            jax.ShapeDtypeStruct((2, dy.shape[0], 2048), BF16),
        ],
        in_specs=[ANY, ANY],
        out_specs=[ANY, ANY],
        scratch_shapes=pairs(GATHER_SLOTS) + pairs(GATHER_SLOTS) + pairs(2) + [pltpu.SemaphoreType.DMA((2,))],
        compiler_params=params(0, 32),
        name="gather_rows",
    )(x, dy)


def gather_keys_kernel(kv_ref, out, send, recv, local):
    group = Group("ctx")
    rows = kv_ref.shape[0]
    step = rows // 4

    def view(member, a, b):
        return out.at[member, pl.ds(step * a, step * (b - a)), :]

    copy = pltpu.make_async_copy(kv_ref, view(group.me, 0, 4), local.at[0])
    copy.start()
    barrier(group.neighbours())
    copy.wait()
    drain(gather(group, view, (send, recv)))


def gather_keys(kv):
    return pl.pallas_call(
        gather_keys_kernel,
        out_shape=jax.ShapeDtypeStruct((8,) + kv.shape, BF16),
        in_specs=[ANY],
        out_specs=ANY,
        scratch_shapes=pairs(GATHER_SLOTS) + [pltpu.SemaphoreType.DMA((1,))],
        compiler_params=params(1, 32),
        name="gather_keys",
    )(kv)


def cut_rows(ref, a, b):
    step = ref.shape[0] // 4
    return ref.at[pl.ds(step * a, step * (b - a)), :]


def scatter_keys_kernel(part_ref, out, hold, send, recv):
    group = Group("ctx")
    barrier(group.neighbours())

    def part(step, flip, a, b):
        return cut_rows(part_ref.at[group.member(step, flip)], a, b)

    def result(a, b, refs):
        target = cut_rows(out, a, b)
        target[...] = total_of(refs)

    drain(scatter(group, part, cut_rows, hold, result, (send, recv)))


def scatter_keys(part):
    return pl.pallas_call(
        scatter_keys_kernel,
        out_shape=jax.ShapeDtypeStruct(part.shape[1:], F32),
        in_specs=[VMEM],
        out_specs=VMEM,
        scratch_shapes=[pltpu.VMEM((HOLD,) + part.shape[1:], BF16)] + pairs(SCATTER_SLOTS),
        compiler_params=params(2, 48),
        name="scatter_keys",
    )(part)


def scatter_rows_kernel(part_ref, out, arriving, hold, cs, cr, send, recv):
    group = Group("fsdp")
    core, partner = group.core, other_core(group)
    barrier(group.neighbours() + [partner])
    copy = remote(part_ref.at[1 - core], arriving, (cs, cr), 0, partner)
    copy.start()
    copy.wait()

    def one(i, carry):
        rows = pl.ds(pl.multiple_of(i * 32, 32), 32)
        arriving[rows, :] = (arriving[rows, :].astype(F32) + part_ref[core, rows, :].astype(F32)).astype(BF16)
        return carry

    lax.fori_loop(0, arriving.shape[0] // 32, one, 0)
    width = out.shape[1]

    def part(step, flip, a, b):
        columns = pl.ds(pl.multiple_of(group.member(step, flip) * width, width), width)
        return arriving.at[pl.ds(96 * a, 96 * (b - a)), columns]

    def result(a, b, refs):
        target = cut_rows(out, a, b)
        target[...] = total_of(refs)

    drain(scatter(group, part, cut_rows, hold, result, (send, recv)))


def scatter_rows(part, collective_id):
    rows, width = part.shape[1], part.shape[2] // 8
    return pl.pallas_call(
        scatter_rows_kernel,
        out_shape=jax.ShapeDtypeStruct((rows, width), F32),
        in_specs=[VMEM],
        out_specs=VMEM,
        scratch_shapes=[pltpu.VMEM((rows, part.shape[2]), BF16), pltpu.VMEM((HOLD, rows, width), BF16)]
        + pairs(1)
        + pairs(SCATTER_SLOTS),
        compiler_params=params(collective_id, 32),
        name="scatter_rows",
    )(part)


def sum_small_kernel(axis, x_ref, out, hold, send, recv):
    ctx, fsdp = lax.axis_index("ctx"), lax.axis_index("fsdp")
    count = lax.axis_size(axis)
    me = ctx if axis == "ctx" else fsdp

    def device(offset):
        other = lax.rem(me + offset, count)
        return (other, fsdp) if axis == "ctx" else (ctx, other)

    barrier([device(offset) for offset in range(1, count)])
    copies = [
        remote(x_ref, hold.at[offset - 1], (send, recv), offset - 1, device(offset))
        for offset in range(1, count)
    ]
    for copy in copies:
        copy.start()
    total = x_ref[...]
    for offset in range(1, count):
        copies[offset - 1].wait_recv()
        total = total + hold[offset - 1]
    out[...] = total
    for copy in copies:
        copy.wait_send()


def sum_small(x, axis, collective_id):
    count = lax.axis_size(axis) - 1
    return pl.pallas_call(
        partial(sum_small_kernel, axis),
        out_shape=jax.ShapeDtypeStruct(x.shape, F32),
        in_specs=[VMEM],
        out_specs=VMEM,
        scratch_shapes=[pltpu.VMEM((count,) + x.shape, F32)] + pairs(count),
        compiler_params=params(collective_id, 16),
        name="sum_small",
    )(x)


def reduce_weights_kernel(count, *refs):
    ins, outs = refs[:count], refs[count : 2 * count]
    holds = refs[2 * count : 3 * count]
    sems = refs[3 * count :]
    group = Group("ctx")
    core, partner = group.core, other_core(group)
    barrier(group.neighbours() + [partner])

    def whole(i):
        source, target, hold = ins[i], outs[i], holds[i]
        rs, rr, gs, gr, cs, cr = sems[6 * i : 6 * i + 6]
        rows, width = source.shape[0] // 8, source.shape[1]
        by_rows = rows % 64 == 0

        def quarters(ref, a, b):
            if by_rows:
                return ref.at[pl.ds(rows // 4 * a, rows // 4 * (b - a)), :]
            return ref.at[:, pl.ds(width // 4 * a, width // 4 * (b - a))]

        def part(step, flip, a, b):
            start = pl.multiple_of(group.member(step, flip) * rows, rows)
            return quarters(source.at[pl.ds(start, rows), :], a, b)

        def view(member, a, b):
            start = pl.multiple_of(member * rows, rows)
            return quarters(target.at[core, pl.ds(start, rows), :], a, b)

        def result(a, b, terms):
            place = view(group.me, a, b)
            place[...] = total_of(terms).astype(BF16)

        copies = []

        def arrived(member, a, b):
            ref = view(member, a, b)
            copy = remote(ref, ref, (cs, cr), len(copies), partner)
            copy.start()
            copies.append(copy)

        yield from scatter(group, part, quarters, hold, result, (rs, rr))
        yield from gather(group, view, (gs, gr), arrived)
        yield
        for copy in copies:
            copy.wait()

    drain(*[whole(i) for i in range(count)])


def reduce_weights(parts, collective_id):
    count = len(parts)
    return pl.pallas_call(
        partial(reduce_weights_kernel, count),
        out_shape=[jax.ShapeDtypeStruct((2,) + x.shape, BF16) for x in parts],
        in_specs=[VMEM] * count,
        out_specs=[VMEM] * count,
        scratch_shapes=[pltpu.VMEM((HOLD, x.shape[0] // 8, x.shape[1]), BF16) for x in parts]
        + (pairs(SCATTER_SLOTS) + pairs(GATHER_SLOTS) + pairs(GATHER_SLOTS + 1)) * count,
        compiler_params=params(collective_id, 60),
        name="reduce_weights",
    )(*parts)


TILE = 2 * GROUP
TILES = SEQ_LEN // TILE
ITEMS = TILES + 1
NT = (((1,), (1,)), ((), ()))
TN = (((0,), (0,)), ((), ()))


def dot(a, b, dims=(((1,), (0,)), ((), ()))):
    return lax.dot_general(a, b, dims, preferred_element_type=F32)


def attention_kernel(
    table, qd_ref, kv_ref, begin_ref, att_ref, dq_ref, dkv_ref, kvp, state_max, state_sum, state_acc, dq_items, dkv_items, lse_ref, delta_ref
):
    lane = lax.broadcasted_iota(jnp.int32, (1, 128), 1)
    left = lane < HEAD_DIM

    def place(g, carry):
        tile, half = lax.div(g, 2), lax.rem(g, 2)
        kvp[tile, pl.ds(pl.multiple_of(half * GROUP, GROUP), GROUP), :] = kv_ref[table[g]]
        return carry

    lax.fori_loop(0, GROUPS, place, 0)

    def pair_facts(p):
        g0, g1 = table[32 + 2 * p], table[33 + 2 * p]
        low, high = jnp.minimum(g0, g1), jnp.maximum(g0, g1)
        low_slot = jnp.where(g0 < g1, 0, 1)
        return low, high, low_slot, lax.div(low, 2) + 1

    def item_facts(p, j):
        low, high, low_slot, count = pair_facts(p)
        second = j >= count
        tile = jnp.where(second, TILES, count - 1) - j
        slot = 2 * p + jnp.where(second, 1 - low_slot, low_slot)
        position = jnp.where(second, high, low) * GROUP
        key_pos = tile * TILE + lax.broadcasted_iota(jnp.int32, (1, TILE), 1)
        query_pos = position + lax.broadcasted_iota(jnp.int32, (GROUP, 1), 0)
        allowed = (key_pos <= query_pos) & (key_pos >= begin_ref[slot])
        first = (j == 0) | (j == count)
        return tile, slot, allowed, first

    for p in range(2):
        for h in range(2):
            state_max[p, h, 0] = jnp.full((GROUP, 128), FLOOR, F32)
            state_sum[p, h, 0] = jnp.zeros((GROUP, 128), F32)
            state_acc[p, h, 0] = jnp.zeros((GROUP, 128), F32)

    def forward(j, carry):
        for p in range(2):
            tile, slot, allowed, first = item_facts(p, j)
            for h in range(2):
                lanes = slice(128 * h, 128 * h + 128)
                queries = jnp.where(left, qd_ref[slot, :, lanes], 0).astype(BF16)
                keys = kvp[tile, :, lanes]
                scores = jnp.where(allowed, dot(queries, keys, NT), MASKED)
                old_max = jnp.where(first, FLOOR, state_max[p, h, j])
                new_max = jnp.maximum(old_max, jnp.max(scores, axis=1, keepdims=True))
                weights = jnp.exp(scores - new_max[:, :1])
                factor = jnp.exp(old_max - new_max)
                state_max[p, h, j + 1] = new_max
                state_sum[p, h, j + 1] = state_sum[p, h, j] * factor + jnp.sum(weights, axis=1, keepdims=True)
                state_acc[p, h, j + 1] = state_acc[p, h, j] * factor + dot(weights.astype(BF16), keys)
        return carry

    lax.fori_loop(0, ITEMS, forward, 0)

    for p in range(2):
        low, high, low_slot, count = pair_facts(p)
        for i in range(2):
            item = jnp.where(low_slot == i, count, ITEMS)
            slot = 2 * p + i
            outs = []
            for h in range(2):
                total = state_sum[p, h, item]
                out = state_acc[p, h, item] / total
                outs.append(out)
                lse_ref[h, slot] = state_max[p, h, item] + jnp.log(total)
                cotangent = qd_ref[slot, :, 128 * h : 128 * h + 128].astype(F32)
                product = jnp.where(left, 0.0, cotangent * out)
                delta_ref[h, slot] = jnp.broadcast_to(jnp.sum(product, axis=1, keepdims=True), (GROUP, 128))
            att_ref[slot] = jnp.where(left, pltpu.roll(outs[0], HEAD_DIM, 1), outs[1]).astype(BF16)

    for p in range(2):
        dq_items[p, 0] = jnp.zeros((GROUP, 256), F32)

    def backward(j, carry):
        for p in range(2):
            tile, slot, allowed, first = item_facts(p, j)
            keep = jnp.where(first, 0.0, 1.0)
            for h in range(2):
                lanes = slice(128 * h, 128 * h + 128)
                both = qd_ref[slot, :, lanes]
                queries = jnp.where(left, both, 0).astype(BF16)
                cotangent = jnp.where(left, 0, both).astype(BF16)
                keys = kvp[tile, :, lanes]
                scores = dot(queries, keys, NT)
                probs = jnp.where(allowed, jnp.exp(scores - lse_ref[h, slot][:, :1]), 0.0)
                prob_grad = dot(cotangent, keys, NT)
                score_grad = (probs * (prob_grad - delta_ref[h, slot][:, :1])).astype(BF16)
                dq_items[p, j + 1, :, lanes] = dq_items[p, j, :, lanes] * keep + dot(score_grad, keys)
                dkv_items[p, j, :, lanes] = (
                    dot(score_grad, queries, TN) + dot(probs.astype(BF16), cotangent, TN)
                ).astype(dkv_items.dtype)
        return carry

    lax.fori_loop(0, ITEMS, backward, 0)

    for p in range(2):
        low, high, low_slot, count = pair_facts(p)
        for i in range(2):
            item = jnp.where(low_slot == i, count, ITEMS)
            grad = dq_items[p, item]
            dq_ref[2 * p + i] = jnp.where(left, grad[:, :128], pltpu.roll(grad[:, 128:], HEAD_DIM, 1))

    counts = [pair_facts(p)[3] for p in range(2)]

    def collect(s, carry):
        group = table[36 + s]
        tile, half = lax.div(group, 2), lax.rem(group, 2)
        rows = pl.ds(pl.multiple_of(half * GROUP, GROUP), GROUP)
        total = jnp.zeros((GROUP, 256), F32)
        for p in range(2):
            low_item = dkv_items[p, jnp.maximum(counts[p] - 1 - tile, 0), rows, :].astype(F32)
            high_item = dkv_items[p, jnp.maximum(TILES - tile, counts[p]), rows, :].astype(F32)
            total = total + jnp.where(tile < counts[p], low_item, 0.0)
            total = total + jnp.where(TILES - tile >= counts[p], high_item, 0.0)
        dkv_ref[s] = total.astype(BF16)
        return carry

    lax.fori_loop(0, GROUPS, collect, 0)


def attention(table, qd, kv, begin):
    return pl.pallas_call(
        attention_kernel,
        out_shape=[
            jax.ShapeDtypeStruct((4, GROUP, 128), BF16),
            jax.ShapeDtypeStruct((4, GROUP, 128), F32),
            jax.ShapeDtypeStruct((GROUPS, GROUP, 256), BF16),
        ],
        in_specs=[SMEM, VMEM, VMEM, VMEM],
        out_specs=[VMEM, VMEM, VMEM],
        scratch_shapes=[
            pltpu.VMEM((TILES, TILE, 256), BF16),
            pltpu.VMEM((2, 2, ITEMS + 1, GROUP, 128), F32),
            pltpu.VMEM((2, 2, ITEMS + 1, GROUP, 128), F32),
            pltpu.VMEM((2, 2, ITEMS + 1, GROUP, 128), F32),
            pltpu.VMEM((2, ITEMS + 1, GROUP, 256), F32),
            pltpu.VMEM((2, ITEMS, TILE, 256), BF16),
            pltpu.VMEM((2, 4, GROUP, 128), F32),
            pltpu.VMEM((2, 4, GROUP, 128), F32),
        ],
        compiler_params=pltpu.CompilerParams(vmem_limit_bytes=60 * MIB),
        name="attention",
    )(table, qd, kv, begin)


def turn(values, cosine, sine):
    first, second = values[..., : ROT // 2], values[..., ROT // 2 : ROT]
    return jnp.concatenate(
        [first * cosine - second * sine, second * cosine + first * sine, values[..., ROT:]], axis=-1
    )


def body(
    layer_input,
    norm_gain,
    norm_bias,
    query_weight,
    query_bias,
    key_weight,
    key_bias,
    value_weight,
    value_bias,
    out_weight,
    out_bias,
    inner_weight,
    inner_bias,
    outer_weight,
    outer_bias,
    output_grad,
    group_order,
    sequence_ids,
):
    ctx = lax.axis_index("ctx")
    fsdp = lax.axis_index("fsdp")
    core = lax.rem(ctx, 2)
    rows = layer_input.shape[0]
    both = 2 * rows

    def half(array, axis):
        size = array.shape[axis] // 2
        return lax.dynamic_slice_in_dim(array, core * size, size, axis)

    wq, wk, wv = half(query_weight, 1), half(key_weight, 1), half(value_weight, 1)
    wo, wi, wu = half(out_weight, 0), half(inner_weight, 1), half(outer_weight, 0)
    bq, bk, bv, bi = half(query_bias, 0), half(key_bias, 0), half(value_bias, 0), half(inner_bias, 0)

    slots = lax.div(ctx, 2) * 4 + jnp.arange(4, dtype=jnp.int32)
    my_groups = group_order[slots]
    position = (my_groups[:, None] * GROUP + jnp.arange(GROUP, dtype=jnp.int32)[None, :]).reshape(both)
    begins = jnp.sum(
        (sequence_ids[None, :] < jnp.arange(DOCS, dtype=jnp.int32)[:, None]).astype(jnp.int32), axis=1
    )
    my_docs = sequence_ids.reshape(GROUPS, GROUP)[my_groups]
    begin = jnp.zeros((4, GROUP), jnp.int32)
    for doc in range(1, DOCS):
        begin = jnp.where(my_docs == doc, begins[doc], begin)
    slot_of = jnp.sum(
        jnp.where(group_order[None, :] == jnp.arange(GROUPS)[:, None], jnp.arange(GROUPS)[None, :], 0), axis=1
    ).astype(jnp.int32)
    table = jnp.concatenate([slot_of, my_groups, group_order]).astype(jnp.int32)
    freqs = 10000.0 ** (-(jnp.arange(ROT // 2, dtype=F32) * 2.0 / ROT))
    angles = position.astype(F32)[:, None] * freqs[None, :]
    cosine, sine = jnp.cos(angles)[:, None, :], jnp.sin(angles)[:, None, :]

    extra = jnp.concatenate([norm_gain[None], norm_bias[None], jnp.zeros((14, norm_gain.shape[0]), BF16)])
    x_all, dy_all = gather_rows(jnp.concatenate([layer_input, extra]), output_grad)
    gain = x_all[0, rows].astype(F32)
    shift = x_all[0, rows + 1].astype(F32)
    dy = dy_all.reshape(both, -1)
    inputs = x_all[:, :rows].reshape(both, -1).astype(F32)
    row_mean = jnp.mean(inputs, axis=-1, keepdims=True)
    centered = inputs - row_mean
    inv_std = lax.rsqrt(jnp.mean(centered * centered, axis=-1, keepdims=True) + EPS)
    normed = (centered * inv_std * gain + shift).astype(BF16)

    def project(matrix, vector):
        return jnp.dot(normed, matrix, preferred_element_type=F32) + vector.astype(F32)

    queries = turn(project(wq, bq).reshape(both, 2, HEAD_DIM), cosine, sine).astype(BF16)
    keys = turn(project(wk, bk).reshape(both, 2, HEAD_DIM), cosine, sine).astype(BF16)
    values = project(wv, bv).astype(BF16).reshape(both, 2, HEAD_DIM)
    kv = jnp.concatenate([keys, values], axis=-1).reshape(both, 256)
    kv_all = gather_keys(kv).reshape(GROUPS, GROUP, 256)
    attended_grad = jnp.einsum("rd,cd->rc", dy, wo, preferred_element_type=F32).astype(BF16)
    scaled = (queries.astype(F32) * HEAD_DIM ** (-0.5)).astype(BF16)
    qd = jnp.concatenate([scaled, attended_grad.reshape(both, 2, HEAD_DIM)], axis=-1).reshape(4, GROUP, 256)
    attended, dq, dkv = attention(table, qd, kv_all, begin[:, :, None])
    attended = attended.reshape(both, 128)
    dkv_own = scatter_keys(dkv.reshape(8, both, 256))

    inner = project(wi, bi)
    activated = jax.nn.gelu(inner, approximate=True).astype(BF16)
    act_grad = jnp.einsum("rd,fd->rf", dy, wu, preferred_element_type=F32)
    _, gelu_pull = jax.vjp(partial(jax.nn.gelu, approximate=True), inner)
    inner_grad = gelu_pull(act_grad)[0].astype(BF16)
    branches = jnp.dot(attended, wo, preferred_element_type=F32) + jnp.dot(activated, wu, preferred_element_type=F32)
    summed = scatter_rows(branches.astype(BF16).reshape(2, rows, -1), 3)
    layer_output = (
        layer_input.astype(F32) + summed + out_bias.astype(F32) + outer_bias.astype(F32)
    ).astype(BF16)

    def weight_grad(left, right):
        return jnp.einsum("rc,rd->cd", left, right, preferred_element_type=F32).astype(BF16)

    query_pre_grad = turn(dq.reshape(both, 2, HEAD_DIM) * HEAD_DIM ** (-0.5), cosine, -sine)
    query_pre_grad = query_pre_grad.reshape(both, 128).astype(BF16)
    dkv_own = dkv_own.reshape(both, 2, 128)
    key_pre_grad = turn(dkv_own[..., :HEAD_DIM], cosine, -sine).reshape(both, 128).astype(BF16)
    value_pre_grad = dkv_own[..., HEAD_DIM:].reshape(both, 128).astype(BF16)
    pre_grads = jnp.concatenate([query_pre_grad, key_pre_grad, value_pre_grad], axis=1)
    normed_grad = jnp.einsum("rf,df->rd", inner_grad, wi, preferred_element_type=F32) + jnp.einsum(
        "rc,dc->rd", pre_grads, jnp.concatenate([wq, wk, wv], axis=1), preferred_element_type=F32
    )
    local_grad = scatter_rows(normed_grad.astype(BF16).reshape(2, rows, -1), 4)
    my_mean = lax.dynamic_slice_in_dim(row_mean, core * rows, rows, 0)
    my_inv = lax.dynamic_slice_in_dim(inv_std, core * rows, rows, 0)
    unit = (layer_input.astype(F32) - my_mean) * my_inv
    scaled_grad = local_grad * norm_gain.astype(F32)
    sums = jnp.stack([jnp.sum(scaled_grad, axis=1), jnp.sum(scaled_grad * unit, axis=1)])
    sums = sum_small(jnp.pad(sums, ((0, 6), (0, 0))), "fsdp", 5) * (1.0 / 2048)
    input_grad = output_grad.astype(F32) + my_inv * (scaled_grad - sums[0][:, None] - unit * sums[1][:, None])

    def spread(vector):
        out = jnp.zeros((2,) + vector.shape, F32)
        return lax.dynamic_update_index_in_dim(out, vector, core, 0).reshape(-1)

    def columns(array):
        return jnp.sum(array.astype(F32), axis=0)

    vectors = jnp.concatenate(
        [
            jnp.sum(local_grad * unit, axis=0),
            columns(local_grad),
            columns(output_grad),
            spread(columns(query_pre_grad)),
            spread(columns(key_pre_grad)),
            spread(columns(value_pre_grad)),
            spread(columns(inner_grad)),
        ]
    ).reshape(10, 256)
    vectors = sum_small(jnp.pad(vectors, ((0, 6), (0, 0))), "ctx", 6)
    qkv_grad, out_grad, inner_w_grad, outer_w_grad = reduce_weights(
        [weight_grad(normed, pre_grads), weight_grad(attended, dy), weight_grad(normed, inner_grad), weight_grad(activated, dy)],
        7,
    )

    def side_by_side(array):
        return jnp.concatenate([array[0], array[1]], axis=1).astype(F32)

    return (
        layer_output,
        input_grad,
        vectors[0],
        vectors[1],
        side_by_side(qkv_grad[:, :, :128]),
        vectors[3],
        side_by_side(qkv_grad[:, :, 128:256]),
        vectors[4],
        side_by_side(qkv_grad[:, :, 256:]),
        vectors[5],
        out_grad.reshape(256, 2048).astype(F32),
        vectors[2],
        side_by_side(inner_w_grad),
        vectors[6:10].reshape(1024),
        outer_w_grad.reshape(1024, 2048).astype(F32),
        vectors[2],
    )


def solution(mesh):
    in_specs = (
        P("ctx", "fsdp"),
        P("fsdp"),
        P("fsdp"),
        P(None, "fsdp"),
        P("fsdp"),
        P(None, "fsdp"),
        P("fsdp"),
        P(None, "fsdp"),
        P("fsdp"),
        P("fsdp", None),
        P("fsdp"),
        P(None, "fsdp"),
        P("fsdp"),
        P("fsdp", None),
        P("fsdp"),
        P("ctx", "fsdp"),
        P(),
        P(),
    )
    out_specs = (
        P("ctx", "fsdp"),
        P("ctx", "fsdp"),
        P("fsdp"),
        P("fsdp"),
        P(None, "fsdp"),
        P("fsdp"),
        P(None, "fsdp"),
        P("fsdp"),
        P(None, "fsdp"),
        P("fsdp"),
        P("fsdp", None),
        P("fsdp"),
        P(None, "fsdp"),
        P("fsdp"),
        P("fsdp", None),
        P("fsdp"),
    )
    return jax.shard_map(body, mesh=mesh, in_specs=in_specs, out_specs=out_specs, check_vma=False)
```

```python
from functools import partial

import jax
import jax.numpy as jnp
from jax import lax
from jax.experimental import pallas as pl
from jax.experimental.pallas import tpu as pltpu
from jax.sharding import PartitionSpec as P

HEAD_DIM = 64
ROT = 32
GROUP = 192
GROUPS = 32
SEQ_LEN = 6144
DOCS = 5
EPS = 1e-05
MASKED = -1e30
FLOOR = -1e29
MESH = pl.DeviceIdType.MESH
BF16 = jnp.bfloat16
F32 = jnp.float32
ANY = pl.BlockSpec(memory_space=pl.ANY)
VMEM = pl.BlockSpec(memory_space=pltpu.VMEM)
SMEM = pl.BlockSpec(memory_space=pltpu.SMEM)
MIB = 2**20


class Group:
    def __init__(self, axis):
        ctx, fsdp = lax.axis_index("ctx"), lax.axis_index("fsdp")
        self.axis, self.ctx, self.fsdp = axis, ctx, fsdp
        self.core = lax.rem(ctx, 2)
        self.me = lax.div(ctx, 2) if axis == "ctx" else fsdp
        self.ring, self.pair = lax.rem(self.me, 4), lax.div(self.me, 4)

    def member(self, step, flip):
        pair = 1 - self.pair if flip else self.pair
        return pair * 4 + lax.rem(self.ring + (step + 4), 4)

    def device(self, step, flip):
        member = self.member(step, flip)
        if self.axis == "ctx":
            return (member * 2 + self.core, self.fsdp)
        return (self.ctx, member)

    def neighbours(self):
        return [self.device(1, 0), self.device(-1, 0), self.device(0, 1)]


def other_core(group):
    return (group.ctx + 1 - 2 * group.core, group.fsdp)


def barrier(devices):
    semaphore = pltpu.get_barrier_semaphore()
    for device in devices:
        pl.semaphore_signal(semaphore, inc=1, device_id=device, device_id_type=MESH)
    pl.semaphore_wait(semaphore, len(devices))


def remote(source, target, sems, slot, device):
    return pltpu.make_async_remote_copy(
        src_ref=source,
        dst_ref=target,
        send_sem=sems[0].at[slot],
        recv_sem=sems[1].at[slot],
        device_id=device,
        device_id_type=MESH,
    )


GATHER = (
    (1, 0, (0, 0), 0, 2, None),
    (-1, 0, (0, 0), 0, 2, None),
    (0, 1, (0, 0), 2, 4, None),
    (1, 0, (0, 0), 2, 4, None),
    (-1, 0, (0, 0), 2, 4, None),
    (0, 1, (0, 0), 0, 2, None),
    (1, 0, (-1, 0), 0, 1, 0),
    (-1, 0, (1, 0), 1, 2, 1),
    (0, 1, (-1, 0), 0, 2, 0),
    (0, 1, (1, 0), 0, 2, 1),
    (0, 1, (2, 0), 0, 1, 6),
    (0, 1, (2, 0), 1, 2, 7),
    (1, 0, (0, 1), 2, 4, 2),
    (-1, 0, (0, 1), 2, 4, 2),
    (1, 0, (-1, 0), 2, 3, 3),
    (-1, 0, (1, 0), 3, 4, 4),
    (1, 0, (-1, 1), 2, 3, 12),
    (-1, 0, (1, 1), 3, 4, 13),
)
GATHER_ORDER = (0, 1, 2, 3, 4, 6, 7, 12, 13, 5, 8, 9, 10, 11, 14, 15, 16, 17)
GATHER_SLOTS = len(GATHER)


def gather(group, view, sems, arrived=None):
    started = []

    def start(slot):
        step, flip, block, a, b, _ = GATHER[slot]

        def copy():
            ref = view(group.member(*block), a, b)
            return remote(ref, ref, sems, slot, group.device(step, flip))

        copy().start()
        started.append(copy)

    for slot, row in enumerate(GATHER):
        if row[5] is None:
            start(slot)
    if arrived:
        arrived((0, 0), 0, 4)
    for slot in GATHER_ORDER:
        step, flip, block, a, b, _ = GATHER[slot]
        yield
        source = (block[0] - step, block[1] ^ flip)
        ref = view(group.member(*source), a, b)
        remote(ref, ref, sems, slot, group.device(step, flip)).wait_recv()
        for later, row in enumerate(GATHER):
            if row[5] == slot:
                start(later)
        if arrived:
            arrived(source, a, b)
    for copy in started:
        copy().wait_send()


SCATTER_SLOTS = 23
HOLD = 7


def add_into(target, *sources):
    total = target[...].astype(F32)
    for source in sources:
        total = total + source[...].astype(F32)
    target[...] = total.astype(target.dtype)


def scatter(group, part, quarters, hold, result, sems):
    started = []

    def held(k, a, b):
        return quarters(hold.at[k], a, b)

    def start(slot, source, step, flip, k, a, b):
        def copy():
            return remote(source(), held(k, a, b), sems, slot, group.device(step, flip))

        copy().start()
        started.append(copy)

    def send_part(slot, block, step, flip, k, a, b):
        start(slot, lambda: part(*block, a, b), step, flip, k, a, b)

    def send_held(slot, source, step, flip, k, a, b):
        start(slot, lambda: held(source, a, b), step, flip, k, a, b)

    def wait(slot, k, a, b):
        ref = held(k, a, b)
        remote(ref, ref, sems, slot, group.device(0, 1)).wait_recv()

    send_part(0, (2, 1), 0, 1, 0, 0, 2)
    send_part(10, (2, 1), 1, 0, 0, 2, 3)
    send_part(11, (2, 1), -1, 0, 0, 3, 4)
    send_part(1, (1, 1), 0, 1, 1, 0, 2)
    send_part(2, (-1, 1), 0, 1, 2, 0, 2)
    send_part(16, (2, 0), 1, 0, 3, 2, 3)
    send_part(17, (2, 0), -1, 0, 3, 3, 4)
    send_part(12, (1, 1), 1, 0, 1, 3, 4)
    send_part(13, (-1, 1), -1, 0, 2, 2, 3)
    send_part(18, (1, 0), 1, 0, 4, 3, 4)
    send_part(19, (-1, 0), -1, 0, 5, 2, 3)
    send_part(3, (0, 1), 0, 1, 3, 0, 2)
    yield
    wait(10, 0, 2, 3)
    add_into(held(0, 2, 3), part(1, 1, 2, 3))
    send_held(14, 0, 1, 0, 1, 2, 3)
    wait(11, 0, 3, 4)
    add_into(held(0, 3, 4), part(-1, 1, 3, 4))
    send_held(15, 0, -1, 0, 2, 3, 4)
    yield
    wait(0, 0, 0, 2)
    add_into(held(0, 0, 2), part(2, 0, 0, 2))
    send_held(4, 0, 1, 0, 4, 0, 1)
    send_held(5, 0, -1, 0, 4, 1, 2)
    yield
    wait(16, 3, 2, 3)
    add_into(held(3, 2, 3), part(1, 0, 2, 3))
    send_held(20, 3, 1, 0, 4, 2, 3)
    wait(17, 3, 3, 4)
    add_into(held(3, 3, 4), part(-1, 0, 3, 4))
    send_held(21, 3, -1, 0, 5, 3, 4)
    yield
    wait(1, 1, 0, 2)
    add_into(held(1, 0, 2), part(1, 0, 0, 2))
    send_held(6, 1, 1, 0, 5, 1, 2)
    wait(2, 2, 0, 2)
    add_into(held(2, 0, 2), part(-1, 0, 0, 2))
    send_held(8, 2, -1, 0, 6, 0, 1)
    yield
    wait(4, 4, 0, 1)
    add_into(held(1, 0, 1), held(4, 0, 1))
    send_held(7, 1, 1, 0, 5, 0, 1)
    wait(5, 4, 1, 2)
    add_into(held(2, 1, 2), held(4, 1, 2))
    send_held(9, 2, -1, 0, 6, 1, 2)
    yield
    wait(12, 1, 3, 4)
    wait(14, 1, 2, 3)
    wait(13, 2, 2, 3)
    wait(15, 2, 3, 4)
    add_into(held(1, 2, 4), held(2, 2, 4), part(0, 1, 2, 4))
    send_held(22, 1, 0, 1, 6, 2, 4)
    yield
    wait(3, 3, 0, 2)
    wait(6, 5, 1, 2)
    wait(8, 6, 0, 1)
    wait(7, 5, 0, 1)
    wait(9, 6, 1, 2)
    result(0, 2, [part(0, 0, 0, 2), held(3, 0, 2), held(5, 0, 2), held(6, 0, 2)])
    yield
    wait(18, 4, 3, 4)
    wait(20, 4, 2, 3)
    wait(19, 5, 2, 3)
    wait(21, 5, 3, 4)
    wait(22, 6, 2, 4)
    result(2, 4, [part(0, 0, 2, 4), held(4, 2, 4), held(5, 2, 4), held(6, 2, 4)])
    for copy in started:
        copy().wait_send()


def total_of(refs):
    total = refs[0][...].astype(F32)
    for ref in refs[1:]:
        total = total + ref[...].astype(F32)
    return total


def drain(*programs):
    programs = list(programs)
    while programs:
        programs = [p for p in programs if next(p, "end") != "end"]


def pairs(count):
    return [pltpu.SemaphoreType.DMA((count,)), pltpu.SemaphoreType.DMA((count,))]


def params(collective_id, mib):
    return pltpu.CompilerParams(
        collective_id=collective_id, has_side_effects=True, vmem_limit_bytes=mib * MIB
    )


ROW_CUTS = (0, 96, 192, 288, 400)


def gather_rows_kernel(x_ref, dy_ref, x_out, dy_out, xs, xr, ds, dr, cs, cr, local):
    group = Group("fsdp")
    core = group.core
    width = x_ref.shape[1]
    partner = other_core(group)

    def x_view(member, a, b):
        columns = pl.ds(pl.multiple_of(member * width, width), width)
        return x_out.at[core, pl.ds(ROW_CUTS[a], ROW_CUTS[b] - ROW_CUTS[a]), columns]

    def dy_view(member, a, b):
        columns = pl.ds(pl.multiple_of(member * width, width), width)
        return dy_out.at[core, pl.ds(96 * a, 96 * (b - a)), columns]

    copies = [
        pltpu.make_async_copy(x_ref, x_view(group.me, 0, 4), local.at[0]),
        pltpu.make_async_copy(dy_ref, dy_view(group.me, 0, 4), local.at[1]),
    ]
    for copy in copies:
        copy.start()
    barrier(group.neighbours() + [partner])
    for copy in copies:
        copy.wait()
    drain(gather(group, x_view, (xs, xr)), gather(group, dy_view, (ds, dr)))
    last = [
        remote(x_out.at[core], x_out.at[core], (cs, cr), 0, partner),
        remote(dy_out.at[core], dy_out.at[core], (cs, cr), 1, partner),
    ]
    for copy in last:
        copy.start()
    for copy in last:
        copy.wait()


def gather_rows(x, dy):
    return pl.pallas_call(
        gather_rows_kernel,
        out_shape=[
            jax.ShapeDtypeStruct((2, x.shape[0], 2048), BF16),
            jax.ShapeDtypeStruct((2, dy.shape[0], 2048), BF16),
        ],
        in_specs=[ANY, ANY],
        out_specs=[ANY, ANY],
        scratch_shapes=pairs(GATHER_SLOTS) + pairs(GATHER_SLOTS) + pairs(2) + [pltpu.SemaphoreType.DMA((2,))],
        compiler_params=params(0, 32),
        name="gather_rows",
    )(x, dy)


def gather_keys_kernel(kv_ref, out, send, recv, local):
    group = Group("ctx")
    rows = kv_ref.shape[0]
    step = rows // 4

    def view(member, a, b):
        return out.at[member, pl.ds(step * a, step * (b - a)), :]

    copy = pltpu.make_async_copy(kv_ref, view(group.me, 0, 4), local.at[0])
    copy.start()
    barrier(group.neighbours())
    copy.wait()
    drain(gather(group, view, (send, recv)))


def gather_keys(kv):
    return pl.pallas_call(
        gather_keys_kernel,
        out_shape=jax.ShapeDtypeStruct((8,) + kv.shape, BF16),
        in_specs=[ANY],
        out_specs=ANY,
        scratch_shapes=pairs(GATHER_SLOTS) + [pltpu.SemaphoreType.DMA((1,))],
        compiler_params=params(1, 32),
        name="gather_keys",
    )(kv)


def cut_rows(ref, a, b):
    step = ref.shape[0] // 4
    return ref.at[pl.ds(step * a, step * (b - a)), :]


def scatter_keys_kernel(part_ref, out, hold, send, recv):
    group = Group("ctx")
    barrier(group.neighbours())

    def part(step, flip, a, b):
        return cut_rows(part_ref.at[group.member(step, flip)], a, b)

    def result(a, b, refs):
        target = cut_rows(out, a, b)
        target[...] = total_of(refs)

    drain(scatter(group, part, cut_rows, hold, result, (send, recv)))


def scatter_keys(part):
    return pl.pallas_call(
        scatter_keys_kernel,
        out_shape=jax.ShapeDtypeStruct(part.shape[1:], F32),
        in_specs=[VMEM],
        out_specs=VMEM,
        scratch_shapes=[pltpu.VMEM((HOLD,) + part.shape[1:], BF16)] + pairs(SCATTER_SLOTS),
        compiler_params=params(2, 48),
        name="scatter_keys",
    )(part)


def rows_scatter(group, part_ref, out, arriving, hold, sems):
    cs, cr, send, recv = sems
    core, partner = group.core, other_core(group)

    def exchange():
        return remote(part_ref.at[1 - core], arriving, (cs, cr), 0, partner)

    exchange().start()
    yield
    exchange().wait()

    def one(i, carry):
        rows = pl.ds(pl.multiple_of(i * 32, 32), 32)
        arriving[rows, :] = (arriving[rows, :].astype(F32) + part_ref[core, rows, :].astype(F32)).astype(BF16)
        return carry

    lax.fori_loop(0, arriving.shape[0] // 32, one, 0)
    width = out.shape[1]

    def part(step, flip, a, b):
        columns = pl.ds(pl.multiple_of(group.member(step, flip) * width, width), width)
        return arriving.at[pl.ds(96 * a, 96 * (b - a)), columns]

    def result(a, b, refs):
        target = cut_rows(out, a, b)
        target[...] = total_of(refs)

    yield from scatter(group, part, cut_rows, hold, result, (send, recv))


def scatter_rows_kernel(part_ref, out, arriving, hold, *sems):
    group = Group("fsdp")
    barrier(group.neighbours() + [other_core(group)])
    drain(rows_scatter(group, part_ref, out, arriving, hold, sems))


def scatter_rows(part, collective_id):
    rows, width = part.shape[1], part.shape[2] // 8
    return pl.pallas_call(
        scatter_rows_kernel,
        out_shape=jax.ShapeDtypeStruct((rows, width), F32),
        in_specs=[VMEM],
        out_specs=VMEM,
        scratch_shapes=[pltpu.VMEM((rows, part.shape[2]), BF16), pltpu.VMEM((HOLD, rows, width), BF16)]
        + pairs(1)
        + pairs(SCATTER_SLOTS),
        compiler_params=params(collective_id, 32),
        name="scatter_rows",
    )(part)


def sum_small_kernel(axis, x_ref, out, hold, send, recv):
    ctx, fsdp = lax.axis_index("ctx"), lax.axis_index("fsdp")
    count = lax.axis_size(axis)
    me = ctx if axis == "ctx" else fsdp

    def device(offset):
        other = lax.rem(me + offset, count)
        return (other, fsdp) if axis == "ctx" else (ctx, other)

    barrier([device(offset) for offset in range(1, count)])
    copies = [
        remote(x_ref, hold.at[offset - 1], (send, recv), offset - 1, device(offset))
        for offset in range(1, count)
    ]
    for copy in copies:
        copy.start()
    total = x_ref[...]
    for offset in range(1, count):
        copies[offset - 1].wait_recv()
        total = total + hold[offset - 1]
    out[...] = total
    for copy in copies:
        copy.wait_send()


def sum_small(x, axis, collective_id):
    count = lax.axis_size(axis) - 1
    return pl.pallas_call(
        partial(sum_small_kernel, axis),
        out_shape=jax.ShapeDtypeStruct(x.shape, F32),
        in_specs=[VMEM],
        out_specs=VMEM,
        scratch_shapes=[pltpu.VMEM((count,) + x.shape, F32)] + pairs(count),
        compiler_params=params(collective_id, 16),
        name="sum_small",
    )(x)


REDUCE_SEMS = 6


def reduce_one(group, source, target, hold, sems):
    rs, rr, gs, gr, cs, cr = sems
    core, partner = group.core, other_core(group)
    rows, width = source.shape[0] // 8, source.shape[1]
    by_rows = rows % 64 == 0

    def quarters(ref, a, b):
        if by_rows:
            return ref.at[pl.ds(rows // 4 * a, rows // 4 * (b - a)), :]
        return ref.at[:, pl.ds(width // 4 * a, width // 4 * (b - a))]

    def part(step, flip, a, b):
        start = pl.multiple_of(group.member(step, flip) * rows, rows)
        return quarters(source.at[pl.ds(start, rows), :], a, b)

    def view(member, a, b):
        start = pl.multiple_of(member * rows, rows)
        return quarters(target.at[core, pl.ds(start, rows), :], a, b)

    def result(a, b, terms):
        place = view(group.me, a, b)
        place[...] = total_of(terms).astype(BF16)

    copies = []

    def arrived(block, a, b):
        slot = len(copies)

        def copy():
            ref = view(group.member(*block), a, b)
            return remote(ref, ref, (cs, cr), slot, partner)

        copy().start()
        copies.append(copy)

    yield from scatter(group, part, quarters, hold, result, (rs, rr))
    yield from gather(group, view, (gs, gr), arrived)
    yield
    for copy in copies:
        copy().wait()


def reduce_scratch(shape):
    return pltpu.VMEM((HOLD, shape[0] // 8, shape[1]), BF16)


def reduce_sems():
    return pairs(SCATTER_SLOTS) + pairs(GATHER_SLOTS) + pairs(GATHER_SLOTS + 1)


def reduce_weights_kernel(count, *refs):
    ins, outs = refs[:count], refs[count : 2 * count]
    holds = refs[2 * count : 3 * count]
    sems = refs[3 * count :]
    group = Group("ctx")
    barrier(group.neighbours() + [other_core(group)])
    drain(*[reduce_one(group, ins[i], outs[i], holds[i], sems[6 * i : 6 * i + 6]) for i in range(count)])


def reduce_weights(parts, collective_id):
    count = len(parts)
    return pl.pallas_call(
        partial(reduce_weights_kernel, count),
        out_shape=[jax.ShapeDtypeStruct((2,) + x.shape, BF16) for x in parts],
        in_specs=[VMEM] * count,
        out_specs=[VMEM] * count,
        scratch_shapes=[reduce_scratch(x.shape) for x in parts] + reduce_sems() * count,
        compiler_params=params(collective_id, 60),
        name="reduce_weights",
    )(*parts)


TILE = 2 * GROUP
TILES = SEQ_LEN // TILE
ITEMS = TILES + 1
NT = (((1,), (1,)), ((), ()))
TN = (((0,), (0,)), ((), ()))


def dot(a, b, dims=(((1,), (0,)), ((), ()))):
    return lax.dot_general(a, b, dims, preferred_element_type=F32)


STATES = 11


def state_of(j):
    late = lax.div(j + 7, 16)
    return j * (1 - late) + (9 + lax.rem(j, 2)) * late


class Steps:
    def __init__(self, *programs):
        self.programs = list(programs)

    def take(self, count=1):
        for _ in range(count):
            self.programs = [p for p in self.programs if next(p, "end") != "end"]

    def at(self, j, plan):
        for iteration, count in plan:
            pl.when(j == iteration)(partial(self.take, count))

    def finish(self):
        drain(*self.programs)


FORWARD_PLAN = ((1, 1), (3, 1), (5, 1), (8, 1), (10, 1), (13, 1), (15, 1))
BACKWARD_PLAN = ((1, 1), (2, 1), (3, 1), (4, 2), (5, 1), (6, 2), (7, 1), (8, 2), (9, 1), (10, 2), (11, 1), (12, 2), (13, 1), (14, 1), (15, 1))
BRANCH_PLAN = ((0, 1), (1, 1), (2, 1), (4, 1), (6, 1), (8, 1), (10, 1), (12, 1), (14, 1))


def attention_kernel(
    table, qd_ref, kv_ref, begin_ref, ff_ref, wo_ref, inner_part, outer_part,
    att_ref, dq_ref, dkv_ref, sum_ref, inner_out, outer_out,
    kvp, state_ml, state_acc, dq_items, dkv_items, lse_ref, delta_ref, branch, arriving, branch_hold, inner_hold, outer_hold, *sems
):
    lane = lax.broadcasted_iota(jnp.int32, (1, 128), 1)
    left = lane < HEAD_DIM
    across, along = Group("ctx"), Group("fsdp")
    barrier(across.neighbours() + along.neighbours() + [other_core(across)])
    weights_steps = Steps(
        reduce_one(across, inner_part, inner_out, inner_hold, sems[:6]),
        reduce_one(across, outer_part, outer_out, outer_hold, sems[6:12]),
    )
    branch_steps = Steps(rows_scatter(along, branch, sum_ref, arriving, branch_hold, sems[12:]))
    weights_steps.take()

    def place(g, carry):
        tile, half = lax.div(g, 2), lax.rem(g, 2)
        kvp[tile, pl.ds(pl.multiple_of(half * GROUP, GROUP), GROUP), :] = kv_ref[table[g]]
        return carry

    lax.fori_loop(0, GROUPS, place, 0)

    def bit(number):
        return jnp.minimum(jnp.maximum(number, 0), 1)

    def pair_facts(p):
        g0, g1 = table[32 + 2 * p], table[33 + 2 * p]
        low, high = jnp.minimum(g0, g1), jnp.maximum(g0, g1)
        return low, high, bit(g0 - g1), lax.div(low, 2) + 1

    def item_facts(p, j):
        low, high, low_slot, count = pair_facts(p)
        second = bit(j - count + 1)
        tile = second * TILES + (1 - second) * (count - 1) - j
        slot = 2 * p + second * (1 - low_slot) + (1 - second) * low_slot
        position = (second * high + (1 - second) * low) * GROUP
        key_pos = tile * TILE + lax.broadcasted_iota(jnp.int32, (1, TILE), 1)
        query_pos = position + lax.broadcasted_iota(jnp.int32, (GROUP, 1), 0)
        allowed = (key_pos <= query_pos) & (key_pos >= begin_ref[slot])
        keep = bit(j * (j - count) * (j - count)).astype(F32)
        return tile, slot, allowed, keep

    def final_item(p, i):
        low, high, low_slot, count = pair_facts(p)
        is_low = low_slot if i else 1 - low_slot
        return count * is_low + 10 * (1 - is_low)

    for p in range(2):
        for h in range(2):
            state_ml[p, h, 0] = jnp.where(left, jnp.full((GROUP, 128), FLOOR, F32), 0.0)
            state_acc[p, h, 0] = jnp.zeros((GROUP, 128), F32)

    def forward(j, carry):
        weights_steps.at(j, FORWARD_PLAN)
        now, after = state_of(j), state_of(j + 1)
        for p in range(2):
            tile, slot, allowed, keep = item_facts(p, j)
            for h in range(2):
                lanes = slice(128 * h, 128 * h + 128)
                queries = jnp.where(left, qd_ref[slot, :, lanes], 0).astype(BF16)
                keys = kvp[tile, :, lanes]
                scores = jnp.where(allowed, dot(queries, keys, NT), MASKED)
                state = state_ml[p, h, now]
                old_max = state[:, :1] * keep + FLOOR * (1.0 - keep)
                new_max = jnp.maximum(old_max, jnp.max(scores, axis=1, keepdims=True))
                weights = jnp.exp(scores - new_max)
                factor = jnp.exp(old_max - new_max)
                new_sum = state[:, HEAD_DIM : HEAD_DIM + 1] * factor + jnp.sum(weights, axis=1, keepdims=True)
                state_ml[p, h, after] = jnp.where(left, new_max, new_sum)
                state_acc[p, h, after] = state_acc[p, h, now] * factor + dot(weights.astype(BF16), keys)
        return carry

    lax.fori_loop(0, ITEMS, forward, 0)

    for p in range(2):
        for i in range(2):
            item = final_item(p, i)
            slot = 2 * p + i
            outs = []
            for h in range(2):
                state = state_ml[p, h, item]
                total = state[:, HEAD_DIM : HEAD_DIM + 1]
                out = state_acc[p, h, item] / total
                outs.append(out)
                lse = state[:, :1] + jnp.log(total)
                lse_ref[h, slot] = jnp.broadcast_to(lse, (GROUP, 128))
                cotangent = qd_ref[slot, :, 128 * h : 128 * h + 128].astype(F32)
                product = jnp.where(left, 0.0, cotangent * out)
                delta_ref[h, slot] = jnp.broadcast_to(jnp.sum(product, axis=1, keepdims=True), (GROUP, 128))
            att_ref[slot] = jnp.where(left, pltpu.roll(outs[0], HEAD_DIM, 1), outs[1]).astype(BF16)

    def branches(i, carry):
        slot, columns = lax.div(i, 4), pl.ds(pl.multiple_of(lax.rem(i, 4) * 512, 512), 512)
        core, rows = lax.div(slot, 2), pl.ds(pl.multiple_of(lax.rem(slot, 2) * GROUP, GROUP), GROUP)
        branch[core, rows, columns] = (ff_ref[core, rows, columns].astype(F32) + dot(att_ref[slot], wo_ref[:, columns])).astype(BF16)
        return carry

    lax.fori_loop(0, 16, branches, 0)
    branch_steps.take()

    for p in range(2):
        dq_items[p, 0] = jnp.zeros((GROUP, 256), F32)

    def backward(j, carry):
        weights_steps.at(j, BACKWARD_PLAN)
        branch_steps.at(j, BRANCH_PLAN)
        now, after = state_of(j), state_of(j + 1)
        for p in range(2):
            tile, slot, allowed, keep = item_facts(p, j)
            for h in range(2):
                lanes = slice(128 * h, 128 * h + 128)
                both = qd_ref[slot, :, lanes]
                queries = jnp.where(left, both, 0).astype(BF16)
                cotangent = jnp.where(left, 0, both).astype(BF16)
                keys = kvp[tile, :, lanes]
                scores = dot(queries, keys, NT)
                probs = jnp.where(allowed, jnp.exp(scores - lse_ref[h, slot][:, :1]), 0.0)
                prob_grad = dot(cotangent, keys, NT)
                score_grad = (probs * (prob_grad - delta_ref[h, slot][:, :1])).astype(BF16)
                dq_items[p, after, :, lanes] = dq_items[p, now, :, lanes] * keep + dot(score_grad, keys)
                grad = dot(score_grad, queries, TN) + dot(probs.astype(BF16), cotangent, TN)
                dkv_items[p, j, 0, :, lanes] = grad[:GROUP].astype(BF16)
                dkv_items[p, j, 1, :, lanes] = grad[GROUP:].astype(BF16)
        return carry

    lax.fori_loop(0, ITEMS, backward, 0)

    for p in range(2):
        for i in range(2):
            item = final_item(p, i)
            grad = dq_items[p, item]
            dq_ref[2 * p + i] = jnp.where(left, grad[:, :128], pltpu.roll(grad[:, 128:], HEAD_DIM, 1))

    counts = [pair_facts(p)[3] for p in range(2)]

    def collect(s, carry):
        group = table[36 + s]
        tile, half = lax.div(group, 2), lax.rem(group, 2)
        total = jnp.zeros((GROUP, 256), F32)
        for p in range(2):
            low_item = dkv_items[p, jnp.maximum(counts[p] - 1 - tile, 0), half].astype(F32)
            high_item = dkv_items[p, jnp.maximum(TILES - tile, counts[p]), half].astype(F32)
            total = total + low_item * bit(counts[p] - tile).astype(F32)
            total = total + high_item * bit(TILES - tile - counts[p] + 1).astype(F32)
        dkv_ref[s] = total.astype(BF16)
        return carry

    lax.fori_loop(0, GROUPS, collect, 0)
    branch_steps.finish()
    weights_steps.finish()


def attention(table, qd, kv, begin, ff, wo, inner_part, outer_part):
    rows, width = ff.shape[1], ff.shape[2]
    return pl.pallas_call(
        attention_kernel,
        out_shape=[
            jax.ShapeDtypeStruct((4, GROUP, 128), BF16),
            jax.ShapeDtypeStruct((4, GROUP, 128), F32),
            jax.ShapeDtypeStruct((GROUPS, GROUP, 256), BF16),
            jax.ShapeDtypeStruct((rows, width // 8), F32),
            jax.ShapeDtypeStruct((2,) + inner_part.shape, BF16),
            jax.ShapeDtypeStruct((2,) + outer_part.shape, BF16),
        ],
        in_specs=[SMEM] + [VMEM] * 7,
        out_specs=[VMEM] * 6,
        scratch_shapes=[
            pltpu.VMEM((TILES, TILE, 256), BF16),
            pltpu.VMEM((2, 2, STATES, GROUP, 128), F32),
            pltpu.VMEM((2, 2, STATES, GROUP, 128), F32),
            pltpu.VMEM((2, STATES, GROUP, 256), F32),
            pltpu.VMEM((2, ITEMS, 2, GROUP, 256), BF16),
            pltpu.VMEM((2, 4, GROUP, 128), F32),
            pltpu.VMEM((2, 4, GROUP, 128), F32),
            pltpu.VMEM(ff.shape, BF16),
            pltpu.VMEM((rows, width), BF16),
            pltpu.VMEM((HOLD, rows, width // 8), BF16),
            reduce_scratch(inner_part.shape),
            reduce_scratch(outer_part.shape),
        ]
        + reduce_sems() * 2
        + pairs(1)
        + pairs(SCATTER_SLOTS),
        compiler_params=params(8, 62),
        name="attention",
    )(table, qd, kv, begin, ff, wo, inner_part, outer_part)


def turn(values, cosine, sine):
    first, second = values[..., : ROT // 2], values[..., ROT // 2 : ROT]
    return jnp.concatenate(
        [first * cosine - second * sine, second * cosine + first * sine, values[..., ROT:]], axis=-1
    )


def body(
    layer_input,
    norm_gain,
    norm_bias,
    query_weight,
    query_bias,
    key_weight,
    key_bias,
    value_weight,
    value_bias,
    out_weight,
    out_bias,
    inner_weight,
    inner_bias,
    outer_weight,
    outer_bias,
    output_grad,
    group_order,
    sequence_ids,
):
    ctx = lax.axis_index("ctx")
    fsdp = lax.axis_index("fsdp")
    core = lax.rem(ctx, 2)
    rows = layer_input.shape[0]
    both = 2 * rows

    def half(array, axis):
        size = array.shape[axis] // 2
        return lax.dynamic_slice_in_dim(array, core * size, size, axis)

    wq, wk, wv = half(query_weight, 1), half(key_weight, 1), half(value_weight, 1)
    wo, wi, wu = half(out_weight, 0), half(inner_weight, 1), half(outer_weight, 0)
    bq, bk, bv, bi = half(query_bias, 0), half(key_bias, 0), half(value_bias, 0), half(inner_bias, 0)

    slots = lax.div(ctx, 2) * 4 + jnp.arange(4, dtype=jnp.int32)
    my_groups = group_order[slots]
    position = (my_groups[:, None] * GROUP + jnp.arange(GROUP, dtype=jnp.int32)[None, :]).reshape(both)
    begins = jnp.sum(
        (sequence_ids[None, :] < jnp.arange(DOCS, dtype=jnp.int32)[:, None]).astype(jnp.int32), axis=1
    )
    my_docs = sequence_ids.reshape(GROUPS, GROUP)[my_groups]
    begin = jnp.zeros((4, GROUP), jnp.int32)
    for doc in range(1, DOCS):
        begin = jnp.where(my_docs == doc, begins[doc], begin)
    slot_of = jnp.sum(
        jnp.where(group_order[None, :] == jnp.arange(GROUPS)[:, None], jnp.arange(GROUPS)[None, :], 0), axis=1
    ).astype(jnp.int32)
    table = jnp.concatenate([slot_of, my_groups, group_order]).astype(jnp.int32)
    freqs = 10000.0 ** (-(jnp.arange(ROT // 2, dtype=F32) * 2.0 / ROT))
    angles = position.astype(F32)[:, None] * freqs[None, :]
    cosine, sine = jnp.cos(angles)[:, None, :], jnp.sin(angles)[:, None, :]

    extra = jnp.concatenate([norm_gain[None], norm_bias[None], jnp.zeros((14, norm_gain.shape[0]), BF16)])
    x_all, dy_all = gather_rows(jnp.concatenate([layer_input, extra]), output_grad)
    gain = x_all[0, rows].astype(F32)
    shift = x_all[0, rows + 1].astype(F32)
    dy = dy_all.reshape(both, -1)
    inputs = x_all[:, :rows].reshape(both, -1).astype(F32)
    row_mean = jnp.mean(inputs, axis=-1, keepdims=True)
    centered = inputs - row_mean
    inv_std = lax.rsqrt(jnp.mean(centered * centered, axis=-1, keepdims=True) + EPS)
    normed = (centered * inv_std * gain + shift).astype(BF16)

    def project(matrix, vector):
        return jnp.dot(normed, matrix, preferred_element_type=F32) + vector.astype(F32)

    queries = turn(project(wq, bq).reshape(both, 2, HEAD_DIM), cosine, sine).astype(BF16)
    keys = turn(project(wk, bk).reshape(both, 2, HEAD_DIM), cosine, sine).astype(BF16)
    values = project(wv, bv).astype(BF16).reshape(both, 2, HEAD_DIM)
    kv = jnp.concatenate([keys, values], axis=-1).reshape(both, 256)
    kv_all = gather_keys(kv).reshape(GROUPS, GROUP, 256)
    attended_grad = jnp.einsum("rd,cd->rc", dy, wo, preferred_element_type=F32).astype(BF16)
    scaled = (queries.astype(F32) * HEAD_DIM ** (-0.5)).astype(BF16)
    qd = jnp.concatenate([scaled, attended_grad.reshape(both, 2, HEAD_DIM)], axis=-1).reshape(4, GROUP, 256)
    inner = project(wi, bi)
    activated = jax.nn.gelu(inner, approximate=True).astype(BF16)
    act_grad = jnp.einsum("rd,fd->rf", dy, wu, preferred_element_type=F32)
    _, gelu_pull = jax.vjp(partial(jax.nn.gelu, approximate=True), inner)
    inner_grad = gelu_pull(act_grad)[0].astype(BF16)
    ff = jnp.dot(activated, wu, preferred_element_type=F32).astype(BF16).reshape(2, rows, -1)

    def weight_grad(left, right):
        return jnp.einsum("rc,rd->cd", left, right, preferred_element_type=F32).astype(BF16)

    attended, dq, dkv, summed, inner_w_grad, outer_w_grad = attention(
        table, qd, kv_all, begin[:, :, None], ff, wo, weight_grad(normed, inner_grad), weight_grad(activated, dy)
    )
    attended = attended.reshape(both, 128)
    dkv_own = scatter_keys(dkv.reshape(8, both, 256))
    layer_output = (
        layer_input.astype(F32) + summed + out_bias.astype(F32) + outer_bias.astype(F32)
    ).astype(BF16)

    query_pre_grad = turn(dq.reshape(both, 2, HEAD_DIM) * HEAD_DIM ** (-0.5), cosine, -sine)
    query_pre_grad = query_pre_grad.reshape(both, 128).astype(BF16)
    dkv_own = dkv_own.reshape(both, 2, 128)
    key_pre_grad = turn(dkv_own[..., :HEAD_DIM], cosine, -sine).reshape(both, 128).astype(BF16)
    value_pre_grad = dkv_own[..., HEAD_DIM:].reshape(both, 128).astype(BF16)
    pre_grads = jnp.concatenate([query_pre_grad, key_pre_grad, value_pre_grad], axis=1)
    normed_grad = jnp.einsum("rf,df->rd", inner_grad, wi, preferred_element_type=F32) + jnp.einsum(
        "rc,dc->rd", pre_grads, jnp.concatenate([wq, wk, wv], axis=1), preferred_element_type=F32
    )
    local_grad = scatter_rows(normed_grad.astype(BF16).reshape(2, rows, -1), 4)
    my_mean = lax.dynamic_slice_in_dim(row_mean, core * rows, rows, 0)
    my_inv = lax.dynamic_slice_in_dim(inv_std, core * rows, rows, 0)
    unit = (layer_input.astype(F32) - my_mean) * my_inv
    scaled_grad = local_grad * norm_gain.astype(F32)
    sums = jnp.stack([jnp.sum(scaled_grad, axis=1), jnp.sum(scaled_grad * unit, axis=1)])
    sums = sum_small(jnp.pad(sums, ((0, 6), (0, 0))), "fsdp", 5) * (1.0 / 2048)
    input_grad = output_grad.astype(F32) + my_inv * (scaled_grad - sums[0][:, None] - unit * sums[1][:, None])

    def spread(vector):
        out = jnp.zeros((2,) + vector.shape, F32)
        return lax.dynamic_update_index_in_dim(out, vector, core, 0).reshape(-1)

    def columns(array):
        return jnp.sum(array.astype(F32), axis=0)

    vectors = jnp.concatenate(
        [
            jnp.sum(local_grad * unit, axis=0),
            columns(local_grad),
            columns(output_grad),
            spread(columns(query_pre_grad)),
            spread(columns(key_pre_grad)),
            spread(columns(value_pre_grad)),
            spread(columns(inner_grad)),
        ]
    ).reshape(10, 256)
    vectors = sum_small(jnp.pad(vectors, ((0, 6), (0, 0))), "ctx", 6)
    qkv_grad, out_grad = reduce_weights([weight_grad(normed, pre_grads), weight_grad(attended, dy)], 7)

    def side_by_side(array):
        return jnp.concatenate([array[0], array[1]], axis=1).astype(F32)

    return (
        layer_output,
        input_grad,
        vectors[0],
        vectors[1],
        side_by_side(qkv_grad[:, :, :128]),
        vectors[3],
        side_by_side(qkv_grad[:, :, 128:256]),
        vectors[4],
        side_by_side(qkv_grad[:, :, 256:]),
        vectors[5],
        out_grad.reshape(256, 2048).astype(F32),
        vectors[2],
        side_by_side(inner_w_grad),
        vectors[6:10].reshape(1024),
        outer_w_grad.reshape(1024, 2048).astype(F32),
        vectors[2],
    )


def solution(mesh):
    in_specs = (
        P("ctx", "fsdp"),
        P("fsdp"),
        P("fsdp"),
        P(None, "fsdp"),
        P("fsdp"),
        P(None, "fsdp"),
        P("fsdp"),
        P(None, "fsdp"),
        P("fsdp"),
        P("fsdp", None),
        P("fsdp"),
        P(None, "fsdp"),
        P("fsdp"),
        P("fsdp", None),
        P("fsdp"),
        P("ctx", "fsdp"),
        P(),
        P(),
    )
    out_specs = (
        P("ctx", "fsdp"),
        P("ctx", "fsdp"),
        P("fsdp"),
        P("fsdp"),
        P(None, "fsdp"),
        P("fsdp"),
        P(None, "fsdp"),
        P("fsdp"),
        P(None, "fsdp"),
        P("fsdp"),
        P("fsdp", None),
        P("fsdp"),
        P(None, "fsdp"),
        P("fsdp"),
        P("fsdp", None),
        P("fsdp"),
    )
    return jax.shard_map(body, mesh=mesh, in_specs=in_specs, out_specs=out_specs, check_vma=False)
```

```python
from functools import partial

import jax
import jax.numpy as jnp
from jax import lax
from jax.experimental import pallas as pl
from jax.experimental.pallas import tpu as pltpu
from jax.sharding import PartitionSpec as P

HEAD_DIM = 64
ROT = 32
GROUP = 192
GROUPS = 32
SEQ_LEN = 6144
DOCS = 5
EPS = 1e-05
MASKED = -1e30
FLOOR = -1e29
MESH = pl.DeviceIdType.MESH
BF16 = jnp.bfloat16
F32 = jnp.float32
ANY = pl.BlockSpec(memory_space=pl.ANY)
VMEM = pl.BlockSpec(memory_space=pltpu.VMEM)
SMEM = pl.BlockSpec(memory_space=pltpu.SMEM)
MIB = 2**20


class Group:
    def __init__(self, axis):
        ctx, fsdp = lax.axis_index("ctx"), lax.axis_index("fsdp")
        self.axis, self.ctx, self.fsdp = axis, ctx, fsdp
        self.core = lax.rem(ctx, 2)
        self.me = lax.div(ctx, 2) if axis == "ctx" else fsdp
        self.ring, self.pair = lax.rem(self.me, 4), lax.div(self.me, 4)

    def member(self, step, flip):
        pair = 1 - self.pair if flip else self.pair
        return pair * 4 + lax.rem(self.ring + (step + 4), 4)

    def device(self, step, flip):
        member = self.member(step, flip)
        if self.axis == "ctx":
            return (member * 2 + self.core, self.fsdp)
        return (self.ctx, member)

    def neighbours(self):
        return [self.device(1, 0), self.device(-1, 0), self.device(0, 1)]


def other_core(group):
    return (group.ctx + 1 - 2 * group.core, group.fsdp)


def barrier(devices):
    semaphore = pltpu.get_barrier_semaphore()
    for device in devices:
        pl.semaphore_signal(semaphore, inc=1, device_id=device, device_id_type=MESH)
    pl.semaphore_wait(semaphore, len(devices))


def remote(source, target, sems, slot, device):
    return pltpu.make_async_remote_copy(
        src_ref=source,
        dst_ref=target,
        send_sem=sems[0].at[slot],
        recv_sem=sems[1].at[slot],
        device_id=device,
        device_id_type=MESH,
    )


GATHER = (
    (1, 0, (0, 0), 0, 2, None),
    (-1, 0, (0, 0), 0, 2, None),
    (0, 1, (0, 0), 2, 4, None),
    (1, 0, (0, 0), 2, 4, None),
    (-1, 0, (0, 0), 2, 4, None),
    (0, 1, (0, 0), 0, 2, None),
    (1, 0, (-1, 0), 0, 1, 0),
    (-1, 0, (1, 0), 1, 2, 1),
    (0, 1, (-1, 0), 0, 2, 0),
    (0, 1, (1, 0), 0, 2, 1),
    (0, 1, (2, 0), 0, 1, 6),
    (0, 1, (2, 0), 1, 2, 7),
    (1, 0, (0, 1), 2, 4, 2),
    (-1, 0, (0, 1), 2, 4, 2),
    (1, 0, (-1, 0), 2, 3, 3),
    (-1, 0, (1, 0), 3, 4, 4),
    (1, 0, (-1, 1), 2, 3, 12),
    (-1, 0, (1, 1), 3, 4, 13),
)
GATHER_ORDER = (0, 1, 2, 3, 4, 6, 7, 12, 13, 5, 8, 14, 15, 9, 10, 16, 17, 11)
GATHER_SLOTS = len(GATHER)


def gather(group, view, sems, arrived=None):
    started = []

    def start(slot):
        step, flip, block, a, b, _ = GATHER[slot]

        def copy():
            ref = view(group.member(*block), a, b)
            return remote(ref, ref, sems, slot, group.device(step, flip))

        copy().start()
        started.append(copy)

    for slot, row in enumerate(GATHER):
        if row[5] is None:
            start(slot)
    if arrived:
        arrived((0, 0), 0, 4)
    for slot in GATHER_ORDER:
        step, flip, block, a, b, _ = GATHER[slot]
        yield
        source = (block[0] - step, block[1] ^ flip)
        ref = view(group.member(*source), a, b)
        remote(ref, ref, sems, slot, group.device(step, flip)).wait_recv()
        for later, row in enumerate(GATHER):
            if row[5] == slot:
                start(later)
        if arrived:
            arrived(source, a, b)
    for copy in started:
        copy().wait_send()


SCATTER_SLOTS = 23
HOLD = 7


def add_into(target, *sources):
    total = target[...].astype(F32)
    for source in sources:
        total = total + source[...].astype(F32)
    target[...] = total.astype(target.dtype)


def scatter(group, part, quarters, hold, result, sems, pair_first=True):
    started = []

    def held(k, a, b):
        return quarters(hold.at[k], a, b)

    def start(slot, source, step, flip, k, a, b):
        def copy():
            return remote(source(), held(k, a, b), sems, slot, group.device(step, flip))

        copy().start()
        started.append(copy)

    def send_part(slot, block, step, flip, k, a, b):
        start(slot, lambda: part(*block, a, b), step, flip, k, a, b)

    def send_held(slot, source, step, flip, k, a, b):
        start(slot, lambda: held(source, a, b), step, flip, k, a, b)

    def wait(slot, k, a, b):
        ref = held(k, a, b)
        remote(ref, ref, sems, slot, group.device(0, 1)).wait_recv()

    if pair_first:
        send_part(0, (2, 1), 0, 1, 0, 0, 2)
    send_part(10, (2, 1), 1, 0, 0, 2, 3)
    send_part(11, (2, 1), -1, 0, 0, 3, 4)
    if pair_first:
        send_part(1, (1, 1), 0, 1, 1, 0, 2)
        send_part(2, (-1, 1), 0, 1, 2, 0, 2)
    send_part(16, (2, 0), 1, 0, 3, 2, 3)
    send_part(17, (2, 0), -1, 0, 3, 3, 4)
    send_part(12, (1, 1), 1, 0, 1, 3, 4)
    send_part(13, (-1, 1), -1, 0, 2, 2, 3)
    send_part(18, (1, 0), 1, 0, 4, 3, 4)
    send_part(19, (-1, 0), -1, 0, 5, 2, 3)
    if pair_first:
        send_part(3, (0, 1), 0, 1, 3, 0, 2)
    yield
    wait(10, 0, 2, 3)
    add_into(held(0, 2, 3), part(1, 1, 2, 3))
    send_held(14, 0, 1, 0, 1, 2, 3)
    wait(11, 0, 3, 4)
    add_into(held(0, 3, 4), part(-1, 1, 3, 4))
    send_held(15, 0, -1, 0, 2, 3, 4)
    if pair_first:
        yield
        wait(0, 0, 0, 2)
        add_into(held(0, 0, 2), part(2, 0, 0, 2))
        send_held(4, 0, 1, 0, 4, 0, 1)
        send_held(5, 0, -1, 0, 4, 1, 2)
    yield
    wait(16, 3, 2, 3)
    add_into(held(3, 2, 3), part(1, 0, 2, 3))
    send_held(20, 3, 1, 0, 4, 2, 3)
    wait(17, 3, 3, 4)
    add_into(held(3, 3, 4), part(-1, 0, 3, 4))
    send_held(21, 3, -1, 0, 5, 3, 4)
    if pair_first:
        yield
        wait(1, 1, 0, 2)
        add_into(held(1, 0, 2), part(1, 0, 0, 2))
        send_held(6, 1, 1, 0, 5, 1, 2)
    yield
    wait(12, 1, 3, 4)
    wait(14, 1, 2, 3)
    wait(13, 2, 2, 3)
    wait(15, 2, 3, 4)
    add_into(held(1, 2, 4), held(2, 2, 4), part(0, 1, 2, 4))
    send_held(22, 1, 0, 1, 6, 2, 4)
    if pair_first:
        yield
        wait(2, 2, 0, 2)
        add_into(held(2, 0, 2), part(-1, 0, 0, 2))
        send_held(8, 2, -1, 0, 6, 0, 1)
        yield
        wait(4, 4, 0, 1)
        add_into(held(1, 0, 1), held(4, 0, 1))
        send_held(7, 1, 1, 0, 5, 0, 1)
        wait(5, 4, 1, 2)
        add_into(held(2, 1, 2), held(4, 1, 2))
        send_held(9, 2, -1, 0, 6, 1, 2)
        yield
        wait(3, 3, 0, 2)
        wait(6, 5, 1, 2)
        wait(8, 6, 0, 1)
        wait(7, 5, 0, 1)
        wait(9, 6, 1, 2)
        result(0, 2, [part(0, 0, 0, 2), held(3, 0, 2), held(5, 0, 2), held(6, 0, 2)])
    yield
    wait(18, 4, 3, 4)
    wait(20, 4, 2, 3)
    wait(19, 5, 2, 3)
    wait(21, 5, 3, 4)
    wait(22, 6, 2, 4)
    result(2, 4, [part(0, 0, 2, 4), held(4, 2, 4), held(5, 2, 4), held(6, 2, 4)])
    for copy in started:
        copy().wait_send()


def total_of(refs):
    total = refs[0][...].astype(F32)
    for ref in refs[1:]:
        total = total + ref[...].astype(F32)
    return total


def drain(*programs):
    programs = list(programs)
    while programs:
        programs = [p for p in programs if next(p, "end") != "end"]


def pairs(count):
    return [pltpu.SemaphoreType.DMA((count,)), pltpu.SemaphoreType.DMA((count,))]


def params(collective_id, mib):
    return pltpu.CompilerParams(
        collective_id=collective_id, has_side_effects=True, vmem_limit_bytes=mib * MIB
    )


ROW_CUTS = (0, 96, 192, 288, 400)


def gather_rows_kernel(x_ref, dy_ref, x_out, dy_out, xs, xr, ds, dr, cs, cr, local):
    group = Group("fsdp")
    core = group.core
    width = x_ref.shape[1]
    partner = other_core(group)

    def x_view(member, a, b):
        columns = pl.ds(pl.multiple_of(member * width, width), width)
        return x_out.at[core, pl.ds(ROW_CUTS[a], ROW_CUTS[b] - ROW_CUTS[a]), columns]

    def dy_view(member, a, b):
        columns = pl.ds(pl.multiple_of(member * width, width), width)
        return dy_out.at[core, pl.ds(96 * a, 96 * (b - a)), columns]

    copies = [
        pltpu.make_async_copy(x_ref, x_view(group.me, 0, 4), local.at[0]),
        pltpu.make_async_copy(dy_ref, dy_view(group.me, 0, 4), local.at[1]),
    ]
    for copy in copies:
        copy.start()
    barrier(group.neighbours() + [partner])
    for copy in copies:
        copy.wait()
    drain(gather(group, x_view, (xs, xr)), gather(group, dy_view, (ds, dr)))
    last = [
        remote(x_out.at[core], x_out.at[core], (cs, cr), 0, partner),
        remote(dy_out.at[core], dy_out.at[core], (cs, cr), 1, partner),
    ]
    for copy in last:
        copy.start()
    for copy in last:
        copy.wait()


def gather_rows(x, dy):
    return pl.pallas_call(
        gather_rows_kernel,
        out_shape=[
            jax.ShapeDtypeStruct((2, x.shape[0], 2048), BF16),
            jax.ShapeDtypeStruct((2, dy.shape[0], 2048), BF16),
        ],
        in_specs=[ANY, ANY],
        out_specs=[ANY, ANY],
        scratch_shapes=pairs(GATHER_SLOTS) + pairs(GATHER_SLOTS) + pairs(2) + [pltpu.SemaphoreType.DMA((2,))],
        compiler_params=params(0, 32),
        name="gather_rows",
    )(x, dy)


def gather_keys_kernel(kv_ref, out, send, recv, local):
    group = Group("ctx")
    rows = kv_ref.shape[0]
    step = rows // 4

    def view(member, a, b):
        return out.at[member, pl.ds(step * a, step * (b - a)), :]

    copy = pltpu.make_async_copy(kv_ref, view(group.me, 0, 4), local.at[0])
    copy.start()
    barrier(group.neighbours())
    copy.wait()
    drain(gather(group, view, (send, recv)))


def gather_keys(kv):
    return pl.pallas_call(
        gather_keys_kernel,
        out_shape=jax.ShapeDtypeStruct((8,) + kv.shape, BF16),
        in_specs=[ANY],
        out_specs=ANY,
        scratch_shapes=pairs(GATHER_SLOTS) + [pltpu.SemaphoreType.DMA((1,))],
        compiler_params=params(1, 32),
        name="gather_keys",
    )(kv)


def cut_rows(ref, a, b):
    step = ref.shape[0] // 4
    return ref.at[pl.ds(step * a, step * (b - a)), :]


def rows_scatter(group, part_ref, out, arriving, hold, sems):
    cs, cr, send, recv = sems
    core, partner = group.core, other_core(group)

    def exchange():
        return remote(part_ref.at[1 - core], arriving, (cs, cr), 0, partner)

    exchange().start()
    yield
    exchange().wait()

    def one(i, carry):
        rows = pl.ds(pl.multiple_of(i * 32, 32), 32)
        arriving[rows, :] = (arriving[rows, :].astype(F32) + part_ref[core, rows, :].astype(F32)).astype(BF16)
        return carry

    lax.fori_loop(0, arriving.shape[0] // 32, one, 0)
    width, size = out.shape[1], out.shape[0] // 2

    def cut(ref, a, b):
        return ref.at[pl.ds(size * (a - 2), size * (b - a)), :]

    def part(step, flip, a, b):
        columns = pl.ds(pl.multiple_of(group.member(step, flip) * width, width), width)
        return arriving.at[pl.ds(size * (a - 2), size * (b - a)), columns]

    def result(a, b, refs):
        target = cut(out, a, b)
        target[...] = total_of(refs)

    yield from scatter(group, part, cut, hold, result, (send, recv), pair_first=False)


def peers(axis):
    ctx, fsdp = lax.axis_index("ctx"), lax.axis_index("fsdp")
    count = lax.axis_size(axis)
    if axis == "ctx":
        return [(lax.rem(ctx + offset, count), fsdp) for offset in range(1, count)]
    return [(ctx, lax.rem(fsdp + offset, count)) for offset in range(1, count)]


def sum_small(x_ref, out, hold, sems, devices):
    def copy(i):
        return remote(x_ref, hold.at[i], sems, i, devices[i])

    for i in range(len(devices)):
        copy(i).start()
    yield
    total = x_ref[...]
    for i in range(len(devices)):
        copy(i).wait_recv()
        total = total + hold[i]
    out[...] = total
    for i in range(len(devices)):
        copy(i).wait_send()


def reduce_one(group, source, target, hold, sems):
    rs, rr, gs, gr, cs, cr = sems
    core, partner = group.core, other_core(group)
    rows, width = source.shape[0] // 8, source.shape[1]
    by_rows = rows % 64 == 0

    def quarters(ref, a, b):
        if by_rows:
            return ref.at[pl.ds(rows // 4 * a, rows // 4 * (b - a)), :]
        return ref.at[:, pl.ds(width // 4 * a, width // 4 * (b - a))]

    def part(step, flip, a, b):
        start = pl.multiple_of(group.member(step, flip) * rows, rows)
        return quarters(source.at[pl.ds(start, rows), :], a, b)

    def view(member, a, b):
        start = pl.multiple_of(member * rows, rows)
        return quarters(target.at[core, pl.ds(start, rows), :], a, b)

    def result(a, b, terms):
        place = view(group.me, a, b)
        place[...] = total_of(terms).astype(BF16)

    copies = []

    def arrived(block, a, b):
        slot = len(copies)

        def copy():
            ref = view(group.member(*block), a, b)
            return remote(ref, ref, (cs, cr), slot, partner)

        copy().start()
        copies.append(copy)

    yield from scatter(group, part, quarters, hold, result, (rs, rr))
    yield from gather(group, view, (gs, gr), arrived)
    yield
    for copy in copies:
        copy().wait()


def reduce_scratch(shape):
    return pltpu.VMEM((HOLD, shape[0] // 8, shape[1]), BF16)


def reduce_sems():
    return pairs(SCATTER_SLOTS) + pairs(GATHER_SLOTS) + pairs(GATHER_SLOTS + 1)


TILE = 2 * GROUP
TILES = SEQ_LEN // TILE
ITEMS = TILES + 1
NT = (((1,), (1,)), ((), ()))
TN = (((0,), (0,)), ((), ()))


def dot(a, b, dims=(((1,), (0,)), ((), ()))):
    return lax.dot_general(a, b, dims, preferred_element_type=F32)


STATES = 11


def state_of(j):
    late = lax.div(j + 7, 16)
    return j * (1 - late) + (9 + lax.rem(j, 2)) * late


class Steps:
    def __init__(self, *programs):
        self.programs = list(programs)

    def take(self, count=1):
        for _ in range(count):
            self.programs = [p for p in self.programs if next(p, "end") != "end"]

    def at(self, j, plan):
        for iteration, count in plan:
            pl.when(j == iteration)(partial(self.take, count))

    def finish(self):
        drain(*self.programs)


FORWARD_PLAN = ((2, 1), (5, 1), (6, 1), (10, 1), (13, 1), (15, 1), (16, 1))
BACKWARD_PLAN = ((1, 1), (3, 1), (8, 3), (13, 2), (15, 2))
BRANCH_PLAN = ((2, 1), (5, 1), (8, 1), (12, 1))


def attention_kernel(
    table, q_ref, cotangent_ref, kv_ref, begin_ref, ff_ref, wo_ref, inner_part, outer_part,
    att_ref, dq_ref, dkv_ref, sum_ref, inner_out, outer_out,
    kvp, state_max, state_sum, state_acc, dq_items, dkv_items, lse_ref, delta_ref, branch, arriving, branch_hold, inner_hold, outer_hold, *sems
):
    left = lax.broadcasted_iota(jnp.int32, (1, 128), 1) < HEAD_DIM
    across, along = Group("ctx"), Group("fsdp")
    barrier(across.neighbours() + along.neighbours() + [other_core(across)])
    weights_steps = Steps(
        reduce_one(across, inner_part, inner_out, inner_hold, sems[:6]),
        reduce_one(across, outer_part, outer_out, outer_hold, sems[6:12]),
    )
    branch_steps = Steps(rows_scatter(along, branch, sum_ref, arriving, branch_hold, sems[12:]))
    weights_steps.take()

    def place(g, carry):
        tile, half = lax.div(g, 2), lax.rem(g, 2)
        kvp[tile, pl.ds(pl.multiple_of(half * GROUP, GROUP), GROUP), :] = kv_ref[table[g]]
        return carry

    lax.fori_loop(0, GROUPS, place, 0)

    def bit(number):
        return jnp.minimum(jnp.maximum(number, 0), 1)

    def pair_facts(p):
        g0, g1 = table[32 + 2 * p], table[33 + 2 * p]
        low, high = jnp.minimum(g0, g1), jnp.maximum(g0, g1)
        return low, high, bit(g0 - g1), lax.div(low, 2) + 1

    key_row = lax.broadcasted_iota(jnp.int32, (TILE, TILE), 0)
    column = lax.broadcasted_iota(jnp.int32, (1, TILE), 1)
    query_row = jnp.where(column < GROUP, column, column - GROUP)

    def item_facts(p, j):
        low, high, low_slot, count = pair_facts(p)
        second = bit(j - count + 1)
        tile = second * TILES + (1 - second) * (count - 1) - j
        slot = 2 * p + second * (1 - low_slot) + (1 - second) * low_slot
        position = (second * high + (1 - second) * low) * GROUP
        last = query_row + (position - tile * TILE)
        begin = begin_ref[slot] - tile * TILE
        allowed = (key_row <= last) & (key_row >= begin)
        keep = bit(j * (j - count) * (j - count)).astype(F32)
        return tile, slot, allowed, keep

    def stacked(rows):
        zero = jnp.zeros_like(rows)
        return jnp.concatenate([jnp.where(left, rows, zero), jnp.where(left, zero, rows)], axis=0)

    def unstacked(columns):
        rows = columns.T
        return jnp.where(left, rows[:GROUP], rows[GROUP:])

    def final_item(p, i):
        low, high, low_slot, count = pair_facts(p)
        is_low = low_slot if i else 1 - low_slot
        return count * is_low + 10 * (1 - is_low)

    for p in range(2):
        state_max[p, 0] = jnp.full((1, TILE), FLOOR, F32)
        state_sum[p, 0] = jnp.zeros((1, TILE), F32)
        state_acc[p, 0] = jnp.zeros((128, TILE), F32)

    def forward(j, carry):
        weights_steps.at(j, FORWARD_PLAN)
        now, after = state_of(j), state_of(j + 1)
        for p in range(2):
            tile, slot, allowed, keep = item_facts(p, j)
            scores = jnp.where(allowed, dot(kvp[tile, :, :128], stacked(q_ref[slot]), NT), MASKED)
            old_max = state_max[p, now] * keep + FLOOR * (1.0 - keep)
            new_max = jnp.maximum(old_max, jnp.max(scores, axis=0, keepdims=True))
            weights = jnp.exp(scores - new_max)
            factor = jnp.exp(old_max - new_max)
            state_max[p, after] = new_max
            state_sum[p, after] = state_sum[p, now] * factor + jnp.sum(weights, axis=0, keepdims=True)
            state_acc[p, after] = state_acc[p, now] * factor + dot(kvp[tile, :, 128:], weights.astype(BF16), TN)
        return carry

    lax.fori_loop(0, ITEMS, forward, 0)

    for p in range(2):
        for i in range(2):
            item = final_item(p, i)
            slot = 2 * p + i
            total = state_sum[p, item]
            out = state_acc[p, item] / total
            lse_ref[slot] = state_max[p, item] + jnp.log(total)
            cotangent = stacked(cotangent_ref[slot].astype(F32)).T
            delta_ref[slot] = jnp.sum(cotangent * out, axis=0, keepdims=True)
            att_ref[slot] = unstacked(out).astype(BF16)

    def branches(i, carry):
        slot, columns = lax.div(i, 4), pl.ds(pl.multiple_of(lax.rem(i, 4) * 512, 512), 512)
        core, rows = lax.div(slot, 2), pl.ds(pl.multiple_of(lax.rem(slot, 2) * GROUP, GROUP), GROUP)
        branch[core, rows, columns] = (ff_ref[core, rows, columns].astype(F32) + dot(att_ref[slot], wo_ref[:, columns])).astype(BF16)
        return carry

    lax.fori_loop(0, 16, branches, 0)
    branch_steps.take()

    for p in range(2):
        dq_items[p, 0] = jnp.zeros((128, TILE), F32)

    def backward(j, carry):
        weights_steps.at(j, BACKWARD_PLAN)
        branch_steps.at(j, BRANCH_PLAN)
        now, after = state_of(j), state_of(j + 1)
        for p in range(2):
            tile, slot, allowed, keep = item_facts(p, j)
            queries, cotangent = stacked(q_ref[slot]), stacked(cotangent_ref[slot])
            scores = dot(kvp[tile, :, :128], queries, NT)
            probs = jnp.where(allowed, jnp.exp(scores - lse_ref[slot]), 0.0)
            prob_grad = dot(kvp[tile, :, 128:], cotangent, NT)
            score_grad = (probs * (prob_grad - delta_ref[slot])).astype(BF16)
            dq_items[p, after] = dq_items[p, now] * keep + dot(kvp[tile, :, :128], score_grad, TN)
            key_grad = dot(score_grad, queries).astype(BF16)
            value_grad = dot(probs.astype(BF16), cotangent).astype(BF16)
            for half in range(2):
                rows = slice(GROUP * half, GROUP * half + GROUP)
                dkv_items[p, j, half, :, :128] = key_grad[rows]
                dkv_items[p, j, half, :, 128:] = value_grad[rows]
        return carry

    lax.fori_loop(0, ITEMS, backward, 0)

    for p in range(2):
        for i in range(2):
            dq_ref[2 * p + i] = unstacked(dq_items[p, final_item(p, i)])

    counts = [pair_facts(p)[3] for p in range(2)]

    def collect(s, carry):
        group = table[36 + s]
        tile, half = lax.div(group, 2), lax.rem(group, 2)
        total = jnp.zeros((GROUP, 256), F32)
        for p in range(2):
            low_item = dkv_items[p, jnp.maximum(counts[p] - 1 - tile, 0), half].astype(F32)
            high_item = dkv_items[p, jnp.maximum(TILES - tile, counts[p]), half].astype(F32)
            total = total + low_item * bit(counts[p] - tile).astype(F32)
            total = total + high_item * bit(TILES - tile - counts[p] + 1).astype(F32)
        dkv_ref[s] = total.astype(BF16)
        return carry

    lax.fori_loop(0, GROUPS, collect, 0)
    branch_steps.finish()
    weights_steps.finish()


def attention(table, queries, cotangent, kv, begin, ff, wo, inner_part, outer_part):
    rows, width = ff.shape[1], ff.shape[2]
    return pl.pallas_call(
        attention_kernel,
        out_shape=[
            jax.ShapeDtypeStruct((4, GROUP, 128), BF16),
            jax.ShapeDtypeStruct((4, GROUP, 128), F32),
            jax.ShapeDtypeStruct((GROUPS, GROUP, 256), BF16),
            jax.ShapeDtypeStruct((rows, width // 8), F32),
            jax.ShapeDtypeStruct((2,) + inner_part.shape, BF16),
            jax.ShapeDtypeStruct((2,) + outer_part.shape, BF16),
        ],
        in_specs=[SMEM] + [VMEM] * 8,
        out_specs=[VMEM] * 6,
        scratch_shapes=[
            pltpu.VMEM((TILES, TILE, 256), BF16),
            pltpu.VMEM((2, STATES, 1, TILE), F32),
            pltpu.VMEM((2, STATES, 1, TILE), F32),
            pltpu.VMEM((2, STATES, 128, TILE), F32),
            pltpu.VMEM((2, STATES, 128, TILE), F32),
            pltpu.VMEM((2, ITEMS, 2, GROUP, 256), BF16),
            pltpu.VMEM((4, 1, TILE), F32),
            pltpu.VMEM((4, 1, TILE), F32),
            pltpu.VMEM(ff.shape, BF16),
            pltpu.VMEM((rows, width), BF16),
            pltpu.VMEM((HOLD, rows, width // 8), BF16),
            reduce_scratch(inner_part.shape),
            reduce_scratch(outer_part.shape),
        ]
        + reduce_sems() * 2
        + pairs(1)
        + pairs(SCATTER_SLOTS),
        compiler_params=params(8, 62),
        name="attention",
    )(table, queries, cotangent, kv, begin, ff, wo, inner_part, outer_part)


def turned(values, cosine, sine):
    lane = lax.rem(lax.broadcasted_iota(jnp.int32, (1, 128), 1), HEAD_DIM)
    swapped = jnp.where(lane < ROT // 2, -pltpu.roll(values, 128 - ROT // 2, 1), pltpu.roll(values, ROT // 2, 1))
    return values * cosine + swapped * sine


def backward_kernel(
    dkv_ref, dq_ref, cos_ref, sin_ref, normed_ref, w_ref, ff_ref, out_part, unit_ref, inv_ref, gain_ref, dy_ref, vec_ref,
    q_out, kv_out, out_out, input_out, vec_out,
    keys_hold, own, pre, q_part, kv_part, branch, arriving, rows_hold, local, q_hold, kv_hold, out_hold,
    stats, stats_hold, stats_sum, vec, vec_hold, *sems
):
    across, along = Group("ctx"), Group("fsdp")
    core = across.core
    barrier(peers("ctx") + peers("fsdp"))

    def part(step, flip, a, b):
        return cut_rows(dkv_ref.at[across.member(step, flip)], a, b)

    def result(a, b, refs):
        target = cut_rows(own, a, b)
        target[...] = total_of(refs)

    keys = Steps(scatter(across, part, cut_rows, keys_hold, result, sems[:2]))
    keys.take()
    chunk = pre.shape[0] // 4
    for i in range(4):
        rows = slice(chunk * i, chunk * (i + 1))
        grad = turned(dq_ref[rows, :] * HEAD_DIM ** (-0.5), cos_ref[rows, :], -sin_ref[rows, :])
        pre[rows, :128] = grad.astype(BF16)

    def query_weights(i, carry):
        block = pl.ds(pl.multiple_of(i * 256, 256), 256)
        q_part[block, :] = dot(normed_ref[:, block], pre[:, :128], TN).astype(BF16)
        return carry

    lax.fori_loop(0, 8, query_weights, 0)
    keys.finish()
    for i in range(4):
        rows = slice(chunk * i, chunk * (i + 1))
        grad = turned(own[rows, :128], cos_ref[rows, :], -sin_ref[rows, :])
        pre[rows, 128:256] = grad.astype(BF16)
        pre[rows, 256:] = own[rows, 128:].astype(BF16)

    def key_weights(i, carry):
        block = pl.ds(pl.multiple_of(i * 256, 256), 256)
        kv_part[block, :] = dot(normed_ref[:, block], pre[:, 128:], TN).astype(BF16)
        return carry

    lax.fori_loop(0, 8, key_weights, 0)
    weights = Steps(
        reduce_one(across, kv_part, kv_out, kv_hold, sems[2:8]),
        reduce_one(across, q_part, q_out, q_hold, sems[8:14]),
        reduce_one(across, out_part, out_out, out_hold, sems[14:20]),
    )
    weights.take()

    def normed_grad(of):
        def one(i, carry):
            rows = pl.ds(pl.multiple_of(lax.div(i, 4) * GROUP, GROUP), GROUP)
            columns = pl.ds(pl.multiple_of(lax.rem(i, 4) * 512, 512), 512)
            from_rows = pl.ds(pl.multiple_of(of * 2 * GROUP + lax.div(i, 4) * GROUP, GROUP), GROUP)
            grad = ff_ref[of, rows, columns].astype(F32) + dot(pre[from_rows, :], w_ref[columns, :], NT)
            branch[of, rows, columns] = grad.astype(BF16)
            return carry

        lax.fori_loop(0, 8, one, 0)

    normed_grad(1 - core)
    rows_steps = Steps(rows_scatter(along, branch, local, arriving, rows_hold, sems[20:24]))
    rows_steps.take()
    normed_grad(core)
    for count in (1, 2, 1, 2, 2):
        rows_steps.take()
        weights.take(count)
    rows_steps.finish()

    whole = local[...]
    unit = unit_ref[...]
    scaled = whole * gain_ref[...]
    lane = lax.broadcasted_iota(jnp.int32, (1, 128), 1)
    first = jnp.sum(scaled, axis=1, keepdims=True)
    second = jnp.sum(scaled * unit, axis=1, keepdims=True)
    stats[...] = jnp.where(lane == 0, first, jnp.where(lane == 1, second, 0.0)).T[:8]
    stats_steps = Steps(sum_small(stats, stats_sum, stats_hold, sems[24:26], peers("fsdp")))
    stats_steps.take()
    vec[...] = vec_ref[...]
    vec[0:1, :] = jnp.sum(whole * unit, axis=0, keepdims=True)
    vec[1:2, :] = jnp.sum(whole, axis=0, keepdims=True)
    half = pl.ds(pl.multiple_of(core * 128, 128), 128)
    for i in range(3):
        vec[3 + i : 4 + i, half] = jnp.sum(pre[:, 128 * i : 128 * i + 128].astype(F32), axis=0, keepdims=True)
    vec_steps = Steps(sum_small(vec, vec_out, vec_hold, sems[26:28], peers("ctx")))
    vec_steps.take()
    weights.take(2)
    stats_steps.finish()
    back = jnp.concatenate([stats_sum[...], jnp.zeros((120, stats_sum.shape[1]), F32)], axis=0).T * (1.0 / 2048)
    input_out[...] = dy_ref[...].astype(F32) + inv_ref[...] * (scaled - back[:, 0:1] - unit * back[:, 1:2])
    vec_steps.finish()
    weights.finish()


def backward(dkv, dq, cosine, sine, normed, w, ff, out_part, unit, inv, gain, dy, vec):
    both, rows, width, wide = normed.shape[0], unit.shape[0], unit.shape[1], normed.shape[1]

    def bf(*shape):
        return pltpu.VMEM(shape, BF16)

    def f32(*shape):
        return pltpu.VMEM(shape, F32)

    return pl.pallas_call(
        backward_kernel,
        out_shape=[
            jax.ShapeDtypeStruct((2, wide, 128), BF16),
            jax.ShapeDtypeStruct((2, wide, 256), BF16),
            jax.ShapeDtypeStruct((2,) + out_part.shape, BF16),
            jax.ShapeDtypeStruct(unit.shape, F32),
            jax.ShapeDtypeStruct(vec.shape, F32),
        ],
        in_specs=[VMEM] * 13,
        out_specs=[VMEM] * 5,
        scratch_shapes=[
            bf(HOLD, both, 256),
            f32(both, 256),
            bf(both, 384),
            bf(wide, 128),
            bf(wide, 256),
            bf(2, rows, wide),
            bf(rows, wide),
            bf(HOLD, rows, width),
            f32(rows, width),
            reduce_scratch((wide, 128)),
            reduce_scratch((wide, 256)),
            reduce_scratch(out_part.shape),
            f32(8, rows),
            f32(7, 8, rows),
            f32(8, rows),
            f32(*vec.shape),
            f32(15, *vec.shape),
        ]
        + pairs(SCATTER_SLOTS)
        + reduce_sems() * 3
        + pairs(1)
        + pairs(SCATTER_SLOTS)
        + pairs(7)
        + pairs(15),
        compiler_params=params(9, 56),
        name="backward",
    )(dkv, dq, cosine, sine, normed, w, ff, out_part, unit, inv, gain, dy, vec)


def body(
    layer_input,
    norm_gain,
    norm_bias,
    query_weight,
    query_bias,
    key_weight,
    key_bias,
    value_weight,
    value_bias,
    out_weight,
    out_bias,
    inner_weight,
    inner_bias,
    outer_weight,
    outer_bias,
    output_grad,
    group_order,
    sequence_ids,
):
    ctx = lax.axis_index("ctx")
    fsdp = lax.axis_index("fsdp")
    core = lax.rem(ctx, 2)
    rows = layer_input.shape[0]
    both = 2 * rows

    def half(array, axis):
        size = array.shape[axis] // 2
        return lax.dynamic_slice_in_dim(array, core * size, size, axis)

    wq, wk, wv = half(query_weight, 1), half(key_weight, 1), half(value_weight, 1)
    wo, wi, wu = half(out_weight, 0), half(inner_weight, 1), half(outer_weight, 0)
    bq, bk, bv, bi = half(query_bias, 0), half(key_bias, 0), half(value_bias, 0), half(inner_bias, 0)

    slots = lax.div(ctx, 2) * 4 + jnp.arange(4, dtype=jnp.int32)
    my_groups = group_order[slots]
    position = (my_groups[:, None] * GROUP + jnp.arange(GROUP, dtype=jnp.int32)[None, :]).reshape(both)
    begins = jnp.sum(
        (sequence_ids[None, :] < jnp.arange(DOCS, dtype=jnp.int32)[:, None]).astype(jnp.int32), axis=1
    )
    my_docs = sequence_ids.reshape(GROUPS, GROUP)[my_groups]
    begin = jnp.zeros((4, GROUP), jnp.int32)
    for doc in range(1, DOCS):
        begin = jnp.where(my_docs == doc, begins[doc], begin)
    slot_of = jnp.sum(
        jnp.where(group_order[None, :] == jnp.arange(GROUPS)[:, None], jnp.arange(GROUPS)[None, :], 0), axis=1
    ).astype(jnp.int32)
    table = jnp.concatenate([slot_of, my_groups, group_order]).astype(jnp.int32)
    lane = jnp.arange(128, dtype=jnp.int32) % HEAD_DIM
    freqs = jnp.where(lane < ROT, 10000.0 ** (-((lane % (ROT // 2)).astype(F32) * 2.0 / ROT)), 0.0)
    angles = position.astype(F32)[:, None] * freqs[None, :]
    cosine, sine = jnp.cos(angles), jnp.sin(angles)

    def turn(values):
        second = (lane // (ROT // 2)) == 1
        swapped = jnp.where(second, jnp.roll(values, ROT // 2, 1), -jnp.roll(values, -(ROT // 2), 1))
        return values * cosine + swapped * sine

    extra = jnp.concatenate([norm_gain[None], norm_bias[None], jnp.zeros((14, norm_gain.shape[0]), BF16)])
    x_all, dy_all = gather_rows(jnp.concatenate([layer_input, extra]), output_grad)
    gain = x_all[0, rows].astype(F32)
    shift = x_all[0, rows + 1].astype(F32)
    dy = dy_all.reshape(both, -1)
    inputs = x_all[:, :rows].reshape(both, -1).astype(F32)
    row_mean = jnp.mean(inputs, axis=-1, keepdims=True)
    centered = inputs - row_mean
    inv_std = lax.rsqrt(jnp.mean(centered * centered, axis=-1, keepdims=True) + EPS)
    normed = (centered * inv_std * gain + shift).astype(BF16)

    def project(matrix, vector):
        return jnp.dot(normed, matrix, preferred_element_type=F32) + vector.astype(F32)

    queries = turn(project(wq, bq)).astype(BF16)
    keys = turn(project(wk, bk)).astype(BF16)
    values = project(wv, bv).astype(BF16)
    kv = jnp.concatenate([keys, values], axis=1)
    kv_all = gather_keys(kv).reshape(GROUPS, GROUP, 256)
    attended_grad = jnp.einsum("rd,cd->rc", dy, wo, preferred_element_type=F32).astype(BF16)
    scaled = (queries.astype(F32) * HEAD_DIM ** (-0.5)).astype(BF16).reshape(4, GROUP, 128)
    begin = jnp.concatenate([begin, begin], axis=1)[:, None, :]
    inner = project(wi, bi)
    activated = jax.nn.gelu(inner, approximate=True).astype(BF16)
    act_grad = jnp.einsum("rd,fd->rf", dy, wu, preferred_element_type=F32)
    _, gelu_pull = jax.vjp(partial(jax.nn.gelu, approximate=True), inner)
    inner_grad = gelu_pull(act_grad)[0].astype(BF16)
    ff = jnp.dot(activated, wu, preferred_element_type=F32).astype(BF16).reshape(2, rows, -1)

    def weight_grad(left, right):
        return jnp.einsum("rc,rd->cd", left, right, preferred_element_type=F32).astype(BF16)

    attended, dq, dkv, summed, inner_w_grad, outer_w_grad = attention(
        table, scaled, attended_grad.reshape(4, GROUP, 128), kv_all, begin, ff, wo, weight_grad(normed, inner_grad), weight_grad(activated, dy)
    )
    attended = attended.reshape(both, 128)
    layer_output = (
        layer_input.astype(F32) + summed + out_bias.astype(F32) + outer_bias.astype(F32)
    ).astype(BF16)

    my_mean = lax.dynamic_slice_in_dim(row_mean, core * rows, rows, 0)
    my_inv = lax.dynamic_slice_in_dim(inv_std, core * rows, rows, 0)
    unit = (layer_input.astype(F32) - my_mean) * my_inv
    ff_normed_grad = jnp.einsum("rf,df->rd", inner_grad, wi, preferred_element_type=F32).astype(BF16)
    vec = jnp.zeros((16, 256), F32)
    vec = vec.at[2].set(jnp.sum(output_grad.astype(F32), axis=0))
    inner_bias_sum = jnp.sum(inner_grad.astype(F32), axis=0).reshape(2, 256)
    vec = lax.dynamic_update_slice(vec, inner_bias_sum, (6 + 2 * core, 0))
    query_grad, kv_grad, out_grad, input_grad, vectors = backward(
        dkv.reshape(8, both, 256), dq.reshape(both, 128), cosine, sine, normed, jnp.concatenate([wq, wk, wv], axis=1),
        ff_normed_grad.reshape(2, rows, -1), weight_grad(attended, dy), unit, my_inv, norm_gain.astype(F32)[None], output_grad, vec,
    )

    def side_by_side(array):
        return jnp.concatenate([array[0], array[1]], axis=1).astype(F32)

    return (
        layer_output,
        input_grad,
        vectors[0],
        vectors[1],
        side_by_side(query_grad),
        vectors[3],
        side_by_side(kv_grad[:, :, :128]),
        vectors[4],
        side_by_side(kv_grad[:, :, 128:]),
        vectors[5],
        out_grad.reshape(256, 2048).astype(F32),
        vectors[2],
        side_by_side(inner_w_grad),
        vectors[6:10].reshape(1024),
        outer_w_grad.reshape(1024, 2048).astype(F32),
        vectors[2],
    )


def solution(mesh):
    in_specs = (
        P("ctx", "fsdp"),
        P("fsdp"),
        P("fsdp"),
        P(None, "fsdp"),
        P("fsdp"),
        P(None, "fsdp"),
        P("fsdp"),
        P(None, "fsdp"),
        P("fsdp"),
        P("fsdp", None),
        P("fsdp"),
        P(None, "fsdp"),
        P("fsdp"),
        P("fsdp", None),
        P("fsdp"),
        P("ctx", "fsdp"),
        P(),
        P(),
    )
    out_specs = (
        P("ctx", "fsdp"),
        P("ctx", "fsdp"),
        P("fsdp"),
        P("fsdp"),
        P(None, "fsdp"),
        P("fsdp"),
        P(None, "fsdp"),
        P("fsdp"),
        P(None, "fsdp"),
        P("fsdp"),
        P("fsdp", None),
        P("fsdp"),
        P(None, "fsdp"),
        P("fsdp"),
        P("fsdp", None),
        P("fsdp"),
    )
    return jax.shard_map(body, mesh=mesh, in_specs=in_specs, out_specs=out_specs, check_vma=False)
```

```python
from functools import partial

import jax
import jax.numpy as jnp
from jax import lax
from jax.experimental import pallas as pl
from jax.experimental.pallas import tpu as pltpu
from jax.sharding import PartitionSpec as P

HEAD_DIM = 64
ROT = 32
GROUP = 192
GROUPS = 32
SEQ_LEN = 6144
DOCS = 5
EPS = 1e-05
MASKED = -1e30
FLOOR = -1e29
GELU_A = 0.7978845608028654
GELU_B = 0.044715
MESH = pl.DeviceIdType.MESH
BF16 = jnp.bfloat16
F32 = jnp.float32
ANY = pl.BlockSpec(memory_space=pl.ANY)
VMEM = pl.BlockSpec(memory_space=pltpu.VMEM)
SMEM = pl.BlockSpec(memory_space=pltpu.SMEM)
MIB = 2**20


class Group:
    def __init__(self, axis):
        ctx, fsdp = lax.axis_index("ctx"), lax.axis_index("fsdp")
        self.axis, self.ctx, self.fsdp = axis, ctx, fsdp
        self.core = lax.rem(ctx, 2)
        self.me = lax.div(ctx, 2) if axis == "ctx" else fsdp
        self.ring, self.pair = lax.rem(self.me, 4), lax.div(self.me, 4)

    def member(self, step, flip):
        pair = 1 - self.pair if flip else self.pair
        return pair * 4 + lax.rem(self.ring + (step + 4), 4)

    def device(self, step, flip):
        member = self.member(step, flip)
        if self.axis == "ctx":
            return (member * 2 + self.core, self.fsdp)
        return (self.ctx, member)

    def neighbours(self):
        return [self.device(1, 0), self.device(-1, 0), self.device(0, 1)]


def other_core(group):
    return (group.ctx + 1 - 2 * group.core, group.fsdp)


def barrier(devices):
    semaphore = pltpu.get_barrier_semaphore()
    for device in devices:
        pl.semaphore_signal(semaphore, inc=1, device_id=device, device_id_type=MESH)
    pl.semaphore_wait(semaphore, len(devices))


def remote(source, target, sems, slot, device):
    return pltpu.make_async_remote_copy(
        src_ref=source,
        dst_ref=target,
        send_sem=sems[0].at[slot],
        recv_sem=sems[1].at[slot],
        device_id=device,
        device_id_type=MESH,
    )


GATHER = (
    (1, 0, (0, 0), 0, 2, None),
    (-1, 0, (0, 0), 0, 2, None),
    (0, 1, (0, 0), 2, 4, None),
    (1, 0, (0, 0), 2, 4, None),
    (-1, 0, (0, 0), 2, 4, None),
    (0, 1, (0, 0), 0, 2, None),
    (1, 0, (-1, 0), 0, 1, 0),
    (-1, 0, (1, 0), 1, 2, 1),
    (0, 1, (-1, 0), 0, 2, 0),
    (0, 1, (1, 0), 0, 2, 1),
    (0, 1, (2, 0), 0, 1, 6),
    (0, 1, (2, 0), 1, 2, 7),
    (1, 0, (0, 1), 2, 4, 2),
    (-1, 0, (0, 1), 2, 4, 2),
    (1, 0, (-1, 0), 2, 3, 3),
    (-1, 0, (1, 0), 3, 4, 4),
    (1, 0, (-1, 1), 2, 3, 12),
    (-1, 0, (1, 1), 3, 4, 13),
)
GATHER_ORDER = (0, 1, 2, 3, 4, 6, 7, 12, 13, 5, 8, 14, 15, 9, 10, 16, 17, 11)
GATHER_SLOTS = len(GATHER)
PAIR_ONLY = (2, 3, 4, 12, 13, 14, 15, 16, 17)


def gather(group, view, sems, arrived=None, slots=tuple(range(GATHER_SLOTS))):
    started = []

    def start(slot):
        step, flip, block, a, b, _ = GATHER[slot]

        def copy():
            ref = view(group.member(*block), a, b)
            return remote(ref, ref, sems, slot, group.device(step, flip))

        copy().start()
        started.append(copy)

    for slot in slots:
        if GATHER[slot][5] is None:
            start(slot)
    if arrived:
        arrived((0, 0), 0, 4)
    for slot in [i for i in GATHER_ORDER if i in slots]:
        step, flip, block, a, b, _ = GATHER[slot]
        yield
        source = (block[0] - step, block[1] ^ flip)
        ref = view(group.member(*source), a, b)
        remote(ref, ref, sems, slot, group.device(step, flip)).wait_recv()
        for later in slots:
            if GATHER[later][5] == slot:
                start(later)
        if arrived:
            arrived(source, a, b)
    for copy in started:
        copy().wait_send()


SCATTER_SLOTS = 23
HOLD = 7


def add_into(target, *sources):
    total = target[...].astype(F32)
    for source in sources:
        total = total + source[...].astype(F32)
    target[...] = total.astype(target.dtype)


def scatter(group, part, quarters, hold, result, sems, pair_first=True):
    started = []

    def held(k, a, b):
        return quarters(hold.at[k], a, b)

    def start(slot, source, step, flip, k, a, b):
        def copy():
            return remote(source(), held(k, a, b), sems, slot, group.device(step, flip))

        copy().start()
        started.append(copy)

    def send_part(slot, block, step, flip, k, a, b):
        start(slot, lambda: part(*block, a, b), step, flip, k, a, b)

    def send_held(slot, source, step, flip, k, a, b):
        start(slot, lambda: held(source, a, b), step, flip, k, a, b)

    def wait(slot, k, a, b):
        ref = held(k, a, b)
        remote(ref, ref, sems, slot, group.device(0, 1)).wait_recv()

    if pair_first:
        send_part(0, (2, 1), 0, 1, 0, 0, 2)
    send_part(10, (2, 1), 1, 0, 0, 2, 3)
    send_part(11, (2, 1), -1, 0, 0, 3, 4)
    if pair_first:
        send_part(1, (1, 1), 0, 1, 1, 0, 2)
        send_part(2, (-1, 1), 0, 1, 2, 0, 2)
    send_part(16, (2, 0), 1, 0, 3, 2, 3)
    send_part(17, (2, 0), -1, 0, 3, 3, 4)
    send_part(12, (1, 1), 1, 0, 1, 3, 4)
    send_part(13, (-1, 1), -1, 0, 2, 2, 3)
    send_part(18, (1, 0), 1, 0, 4, 3, 4)
    send_part(19, (-1, 0), -1, 0, 5, 2, 3)
    if pair_first:
        send_part(3, (0, 1), 0, 1, 3, 0, 2)
    yield
    wait(10, 0, 2, 3)
    add_into(held(0, 2, 3), part(1, 1, 2, 3))
    send_held(14, 0, 1, 0, 1, 2, 3)
    wait(11, 0, 3, 4)
    add_into(held(0, 3, 4), part(-1, 1, 3, 4))
    send_held(15, 0, -1, 0, 2, 3, 4)
    if pair_first:
        yield
        wait(0, 0, 0, 2)
        add_into(held(0, 0, 2), part(2, 0, 0, 2))
        send_held(4, 0, 1, 0, 4, 0, 1)
        send_held(5, 0, -1, 0, 4, 1, 2)
    yield
    wait(16, 3, 2, 3)
    add_into(held(3, 2, 3), part(1, 0, 2, 3))
    send_held(20, 3, 1, 0, 4, 2, 3)
    wait(17, 3, 3, 4)
    add_into(held(3, 3, 4), part(-1, 0, 3, 4))
    send_held(21, 3, -1, 0, 5, 3, 4)
    if pair_first:
        yield
        wait(1, 1, 0, 2)
        add_into(held(1, 0, 2), part(1, 0, 0, 2))
        send_held(6, 1, 1, 0, 5, 1, 2)
    yield
    wait(12, 1, 3, 4)
    wait(14, 1, 2, 3)
    wait(13, 2, 2, 3)
    wait(15, 2, 3, 4)
    add_into(held(1, 2, 4), held(2, 2, 4), part(0, 1, 2, 4))
    send_held(22, 1, 0, 1, 6, 2, 4)
    if pair_first:
        yield
        wait(2, 2, 0, 2)
        add_into(held(2, 0, 2), part(-1, 0, 0, 2))
        send_held(8, 2, -1, 0, 6, 0, 1)
        yield
        wait(4, 4, 0, 1)
        add_into(held(1, 0, 1), held(4, 0, 1))
        send_held(7, 1, 1, 0, 5, 0, 1)
        wait(5, 4, 1, 2)
        add_into(held(2, 1, 2), held(4, 1, 2))
        send_held(9, 2, -1, 0, 6, 1, 2)
        yield
        wait(3, 3, 0, 2)
        wait(6, 5, 1, 2)
        wait(8, 6, 0, 1)
        wait(7, 5, 0, 1)
        wait(9, 6, 1, 2)
        result(0, 2, [part(0, 0, 0, 2), held(3, 0, 2), held(5, 0, 2), held(6, 0, 2)])
    yield
    wait(18, 4, 3, 4)
    wait(20, 4, 2, 3)
    wait(19, 5, 2, 3)
    wait(21, 5, 3, 4)
    wait(22, 6, 2, 4)
    result(2, 4, [part(0, 0, 2, 4), held(4, 2, 4), held(5, 2, 4), held(6, 2, 4)])
    for copy in started:
        copy().wait_send()


def total_of(refs):
    total = refs[0][...].astype(F32)
    for ref in refs[1:]:
        total = total + ref[...].astype(F32)
    return total


def drain(*programs):
    programs = list(programs)
    while programs:
        programs = [p for p in programs if next(p, "end") != "end"]


def pairs(count):
    return [pltpu.SemaphoreType.DMA((count,)), pltpu.SemaphoreType.DMA((count,))]


def params(collective_id, mib):
    return pltpu.CompilerParams(
        collective_id=collective_id, has_side_effects=True, vmem_limit_bytes=mib * MIB
    )


ROW_CUTS = (0, 96, 192, 288, 400)


TILE = 2 * GROUP
TILES = SEQ_LEN // TILE
ITEMS = TILES + 1
NT = (((1,), (1,)), ((), ()))
TN = (((0,), (0,)), ((), ()))


def dot(a, b, dims=(((1,), (0,)), ((), ()))):
    return lax.dot_general(a, b, dims, preferred_element_type=F32)


class Steps:
    def __init__(self, *programs):
        self.programs = list(programs)

    def take(self, count=1):
        for _ in range(count):
            self.programs = [p for p in self.programs if next(p, "end") != "end"]

    def at(self, j, plan):
        for iteration, count in plan:
            pl.when(j == iteration)(partial(self.take, count))

    def finish(self):
        drain(*self.programs)


def turned(values, cosine, sine):
    lane = lax.rem(lax.broadcasted_iota(jnp.int32, (1, 128), 1), HEAD_DIM)
    swapped = jnp.where(lane < ROT // 2, -pltpu.roll(values, 128 - ROT // 2, 1), pltpu.roll(values, ROT // 2, 1))
    return values * cosine + swapped * sine


class Copies:
    def __init__(self, sems):
        self.sems, self.made = sems, []

    def start(self, source, target):
        slot = len(self.made)

        def copy():
            return pltpu.make_async_copy(source(), target(), self.sems.at[slot])

        copy().start()
        self.made.append(copy)
        return slot

    def wait(self, *slots):
        for slot in slots:
            self.made[slot]().wait()
            self.made[slot] = None

    def finish(self):
        self.wait(*[slot for slot, copy in enumerate(self.made) if copy])


def chunk_of(i, size):
    return pl.ds(pl.multiple_of(i * size, size), size)


def forward_kernel(
    order_ref, ids_ref, x_ref, dy_ref, bias_ref, wq, wk, wv, wo, wi, wu,
    normed_out, unit_out, inv_out, kv_out, q_out, ag_out, ff_out, ffn_out, inner_out, outer_out, dy_out, cos_out, sin_out, begin_out, bias_out,
    x_all, dy_all, normed, qkv_w, o_w, i_w, u_w, kv, inner, act, grad, ff, ffn, inner_part, outer_part,
    xs, xr, ds, dr, ks, kr, cs, cr, local,
):
    across, along = Group("ctx"), Group("fsdp")
    core, chip, fsdp, partner = across.core, across.me, along.me, other_core(across)
    rows, width = dy_ref.shape
    copies = Copies(local)
    x_cuts = (0, 96, 192, 288, x_ref.shape[0])

    def x_view(member, a, b):
        return x_all.at[pl.ds(x_cuts[a], x_cuts[b] - x_cuts[a]), chunk_of(member, width)]

    def dy_view(member, a, b):
        return dy_all.at[core, pl.ds(rows // 2 * (a - 2), rows // 2 * (b - a)), chunk_of(member, width)]

    own_rows = [
        copies.start(lambda: x_ref, lambda: x_view(fsdp, 0, 4)),
        copies.start(lambda: dy_ref, lambda: dy_view(fsdp, 2, 4)),
    ]
    for i, ref in enumerate((wq, wk, wv)):
        copies.start(lambda ref=ref: ref.at[:, chunk_of(core, 128)], lambda i=i: qkv_w.at[:, pl.ds(128 * i, 128)])
    copies.start(lambda: wi.at[:, chunk_of(core, 512)], lambda: i_w)
    copies.start(lambda: wu.at[chunk_of(core, 512), :], lambda: u_w)
    copies.start(lambda: wo.at[chunk_of(core, 128), :], lambda: o_w)
    barrier(across.neighbours() + along.neighbours() + [partner])
    copies.wait(*own_rows)
    x_steps = Steps(gather(along, x_view, (xs, xr)))
    x_steps.take()
    dy_steps = Steps(gather(along, dy_view, (ds, dr), slots=PAIR_ONLY))
    dy_steps.take()

    lane = lax.rem(lax.broadcasted_iota(jnp.int32, (1, 128), 1), HEAD_DIM)
    freqs = jnp.zeros((1, 128), F32)
    for i in range(ROT):
        freqs = jnp.where(lane == i, 10000.0 ** (-2.0 * (i % (ROT // 2)) / ROT), freqs)
    for slot in range(4):
        group = order_ref[chip * 4 + slot]
        position = (group * GROUP + lax.broadcasted_iota(jnp.int32, (GROUP, 128), 0)).astype(F32)
        angles = position * freqs
        place = slice(GROUP * slot, GROUP * slot + GROUP)
        cos_out[place, :] = jnp.cos(angles)
        sin_out[place, :] = jnp.sin(angles)
        docs = ids_ref[group]
        begin = jnp.zeros((1, GROUP), jnp.int32)
        for doc in range(1, DOCS):
            before = jnp.sum(jnp.where(ids_ref[...] < doc, 1, 0), axis=0)
            before = jnp.sum(before, axis=1, keepdims=True)
            begin = jnp.where(docs == doc, before, begin)
        begin_out[slot] = jnp.concatenate([begin, begin], axis=1)

    x_steps.finish()
    gain, shift = x_all[rows : rows + 1, :].astype(F32), x_all[rows + 1 : rows + 2, :].astype(F32)

    def exchange(ref, i):
        half = ref.at[core, pl.ds(GROUP * i, GROUP), :]
        return remote(half, half, (cs, cr), 2 * (ref is dy_all) + i, partner)

    def norm(i, carry):
        place = chunk_of(i, 32)
        values = x_all[place, :].astype(F32)
        mean = jnp.mean(values, axis=1, keepdims=True)
        centered = values - mean
        inv = lax.rsqrt(jnp.mean(centered * centered, axis=1, keepdims=True) + EPS)
        normed[core, place, :] = (centered * inv * gain + shift).astype(BF16)
        unit_out[place, :] = (x_all[place, chunk_of(fsdp, width)].astype(F32) - mean) * inv
        inv_out[place, :] = inv
        return carry

    for i in range(2):
        lax.fori_loop(GROUP // 32 * i, GROUP // 32 * (i + 1), norm, 0)
        exchange(normed, i).start()
    copies.wait(2, 3, 4)
    dy_steps.take(2)

    def project(i, carry):
        slot = lax.rem(2 * core + i, 4)
        place = chunk_of(slot, GROUP)
        pre = dot(normed[lax.div(slot, 2), chunk_of(lax.rem(slot, 2), GROUP), :], qkv_w[...])
        bias = [bias_ref[:, pl.ds(pl.multiple_of(256 * j + 128 * core, 128), 128)] for j in range(3)]
        cosine, sine = cos_out[place, :], sin_out[place, :]
        queries = turned(pre[:, :128] + bias[0], cosine, sine).astype(BF16)
        q_out[slot] = (queries.astype(F32) * HEAD_DIM ** (-0.5)).astype(BF16)
        kv[place, :128] = turned(pre[:, 128:256] + bias[1], cosine, sine).astype(BF16)
        kv[place, 128:] = (pre[:, 256:] + bias[2]).astype(BF16)
        return carry

    lax.fori_loop(0, 2, project, 0)
    for i in range(2):
        exchange(normed, i).wait()
    lax.fori_loop(2, 4, project, 0)

    def kv_view(member, a, b):
        return kv_out.at[member, pl.ds(GROUP * a, GROUP * (b - a)), :]

    copies.wait(copies.start(lambda: kv, lambda: kv_view(chip, 0, 4)))
    kv_steps = Steps(gather(across, kv_view, (ks, kr)))
    kv_steps.take()
    dy_steps.take(2)
    normed_copy = copies.start(lambda: normed, lambda: normed_out)
    copies.wait(5, 6, 7)

    def four_by_four(one):
        def loop(i, carry):
            slot, j = lax.div(i, 4), lax.rem(i, 4)
            one(lax.div(slot, 2), chunk_of(lax.rem(slot, 2), GROUP), chunk_of(slot, GROUP), chunk_of(j, 512))
            return carry

        lax.fori_loop(0, 16, loop, 0)

    inner_bias = bias_ref[:, pl.ds(pl.multiple_of(768 + 512 * core, 128), 512)]

    def feed(slot, carry):
        place = chunk_of(slot, GROUP)
        value = dot(normed[lax.div(slot, 2), chunk_of(lax.rem(slot, 2), GROUP), :], i_w[...]) + inner_bias
        inner[place, :] = value
        curve = jnp.tanh(GELU_A * (value + GELU_B * value * value * value))
        act[place, :] = (0.5 * value * (1.0 + curve)).astype(BF16)
        return carry

    lax.fori_loop(0, 4, feed, 0)
    dy_steps.take(2)
    kv_steps.take(3)

    def feed_out(of, part, place, columns):
        ff[of, part, columns] = dot(act[place, :], u_w[:, columns]).astype(BF16)

    four_by_four(feed_out)
    copies.start(lambda: ff, lambda: ff_out)
    dy_steps.finish()
    for i in range(2):
        exchange(dy_all, i).start()
    kv_steps.take(2)
    bias_out[...] = jnp.zeros_like(bias_out)

    def gradients(i, carry):
        slot = lax.rem(2 * core + i, 4)
        place = chunk_of(slot, GROUP)
        dy_rows = dy_all[lax.div(slot, 2), chunk_of(lax.rem(slot, 2), GROUP), :]
        ag_out[slot] = dot(dy_rows, o_w[...], NT).astype(BF16)
        value = inner[place, :]
        square = value * value
        curve = jnp.tanh(GELU_A * (value + GELU_B * square * value))
        slope = 0.5 * (1.0 + curve) + 0.5 * value * (1.0 - curve * curve) * (GELU_A * (1.0 + 3.0 * GELU_B * square))
        out = (dot(dy_rows, u_w[...], NT) * slope).astype(BF16)
        grad[place, :] = out
        bias_out[...] += jnp.sum(out.astype(F32), axis=0, keepdims=True)
        return carry

    lax.fori_loop(0, 2, gradients, 0)
    for i in range(2):
        exchange(dy_all, i).wait()
    copies.start(lambda: dy_all, lambda: dy_out)
    lax.fori_loop(2, 4, gradients, 0)
    kv_steps.take(2)

    def inner_weights(i, carry):
        block = chunk_of(i, 256)
        inner_part[block, :] = dot(normed[:, :, block].reshape(2 * rows, 256), grad[...], TN).astype(BF16)
        return carry

    lax.fori_loop(0, 8, inner_weights, 0)
    copies.start(lambda: inner_part, lambda: inner_out)
    kv_steps.take(2)

    def outer_weights(i, carry):
        block = chunk_of(i, 256)
        outer_part[:, block] = dot(act[...], dy_all[:, :, block].reshape(2 * rows, 256), TN).astype(BF16)
        return carry

    lax.fori_loop(0, 8, outer_weights, 0)
    copies.start(lambda: outer_part, lambda: outer_out)
    kv_steps.take(2)

    def feed_back(of, part, place, columns):
        ffn[of, part, columns] = dot(grad[place, :], i_w[columns, :], NT).astype(BF16)

    four_by_four(feed_back)
    copies.start(lambda: ffn, lambda: ffn_out)
    kv_steps.finish()
    copies.finish()


def forward(order, ids, x, dy, bias, wq, wk, wv, wo, wi, wu):
    rows, width = dy.shape
    wide, both = wq.shape[0], 2 * rows

    def bf(*shape):
        return pltpu.VMEM(shape, BF16)

    def of(kind, *shape):
        return jax.ShapeDtypeStruct(shape, kind)

    return pl.pallas_call(
        forward_kernel,
        out_shape=[
            of(BF16, 2, rows, wide),
            of(F32, rows, width),
            of(F32, rows, 1),
            of(BF16, 8, both, 256),
            of(BF16, 4, GROUP, 128),
            of(BF16, 4, GROUP, 128),
            of(BF16, 2, rows, wide),
            of(BF16, 2, rows, wide),
            of(BF16, wide, 512),
            of(BF16, 512, wide),
            of(BF16, 2, rows, wide),
            of(F32, both, 128),
            of(F32, both, 128),
            of(jnp.int32, 4, 1, TILE),
            of(F32, 1, 512),
        ],
        in_specs=[SMEM, VMEM, ANY, ANY, VMEM] + [ANY] * 6,
        out_specs=[ANY, VMEM, VMEM, ANY, VMEM, VMEM, ANY, ANY, ANY, ANY, ANY, VMEM, VMEM, VMEM, VMEM],
        scratch_shapes=[
            bf(x.shape[0], wide),
            bf(2, rows, wide),
            bf(2, rows, wide),
            bf(wide, 384),
            bf(128, wide),
            bf(wide, 512),
            bf(512, wide),
            bf(both, 256),
            pltpu.VMEM((both, 512), F32),
            bf(both, 512),
            bf(both, 512),
            bf(2, rows, wide),
            bf(2, rows, wide),
            bf(wide, 512),
            bf(512, wide),
        ]
        + pairs(GATHER_SLOTS) * 3
        + pairs(4)
        + [pltpu.SemaphoreType.DMA((15,))],
        compiler_params=params(0, 56),
        name="forward",
    )(order, ids, x, dy, bias, wq, wk, wv, wo, wi, wu)


def cut_rows(ref, a, b):
    step = ref.shape[0] // 4
    return ref.at[pl.ds(step * a, step * (b - a)), :]


def rows_scatter(group, part_ref, out, arriving, hold, sems):
    cs, cr, send, recv = sems
    core, partner = group.core, other_core(group)

    def exchange():
        return remote(part_ref.at[1 - core], arriving, (cs, cr), 0, partner)

    exchange().start()
    yield
    exchange().wait()

    def one(i, carry):
        rows = pl.ds(pl.multiple_of(i * 32, 32), 32)
        arriving[rows, :] = (arriving[rows, :].astype(F32) + part_ref[core, rows, :].astype(F32)).astype(BF16)
        return carry

    lax.fori_loop(0, arriving.shape[0] // 32, one, 0)
    width, size = out.shape[1], out.shape[0] // 2

    def cut(ref, a, b):
        return ref.at[pl.ds(size * (a - 2), size * (b - a)), :]

    def part(step, flip, a, b):
        columns = pl.ds(pl.multiple_of(group.member(step, flip) * width, width), width)
        return arriving.at[pl.ds(size * (a - 2), size * (b - a)), columns]

    def result(a, b, refs):
        target = cut(out, a, b)
        target[...] = total_of(refs)

    yield from scatter(group, part, cut, hold, result, (send, recv), pair_first=False)


def peers(axis):
    ctx, fsdp = lax.axis_index("ctx"), lax.axis_index("fsdp")
    count = lax.axis_size(axis)
    if axis == "ctx":
        return [(lax.rem(ctx + offset, count), fsdp) for offset in range(1, count)]
    return [(ctx, lax.rem(fsdp + offset, count)) for offset in range(1, count)]


def sum_small(x_ref, out, hold, sems, devices):
    def copy(i):
        return remote(x_ref, hold.at[i], sems, i, devices[i])

    for i in range(len(devices)):
        copy(i).start()
    yield
    total = x_ref[...]
    for i in range(len(devices)):
        copy(i).wait_recv()
        total = total + hold[i]
    out[...] = total
    for i in range(len(devices)):
        copy(i).wait_send()


def reduce_one(group, source, target, hold, sems):
    rs, rr, gs, gr, cs, cr = sems
    core, partner = group.core, other_core(group)
    rows, width = source.shape[0] // 8, source.shape[1]
    by_rows = rows % 64 == 0

    def quarters(ref, a, b):
        if by_rows:
            return ref.at[pl.ds(rows // 4 * a, rows // 4 * (b - a)), :]
        return ref.at[:, pl.ds(width // 4 * a, width // 4 * (b - a))]

    def part(step, flip, a, b):
        start = pl.multiple_of(group.member(step, flip) * rows, rows)
        return quarters(source.at[pl.ds(start, rows), :], a, b)

    def view(member, a, b):
        start = pl.multiple_of(member * rows, rows)
        return quarters(target.at[core, pl.ds(start, rows), :], a, b)

    def result(a, b, terms):
        place = view(group.me, a, b)
        place[...] = total_of(terms).astype(BF16)

    copies = []

    def arrived(block, a, b):
        slot = len(copies)

        def copy():
            ref = view(group.member(*block), a, b)
            return remote(ref, ref, (cs, cr), slot, partner)

        copy().start()
        copies.append(copy)

    yield from scatter(group, part, quarters, hold, result, (rs, rr))
    yield from gather(group, view, (gs, gr), arrived)
    yield
    for copy in copies:
        copy().wait()


def reduce_scratch(shape):
    return pltpu.VMEM((HOLD, shape[0] // 8, shape[1]), BF16)


def reduce_sems():
    return pairs(SCATTER_SLOTS) + pairs(GATHER_SLOTS) + pairs(GATHER_SLOTS + 1)


STATES = 11


def state_of(j):
    late = lax.div(j + 7, 16)
    return j * (1 - late) + (9 + lax.rem(j, 2)) * late


FORWARD_PLAN = ((2, 1), (5, 1), (6, 1), (10, 1), (13, 1), (15, 1), (16, 1))
BACKWARD_PLAN = ((1, 1), (3, 1), (8, 3), (13, 2), (15, 2))
BRANCH_PLAN = ((2, 1), (5, 1), (8, 1), (12, 1))


def attention_kernel(
    table, q_ref, cotangent_ref, kv_ref, begin_ref, ff_ref, wo_ref, inner_part, outer_part,
    att_ref, dq_ref, dkv_ref, sum_ref, inner_out, outer_out,
    kvp, state_max, state_sum, state_acc, dq_items, dkv_items, lse_ref, delta_ref, branch, arriving, branch_hold, inner_hold, outer_hold, *sems
):
    left = lax.broadcasted_iota(jnp.int32, (1, 128), 1) < HEAD_DIM
    across, along = Group("ctx"), Group("fsdp")
    barrier(across.neighbours() + along.neighbours() + [other_core(across)])
    weights_steps = Steps(
        reduce_one(across, inner_part, inner_out, inner_hold, sems[:6]),
        reduce_one(across, outer_part, outer_out, outer_hold, sems[6:12]),
    )
    branch_steps = Steps(rows_scatter(along, branch, sum_ref, arriving, branch_hold, sems[12:]))
    weights_steps.take()

    def place(g, carry):
        tile, half = lax.div(g, 2), lax.rem(g, 2)
        kvp[tile, pl.ds(pl.multiple_of(half * GROUP, GROUP), GROUP), :] = kv_ref[table[g]]
        return carry

    lax.fori_loop(0, GROUPS, place, 0)

    def bit(number):
        return jnp.minimum(jnp.maximum(number, 0), 1)

    def pair_facts(p):
        g0, g1 = table[32 + 2 * p], table[33 + 2 * p]
        low, high = jnp.minimum(g0, g1), jnp.maximum(g0, g1)
        return low, high, bit(g0 - g1), lax.div(low, 2) + 1

    key_row = lax.broadcasted_iota(jnp.int32, (TILE, TILE), 0)
    column = lax.broadcasted_iota(jnp.int32, (1, TILE), 1)
    query_row = jnp.where(column < GROUP, column, column - GROUP)

    def item_facts(p, j):
        low, high, low_slot, count = pair_facts(p)
        second = bit(j - count + 1)
        tile = second * TILES + (1 - second) * (count - 1) - j
        slot = 2 * p + second * (1 - low_slot) + (1 - second) * low_slot
        position = (second * high + (1 - second) * low) * GROUP
        last = query_row + (position - tile * TILE)
        begin = begin_ref[slot] - tile * TILE
        allowed = (key_row <= last) & (key_row >= begin)
        keep = bit(j * (j - count) * (j - count)).astype(F32)
        return tile, slot, allowed, keep

    def stacked(rows):
        zero = jnp.zeros_like(rows)
        return jnp.concatenate([jnp.where(left, rows, zero), jnp.where(left, zero, rows)], axis=0)

    def unstacked(columns):
        rows = columns.T
        return jnp.where(left, rows[:GROUP], rows[GROUP:])

    def final_item(p, i):
        low, high, low_slot, count = pair_facts(p)
        is_low = low_slot if i else 1 - low_slot
        return count * is_low + 10 * (1 - is_low)

    for p in range(2):
        state_max[p, 0] = jnp.full((1, TILE), FLOOR, F32)
        state_sum[p, 0] = jnp.zeros((1, TILE), F32)
        state_acc[p, 0] = jnp.zeros((128, TILE), F32)

    def forward(j, carry):
        weights_steps.at(j, FORWARD_PLAN)
        now, after = state_of(j), state_of(j + 1)
        for p in range(2):
            tile, slot, allowed, keep = item_facts(p, j)
            scores = jnp.where(allowed, dot(kvp[tile, :, :128], stacked(q_ref[slot]), NT), MASKED)
            old_max = state_max[p, now] * keep + FLOOR * (1.0 - keep)
            new_max = jnp.maximum(old_max, jnp.max(scores, axis=0, keepdims=True))
            weights = jnp.exp(scores - new_max)
            factor = jnp.exp(old_max - new_max)
            state_max[p, after] = new_max
            state_sum[p, after] = state_sum[p, now] * factor + jnp.sum(weights, axis=0, keepdims=True)
            state_acc[p, after] = state_acc[p, now] * factor + dot(kvp[tile, :, 128:], weights.astype(BF16), TN)
        return carry

    lax.fori_loop(0, ITEMS, forward, 0)

    for p in range(2):
        for i in range(2):
            item = final_item(p, i)
            slot = 2 * p + i
            total = state_sum[p, item]
            out = state_acc[p, item] / total
            lse_ref[slot] = state_max[p, item] + jnp.log(total)
            cotangent = stacked(cotangent_ref[slot].astype(F32)).T
            delta_ref[slot] = jnp.sum(cotangent * out, axis=0, keepdims=True)
            att_ref[slot] = unstacked(out).astype(BF16)

    def branches(i, carry):
        slot, columns = lax.div(i, 4), pl.ds(pl.multiple_of(lax.rem(i, 4) * 512, 512), 512)
        core, rows = lax.div(slot, 2), pl.ds(pl.multiple_of(lax.rem(slot, 2) * GROUP, GROUP), GROUP)
        branch[core, rows, columns] = (ff_ref[core, rows, columns].astype(F32) + dot(att_ref[slot], wo_ref[:, columns])).astype(BF16)
        return carry

    lax.fori_loop(0, 16, branches, 0)
    branch_steps.take()

    for p in range(2):
        dq_items[p, 0] = jnp.zeros((128, TILE), F32)

    def backward(j, carry):
        weights_steps.at(j, BACKWARD_PLAN)
        branch_steps.at(j, BRANCH_PLAN)
        now, after = state_of(j), state_of(j + 1)
        for p in range(2):
            tile, slot, allowed, keep = item_facts(p, j)
            queries, cotangent = stacked(q_ref[slot]), stacked(cotangent_ref[slot])
            scores = dot(kvp[tile, :, :128], queries, NT)
            probs = jnp.where(allowed, jnp.exp(scores - lse_ref[slot]), 0.0)
            prob_grad = dot(kvp[tile, :, 128:], cotangent, NT)
            score_grad = (probs * (prob_grad - delta_ref[slot])).astype(BF16)
            dq_items[p, after] = dq_items[p, now] * keep + dot(kvp[tile, :, :128], score_grad, TN)
            key_grad = dot(score_grad, queries).astype(BF16)
            value_grad = dot(probs.astype(BF16), cotangent).astype(BF16)
            for half in range(2):
                rows = slice(GROUP * half, GROUP * half + GROUP)
                dkv_items[p, j, half, :, :128] = key_grad[rows]
                dkv_items[p, j, half, :, 128:] = value_grad[rows]
        return carry

    lax.fori_loop(0, ITEMS, backward, 0)

    for p in range(2):
        for i in range(2):
            dq_ref[2 * p + i] = unstacked(dq_items[p, final_item(p, i)])

    counts = [pair_facts(p)[3] for p in range(2)]

    def collect(s, carry):
        group = table[36 + s]
        tile, half = lax.div(group, 2), lax.rem(group, 2)
        total = jnp.zeros((GROUP, 256), F32)
        for p in range(2):
            low_item = dkv_items[p, jnp.maximum(counts[p] - 1 - tile, 0), half].astype(F32)
            high_item = dkv_items[p, jnp.maximum(TILES - tile, counts[p]), half].astype(F32)
            total = total + low_item * bit(counts[p] - tile).astype(F32)
            total = total + high_item * bit(TILES - tile - counts[p] + 1).astype(F32)
        dkv_ref[s] = total.astype(BF16)
        return carry

    lax.fori_loop(0, GROUPS, collect, 0)
    branch_steps.finish()
    weights_steps.finish()


def attention(table, queries, cotangent, kv, begin, ff, wo, inner_part, outer_part):
    rows, width = ff.shape[1], ff.shape[2]
    return pl.pallas_call(
        attention_kernel,
        out_shape=[
            jax.ShapeDtypeStruct((4, GROUP, 128), BF16),
            jax.ShapeDtypeStruct((4, GROUP, 128), F32),
            jax.ShapeDtypeStruct((GROUPS, GROUP, 256), BF16),
            jax.ShapeDtypeStruct((rows, width // 8), F32),
            jax.ShapeDtypeStruct((2,) + inner_part.shape, BF16),
            jax.ShapeDtypeStruct((2,) + outer_part.shape, BF16),
        ],
        in_specs=[SMEM] + [VMEM] * 8,
        out_specs=[VMEM] * 6,
        scratch_shapes=[
            pltpu.VMEM((TILES, TILE, 256), BF16),
            pltpu.VMEM((2, STATES, 1, TILE), F32),
            pltpu.VMEM((2, STATES, 1, TILE), F32),
            pltpu.VMEM((2, STATES, 128, TILE), F32),
            pltpu.VMEM((2, STATES, 128, TILE), F32),
            pltpu.VMEM((2, ITEMS, 2, GROUP, 256), BF16),
            pltpu.VMEM((4, 1, TILE), F32),
            pltpu.VMEM((4, 1, TILE), F32),
            pltpu.VMEM(ff.shape, BF16),
            pltpu.VMEM((rows, width), BF16),
            pltpu.VMEM((HOLD, rows, width // 8), BF16),
            reduce_scratch(inner_part.shape),
            reduce_scratch(outer_part.shape),
        ]
        + reduce_sems() * 2
        + pairs(1)
        + pairs(SCATTER_SLOTS),
        compiler_params=params(8, 62),
        name="attention",
    )(table, queries, cotangent, kv, begin, ff, wo, inner_part, outer_part)


def backward_kernel(
    dkv_ref, dq_ref, cos_ref, sin_ref, normed_ref, w_ref, ff_ref, out_part, unit_ref, inv_ref, gain_ref, dy_ref, vec_ref,
    q_out, kv_out, out_out, input_out, vec_out,
    keys_hold, own, pre, q_part, kv_part, branch, arriving, rows_hold, local, q_hold, kv_hold, out_hold,
    stats, stats_hold, stats_sum, vec, vec_hold, *sems
):
    across, along = Group("ctx"), Group("fsdp")
    core = across.core
    barrier(peers("ctx") + peers("fsdp"))

    def part(step, flip, a, b):
        return cut_rows(dkv_ref.at[across.member(step, flip)], a, b)

    def result(a, b, refs):
        target = cut_rows(own, a, b)
        target[...] = total_of(refs)

    keys = Steps(scatter(across, part, cut_rows, keys_hold, result, sems[:2]))
    keys.take()
    chunk = pre.shape[0] // 4
    for i in range(4):
        rows = slice(chunk * i, chunk * (i + 1))
        grad = turned(dq_ref[rows, :] * HEAD_DIM ** (-0.5), cos_ref[rows, :], -sin_ref[rows, :])
        pre[rows, :128] = grad.astype(BF16)

    def query_weights(i, carry):
        block = pl.ds(pl.multiple_of(i * 256, 256), 256)
        q_part[block, :] = dot(normed_ref[:, block], pre[:, :128], TN).astype(BF16)
        return carry

    lax.fori_loop(0, 8, query_weights, 0)
    keys.finish()
    for i in range(4):
        rows = slice(chunk * i, chunk * (i + 1))
        grad = turned(own[rows, :128], cos_ref[rows, :], -sin_ref[rows, :])
        pre[rows, 128:256] = grad.astype(BF16)
        pre[rows, 256:] = own[rows, 128:].astype(BF16)

    def key_weights(i, carry):
        block = pl.ds(pl.multiple_of(i * 256, 256), 256)
        kv_part[block, :] = dot(normed_ref[:, block], pre[:, 128:], TN).astype(BF16)
        return carry

    lax.fori_loop(0, 8, key_weights, 0)
    weights = Steps(
        reduce_one(across, kv_part, kv_out, kv_hold, sems[2:8]),
        reduce_one(across, q_part, q_out, q_hold, sems[8:14]),
        reduce_one(across, out_part, out_out, out_hold, sems[14:20]),
    )
    weights.take()

    def normed_grad(of):
        def one(i, carry):
            rows = pl.ds(pl.multiple_of(lax.div(i, 4) * GROUP, GROUP), GROUP)
            columns = pl.ds(pl.multiple_of(lax.rem(i, 4) * 512, 512), 512)
            from_rows = pl.ds(pl.multiple_of(of * 2 * GROUP + lax.div(i, 4) * GROUP, GROUP), GROUP)
            grad = ff_ref[of, rows, columns].astype(F32) + dot(pre[from_rows, :], w_ref[columns, :], NT)
            branch[of, rows, columns] = grad.astype(BF16)
            return carry

        lax.fori_loop(0, 8, one, 0)

    normed_grad(1 - core)
    rows_steps = Steps(rows_scatter(along, branch, local, arriving, rows_hold, sems[20:24]))
    rows_steps.take()
    normed_grad(core)
    for count in (1, 2, 1, 2, 2):
        rows_steps.take()
        weights.take(count)
    rows_steps.finish()

    whole = local[...]
    unit = unit_ref[...]
    scaled = whole * gain_ref[...]
    lane = lax.broadcasted_iota(jnp.int32, (1, 128), 1)
    first = jnp.sum(scaled, axis=1, keepdims=True)
    second = jnp.sum(scaled * unit, axis=1, keepdims=True)
    stats[...] = jnp.where(lane == 0, first, jnp.where(lane == 1, second, 0.0)).T[:8]
    stats_steps = Steps(sum_small(stats, stats_sum, stats_hold, sems[24:26], peers("fsdp")))
    stats_steps.take()
    vec[...] = vec_ref[...]
    vec[0:1, :] = jnp.sum(whole * unit, axis=0, keepdims=True)
    vec[1:2, :] = jnp.sum(whole, axis=0, keepdims=True)
    half = pl.ds(pl.multiple_of(core * 128, 128), 128)
    for i in range(3):
        vec[3 + i : 4 + i, half] = jnp.sum(pre[:, 128 * i : 128 * i + 128].astype(F32), axis=0, keepdims=True)
    vec_steps = Steps(sum_small(vec, vec_out, vec_hold, sems[26:28], peers("ctx")))
    vec_steps.take()
    weights.take(2)
    stats_steps.finish()
    back = jnp.concatenate([stats_sum[...], jnp.zeros((120, stats_sum.shape[1]), F32)], axis=0).T * (1.0 / 2048)
    input_out[...] = dy_ref[...].astype(F32) + inv_ref[...] * (scaled - back[:, 0:1] - unit * back[:, 1:2])
    vec_steps.finish()
    weights.finish()


def backward(dkv, dq, cosine, sine, normed, w, ff, out_part, unit, inv, gain, dy, vec):
    both, rows, width, wide = normed.shape[0], unit.shape[0], unit.shape[1], normed.shape[1]

    def bf(*shape):
        return pltpu.VMEM(shape, BF16)

    def f32(*shape):
        return pltpu.VMEM(shape, F32)

    return pl.pallas_call(
        backward_kernel,
        out_shape=[
            jax.ShapeDtypeStruct((2, wide, 128), BF16),
            jax.ShapeDtypeStruct((2, wide, 256), BF16),
            jax.ShapeDtypeStruct((2,) + out_part.shape, BF16),
            jax.ShapeDtypeStruct(unit.shape, F32),
            jax.ShapeDtypeStruct(vec.shape, F32),
        ],
        in_specs=[VMEM] * 13,
        out_specs=[VMEM] * 5,
        scratch_shapes=[
            bf(HOLD, both, 256),
            f32(both, 256),
            bf(both, 384),
            bf(wide, 128),
            bf(wide, 256),
            bf(2, rows, wide),
            bf(rows, wide),
            bf(HOLD, rows, width),
            f32(rows, width),
            reduce_scratch((wide, 128)),
            reduce_scratch((wide, 256)),
            reduce_scratch(out_part.shape),
            f32(8, rows),
            f32(7, 8, rows),
            f32(8, rows),
            f32(*vec.shape),
            f32(15, *vec.shape),
        ]
        + pairs(SCATTER_SLOTS)
        + reduce_sems() * 3
        + pairs(1)
        + pairs(SCATTER_SLOTS)
        + pairs(7)
        + pairs(15),
        compiler_params=params(9, 56),
        name="backward",
    )(dkv, dq, cosine, sine, normed, w, ff, out_part, unit, inv, gain, dy, vec)


def body(
    layer_input,
    norm_gain,
    norm_bias,
    query_weight,
    query_bias,
    key_weight,
    key_bias,
    value_weight,
    value_bias,
    out_weight,
    out_bias,
    inner_weight,
    inner_bias,
    outer_weight,
    outer_bias,
    output_grad,
    group_order,
    sequence_ids,
):
    ctx = lax.axis_index("ctx")
    core = lax.rem(ctx, 2)
    rows = layer_input.shape[0]
    both = 2 * rows
    extra = jnp.concatenate([norm_gain[None], norm_bias[None], jnp.zeros((14, norm_gain.shape[0]), BF16)])
    bias = jnp.concatenate([query_bias, key_bias, value_bias, inner_bias]).astype(F32)[None]
    (normed, unit, inv, kv_all, scaled, attended_grad, ff, ff_normed_grad, inner_part, outer_part, dy, cosine, sine, begin, inner_sum) = forward(
        group_order, sequence_ids.reshape(GROUPS, 1, GROUP), jnp.concatenate([layer_input, extra]), output_grad, bias,
        query_weight, key_weight, value_weight, out_weight, inner_weight, outer_weight,
    )

    def half(array, axis):
        size = array.shape[axis] // 2
        return lax.dynamic_slice_in_dim(array, core * size, size, axis)

    wo = half(out_weight, 0)
    slot_of = jnp.sum(
        jnp.where(group_order[None, :] == jnp.arange(GROUPS)[:, None], jnp.arange(GROUPS)[None, :], 0), axis=1
    ).astype(jnp.int32)
    my_groups = lax.dynamic_slice_in_dim(group_order, lax.div(ctx, 2) * 4, 4, 0)
    table = jnp.concatenate([slot_of, my_groups, group_order]).astype(jnp.int32)
    attended, dq, dkv, summed, inner_w_grad, outer_w_grad = attention(
        table, scaled, attended_grad, kv_all.reshape(GROUPS, GROUP, 256), begin, ff, wo, inner_part, outer_part
    )
    attended = attended.reshape(both, 128)

    def weight_grad(left, right):
        return jnp.einsum("rc,rd->cd", left, right, preferred_element_type=F32).astype(BF16)

    layer_output = (
        layer_input.astype(F32) + summed + out_bias.astype(F32) + outer_bias.astype(F32)
    ).astype(BF16)

    vec = jnp.zeros((16, 256), F32)
    vec = vec.at[2].set(jnp.sum(output_grad.astype(F32), axis=0))
    vec = lax.dynamic_update_slice(vec, inner_sum.reshape(2, 256), (6 + 2 * core, 0))
    query_grad, kv_grad, out_grad, input_grad, vectors = backward(
        dkv.reshape(8, both, 256), dq.reshape(both, 128), cosine, sine, normed.reshape(both, -1),
        jnp.concatenate([half(query_weight, 1), half(key_weight, 1), half(value_weight, 1)], axis=1),
        ff_normed_grad, weight_grad(attended, dy.reshape(both, -1)), unit, inv, norm_gain.astype(F32)[None], output_grad, vec,
    )

    def side_by_side(array):
        return jnp.concatenate([array[0], array[1]], axis=1).astype(F32)

    return (
        layer_output,
        input_grad,
        vectors[0],
        vectors[1],
        side_by_side(query_grad),
        vectors[3],
        side_by_side(kv_grad[:, :, :128]),
        vectors[4],
        side_by_side(kv_grad[:, :, 128:]),
        vectors[5],
        out_grad.reshape(256, 2048).astype(F32),
        vectors[2],
        side_by_side(inner_w_grad),
        vectors[6:10].reshape(1024),
        outer_w_grad.reshape(1024, 2048).astype(F32),
        vectors[2],
    )


def solution(mesh):
    in_specs = (
        P("ctx", "fsdp"),
        P("fsdp"),
        P("fsdp"),
        P(None, "fsdp"),
        P("fsdp"),
        P(None, "fsdp"),
        P("fsdp"),
        P(None, "fsdp"),
        P("fsdp"),
        P("fsdp", None),
        P("fsdp"),
        P(None, "fsdp"),
        P("fsdp"),
        P("fsdp", None),
        P("fsdp"),
        P("ctx", "fsdp"),
        P(),
        P(),
    )
    out_specs = (
        P("ctx", "fsdp"),
        P("ctx", "fsdp"),
        P("fsdp"),
        P("fsdp"),
        P(None, "fsdp"),
        P("fsdp"),
        P(None, "fsdp"),
        P("fsdp"),
        P(None, "fsdp"),
        P("fsdp"),
        P("fsdp", None),
        P("fsdp"),
        P(None, "fsdp"),
        P("fsdp"),
        P("fsdp", None),
        P("fsdp"),
    )
    return jax.shard_map(body, mesh=mesh, in_specs=in_specs, out_specs=out_specs, check_vma=False)
```

```python
from functools import partial

import jax
import jax.numpy as jnp
from jax import lax
from jax.experimental import pallas as pl
from jax.experimental.pallas import tpu as pltpu
from jax.sharding import PartitionSpec as P

HEAD_DIM = 64
ROT = 32
GROUP = 192
GROUPS = 32
SEQ_LEN = 6144
DOCS = 5
EPS = 1e-05
MASKED = -1e30
FLOOR = -1e29
GELU_A = 0.7978845608028654
GELU_B = 0.044715
MESH = pl.DeviceIdType.MESH
BF16 = jnp.bfloat16
F32 = jnp.float32
ANY = pl.BlockSpec(memory_space=pl.ANY)
VMEM = pl.BlockSpec(memory_space=pltpu.VMEM)
SMEM = pl.BlockSpec(memory_space=pltpu.SMEM)
MIB = 2**20


class Group:
    def __init__(self, axis):
        ctx, fsdp = lax.axis_index("ctx"), lax.axis_index("fsdp")
        self.axis, self.ctx, self.fsdp = axis, ctx, fsdp
        self.core = lax.rem(ctx, 2)
        self.me = lax.div(ctx, 2) if axis == "ctx" else fsdp
        self.ring, self.pair = lax.rem(self.me, 4), lax.div(self.me, 4)

    def member(self, step, flip):
        pair = 1 - self.pair if flip else self.pair
        return pair * 4 + lax.rem(self.ring + (step + 4), 4)

    def device(self, step, flip):
        member = self.member(step, flip)
        if self.axis == "ctx":
            return (member * 2 + self.core, self.fsdp)
        return (self.ctx, member)

    def neighbours(self):
        return [self.device(1, 0), self.device(-1, 0), self.device(0, 1)]


def other_core(group):
    return (group.ctx + 1 - 2 * group.core, group.fsdp)


def barrier(devices):
    semaphore = pltpu.get_barrier_semaphore()
    for device in devices:
        pl.semaphore_signal(semaphore, inc=1, device_id=device, device_id_type=MESH)
    pl.semaphore_wait(semaphore, len(devices))


def remote(source, target, sems, slot, device):
    return pltpu.make_async_remote_copy(
        src_ref=source,
        dst_ref=target,
        send_sem=sems[0].at[slot],
        recv_sem=sems[1].at[slot],
        device_id=device,
        device_id_type=MESH,
    )


GATHER = (
    (1, 0, (0, 0), 0, 2, None),
    (-1, 0, (0, 0), 0, 2, None),
    (0, 1, (0, 0), 2, 4, None),
    (1, 0, (0, 0), 2, 4, None),
    (-1, 0, (0, 0), 2, 4, None),
    (0, 1, (0, 0), 0, 2, None),
    (1, 0, (-1, 0), 0, 1, 0),
    (-1, 0, (1, 0), 1, 2, 1),
    (0, 1, (-1, 0), 0, 2, 0),
    (0, 1, (1, 0), 0, 2, 1),
    (0, 1, (2, 0), 0, 1, 6),
    (0, 1, (2, 0), 1, 2, 7),
    (1, 0, (0, 1), 2, 4, 2),
    (-1, 0, (0, 1), 2, 4, 2),
    (1, 0, (-1, 0), 2, 3, 3),
    (-1, 0, (1, 0), 3, 4, 4),
    (1, 0, (-1, 1), 2, 3, 12),
    (-1, 0, (1, 1), 3, 4, 13),
)
GATHER_ORDER = (0, 1, 2, 3, 4, 6, 7, 12, 13, 5, 8, 14, 15, 9, 10, 16, 17, 11)
GATHER_SLOTS = len(GATHER)
PAIR_ONLY = (2, 3, 4, 12, 13, 14, 15, 16, 17)


def gather(group, view, sems, arrived=None, slots=tuple(range(GATHER_SLOTS)), own=None):
    started = []

    def start(slot):
        step, flip, block, a, b, _ = GATHER[slot]

        def copy():
            ref = view(group.member(*block), a, b)
            source = own(a, b) if own and block == (0, 0) else ref
            return remote(source, ref, sems, slot, group.device(step, flip))

        copy().start()
        started.append(copy)

    for slot in slots:
        if GATHER[slot][5] is None:
            start(slot)
    if arrived:
        arrived((0, 0), 0, 4)
    for slot in [i for i in GATHER_ORDER if i in slots]:
        step, flip, block, a, b, _ = GATHER[slot]
        yield
        source = (block[0] - step, block[1] ^ flip)
        ref = view(group.member(*source), a, b)
        remote(ref, ref, sems, slot, group.device(step, flip)).wait_recv()
        for later in slots:
            if GATHER[later][5] == slot:
                start(later)
        if arrived:
            arrived(source, a, b)
    for copy in started:
        copy().wait_send()


SCATTER_SLOTS = 23
HOLD = 7


def add_into(target, *sources):
    total = target[...].astype(F32)
    for source in sources:
        total = total + source[...].astype(F32)
    target[...] = total.astype(target.dtype)


def scatter(group, part, quarters, hold, result, sems, pair_first=True):
    started = []

    def held(k, a, b):
        return quarters(hold.at[k], a, b)

    def start(slot, source, step, flip, k, a, b):
        def copy():
            return remote(source(), held(k, a, b), sems, slot, group.device(step, flip))

        copy().start()
        started.append(copy)

    def send_part(slot, block, step, flip, k, a, b):
        start(slot, lambda: part(*block, a, b), step, flip, k, a, b)

    def send_held(slot, source, step, flip, k, a, b):
        start(slot, lambda: held(source, a, b), step, flip, k, a, b)

    def wait(slot, k, a, b):
        ref = held(k, a, b)
        remote(ref, ref, sems, slot, group.device(0, 1)).wait_recv()

    if pair_first:
        send_part(0, (2, 1), 0, 1, 0, 0, 2)
    send_part(10, (2, 1), 1, 0, 0, 2, 3)
    send_part(11, (2, 1), -1, 0, 0, 3, 4)
    if pair_first:
        send_part(1, (1, 1), 0, 1, 1, 0, 2)
        send_part(2, (-1, 1), 0, 1, 2, 0, 2)
    send_part(16, (2, 0), 1, 0, 3, 2, 3)
    send_part(17, (2, 0), -1, 0, 3, 3, 4)
    send_part(12, (1, 1), 1, 0, 1, 3, 4)
    send_part(13, (-1, 1), -1, 0, 2, 2, 3)
    send_part(18, (1, 0), 1, 0, 4, 3, 4)
    send_part(19, (-1, 0), -1, 0, 5, 2, 3)
    if pair_first:
        send_part(3, (0, 1), 0, 1, 3, 0, 2)
    yield
    wait(10, 0, 2, 3)
    add_into(held(0, 2, 3), part(1, 1, 2, 3))
    send_held(14, 0, 1, 0, 1, 2, 3)
    wait(11, 0, 3, 4)
    add_into(held(0, 3, 4), part(-1, 1, 3, 4))
    send_held(15, 0, -1, 0, 2, 3, 4)
    if pair_first:
        yield
        wait(0, 0, 0, 2)
        add_into(held(0, 0, 2), part(2, 0, 0, 2))
        send_held(4, 0, 1, 0, 4, 0, 1)
        send_held(5, 0, -1, 0, 4, 1, 2)
    yield
    wait(16, 3, 2, 3)
    add_into(held(3, 2, 3), part(1, 0, 2, 3))
    send_held(20, 3, 1, 0, 4, 2, 3)
    wait(17, 3, 3, 4)
    add_into(held(3, 3, 4), part(-1, 0, 3, 4))
    send_held(21, 3, -1, 0, 5, 3, 4)
    if pair_first:
        yield
        wait(1, 1, 0, 2)
        add_into(held(1, 0, 2), part(1, 0, 0, 2))
        send_held(6, 1, 1, 0, 5, 1, 2)
    yield
    wait(12, 1, 3, 4)
    wait(14, 1, 2, 3)
    wait(13, 2, 2, 3)
    wait(15, 2, 3, 4)
    add_into(held(1, 2, 4), held(2, 2, 4), part(0, 1, 2, 4))
    send_held(22, 1, 0, 1, 6, 2, 4)
    if pair_first:
        yield
        wait(2, 2, 0, 2)
        add_into(held(2, 0, 2), part(-1, 0, 0, 2))
        send_held(8, 2, -1, 0, 6, 0, 1)
        yield
        wait(4, 4, 0, 1)
        add_into(held(1, 0, 1), held(4, 0, 1))
        send_held(7, 1, 1, 0, 5, 0, 1)
        wait(5, 4, 1, 2)
        add_into(held(2, 1, 2), held(4, 1, 2))
        send_held(9, 2, -1, 0, 6, 1, 2)
        yield
        wait(3, 3, 0, 2)
        wait(6, 5, 1, 2)
        wait(8, 6, 0, 1)
        wait(7, 5, 0, 1)
        wait(9, 6, 1, 2)
        result(0, 2, [part(0, 0, 0, 2), held(3, 0, 2), held(5, 0, 2), held(6, 0, 2)])
    yield
    wait(18, 4, 3, 4)
    wait(20, 4, 2, 3)
    wait(19, 5, 2, 3)
    wait(21, 5, 3, 4)
    wait(22, 6, 2, 4)
    result(2, 4, [part(0, 0, 2, 4), held(4, 2, 4), held(5, 2, 4), held(6, 2, 4)])
    for copy in started:
        copy().wait_send()


def total_of(refs):
    total = refs[0][...].astype(F32)
    for ref in refs[1:]:
        total = total + ref[...].astype(F32)
    return total


def drain(*programs):
    programs = list(programs)
    while programs:
        programs = [p for p in programs if next(p, "end") != "end"]


def pairs(count):
    return [pltpu.SemaphoreType.DMA((count,)), pltpu.SemaphoreType.DMA((count,))]


def params(collective_id, mib):
    return pltpu.CompilerParams(
        collective_id=collective_id, has_side_effects=True, vmem_limit_bytes=mib * MIB
    )


ROW_CUTS = (0, 96, 192, 288, 400)


TILE = 2 * GROUP
TILES = SEQ_LEN // TILE
ITEMS = TILES + 1
KEYS, VALUES = slice(0, 128), slice(128, 256)
NT = (((1,), (1,)), ((), ()))
TN = (((0,), (0,)), ((), ()))


def dot(a, b, dims=(((1,), (0,)), ((), ()))):
    return lax.dot_general(a, b, dims, preferred_element_type=F32)


class Steps:
    def __init__(self, *programs):
        self.programs = list(programs)

    def take(self, count=1):
        for _ in range(count):
            self.programs = [p for p in self.programs if next(p, "end") != "end"]

    def at(self, j, plan):
        for iteration, count in plan:
            pl.when(j == iteration)(partial(self.take, count))

    def finish(self):
        drain(*self.programs)


class Copies:
    def __init__(self, sems):
        self.sems, self.made = sems, []

    def start(self, source, target):
        slot = len(self.made)

        def copy():
            return pltpu.make_async_copy(source(), target(), self.sems.at[slot])

        copy().start()
        self.made.append(copy)
        return slot

    def wait(self, *slots):
        for slot in slots:
            self.made[slot]().wait()
            self.made[slot] = None

    def finish(self):
        self.wait(*[slot for slot, copy in enumerate(self.made) if copy])


def chunk_of(i, size):
    return pl.ds(pl.multiple_of(i * size, size), size)


def turned(values, cosine, sine):
    lane = lax.rem(lax.broadcasted_iota(jnp.int32, (1, 128), 1), HEAD_DIM)
    swapped = jnp.where(lane < ROT // 2, -pltpu.roll(values, 128 - ROT // 2, 1), pltpu.roll(values, ROT // 2, 1))
    return values * cosine + swapped * sine


def cut_rows(ref, a, b):
    step = ref.shape[0] // 4
    return ref.at[pl.ds(step * a, step * (b - a)), :]


def rows_scatter(group, part_ref, out, arriving, hold, sems):
    cs, cr, send, recv = sems
    core, partner = group.core, other_core(group)

    def exchange():
        return remote(part_ref.at[1 - core], arriving, (cs, cr), 0, partner)

    exchange().start()
    yield
    exchange().wait()

    def one(i, carry):
        rows = pl.ds(pl.multiple_of(i * 32, 32), 32)
        arriving[rows, :] = (arriving[rows, :].astype(F32) + part_ref[core, rows, :].astype(F32)).astype(BF16)
        return carry

    lax.fori_loop(0, arriving.shape[0] // 32, one, 0)
    width, size = out.shape[1], out.shape[0] // 2

    def cut(ref, a, b):
        return ref.at[pl.ds(size * (a - 2), size * (b - a)), :]

    def part(step, flip, a, b):
        columns = pl.ds(pl.multiple_of(group.member(step, flip) * width, width), width)
        return arriving.at[pl.ds(size * (a - 2), size * (b - a)), columns]

    def result(a, b, refs):
        target = cut(out, a, b)
        target[...] = total_of(refs)

    yield from scatter(group, part, cut, hold, result, (send, recv), pair_first=False)


def peers(axis):
    ctx, fsdp = lax.axis_index("ctx"), lax.axis_index("fsdp")
    count = lax.axis_size(axis)
    if axis == "ctx":
        return [(lax.rem(ctx + offset, count), fsdp) for offset in range(1, count)]
    return [(ctx, lax.rem(fsdp + offset, count)) for offset in range(1, count)]


def sum_small(x_ref, out, hold, sems, devices):
    def copy(i):
        return remote(x_ref, hold.at[i], sems, i, devices[i])

    for i in range(len(devices)):
        copy(i).start()
    yield
    total = x_ref[...]
    for i in range(len(devices)):
        copy(i).wait_recv()
        total = total + hold[i]
    out[...] = total
    for i in range(len(devices)):
        copy(i).wait_send()


def reduce_one(group, source, target, hold, sems):
    rs, rr, gs, gr, cs, cr, ls = sems
    core, partner = group.core, other_core(group)
    rows, width = source.shape[0] // 8, source.shape[1]
    by_rows = rows % 64 == 0

    def quarters(ref, a, b):
        if by_rows:
            return ref.at[pl.ds(rows // 4 * a, rows // 4 * (b - a)), :]
        return ref.at[:, pl.ds(width // 4 * a, width // 4 * (b - a))]

    def part(step, flip, a, b):
        return quarters(source.at[chunk_of(group.member(step, flip), rows), :], a, b)

    def view(member, a, b):
        return quarters(target(core).at[chunk_of(member, rows), :], a, b)

    def own(a, b):
        return quarters(hold.at[HOLD - 1], a, b)

    def result(a, b, terms):
        place = own(a, b)
        place[...] = total_of(terms).astype(BF16)

    def keep():
        return pltpu.make_async_copy(own(0, 4), view(group.me, 0, 4), ls.at[0])

    copies = []

    def arrived(block, a, b):
        slot = len(copies)

        def copy():
            ref = view(group.member(*block), a, b)
            return remote(own(a, b) if block == (0, 0) else ref, ref, (cs, cr), slot, partner)

        copy().start()
        copies.append(copy)

    yield from scatter(group, part, quarters, hold, result, (rs, rr))
    keep().start()
    yield from gather(group, view, (gs, gr), arrived, own=own)
    yield
    keep().wait()
    for copy in copies:
        copy().wait()


def reduce_scratch(shape):
    return pltpu.VMEM((HOLD, shape[0] // 8, shape[1]), BF16)


def reduce_sems():
    return pairs(SCATTER_SLOTS) + pairs(GATHER_SLOTS) + pairs(GATHER_SLOTS + 1) + [pltpu.SemaphoreType.DMA((1,))]


STATES = 11


def state_of(j):
    late = lax.div(j + 7, 16)
    return j * (1 - late) + (9 + lax.rem(j, 2)) * late


FORWARD_PLAN = ((2, 1), (5, 1), (6, 1), (10, 1), (13, 1), (15, 1), (16, 1))
BACKWARD_PLAN = ((1, 1), (3, 1), (8, 3), (13, 2), (15, 2))
BRANCH_PLAN = ((2, 1), (5, 1), (8, 1), (12, 1))


def layer_kernel(
    order_ref, ids_ref, x_ref, dy_ref, gain_ref, shift_ref, bq_ref, bk_ref, bv_ref, bo_ref, bi_ref, bu_ref, wq, wk, wv, wo, wi, wu,
    layer_out, input_out, vec_out, q_out, kv_out, out_out, inner_out, outer_out,
    x_all, dy_all, normed, qkv_w, o_w, i_w, u_w, kv_all, inner, act, grad, ff, ffn, inner_part, outer_part,
    cos_ref, sin_ref, q_ref, cotangent_ref, begin_ref, unit_ref, inv_ref, inner_sum, slot_of,
    state_max, state_sum, state_acc, dkv_items, lse_ref, delta_ref, att_ref, dq_ref,
    arriving, branch_hold, sum_ref, arriving_back, back_hold, local_ref, inner_hold, outer_hold, q_hold, kv_hold, out_hold, keys_hold, own, pre,
    stats, stats_hold, stats_sum, vec, vec_hold,
    *sems,
):
    across, along = Group("ctx"), Group("fsdp")
    core, chip, fsdp, partner = across.core, across.me, along.me, other_core(across)
    rows, width = dy_ref.shape
    sems = list(sems)

    def sems_for(count):
        taken = sems[:count]
        del sems[:count]
        return taken

    xs, ds, ks, cs = sems_for(2), sems_for(2), sems_for(2), sems_for(2)
    copies = Copies(sems_for(1)[0])
    x_cuts = (0, 96, 192, 288, x_all.shape[0])

    def x_view(member, a, b):
        return x_all.at[pl.ds(x_cuts[a], x_cuts[b] - x_cuts[a]), chunk_of(member, width)]

    def dy_view(member, a, b):
        return dy_all.at[core, pl.ds(rows // 2 * (a - 2), rows // 2 * (b - a)), chunk_of(member, width)]

    copies.start(lambda: x_ref, lambda: x_all.at[pl.ds(0, rows), chunk_of(fsdp, width)])
    copies.start(lambda: dy_ref, lambda: dy_view(fsdp, 2, 4))
    for i, ref in enumerate((wq, wk, wv)):
        copies.start(lambda ref=ref: ref.at[:, chunk_of(core, 128)], lambda i=i: qkv_w.at[:, pl.ds(128 * i, 128)])
    copies.start(lambda: wi.at[:, chunk_of(core, 512)], lambda: i_w)
    copies.start(lambda: wu.at[chunk_of(core, 512), :], lambda: u_w)
    copies.start(lambda: wo.at[chunk_of(core, 128), :], lambda: o_w)
    extra = jnp.concatenate([gain_ref[...], shift_ref[...], jnp.zeros((14, width), BF16)], axis=0)
    x_all[rows:, chunk_of(fsdp, width)] = extra
    barrier(peers("ctx") + peers("fsdp"))
    copies.wait(0, 1)
    x_steps = Steps(gather(along, x_view, xs))
    x_steps.take()
    dy_steps = Steps(gather(along, dy_view, ds, slots=PAIR_ONLY))
    dy_steps.take()

    lane = lax.rem(lax.broadcasted_iota(jnp.int32, (1, 128), 1), HEAD_DIM)
    left = lax.broadcasted_iota(jnp.int32, (1, 128), 1) < HEAD_DIM
    freqs = jnp.zeros((1, 128), F32)
    for i in range(ROT):
        freqs = jnp.where(lane == i, 10000.0 ** (-2.0 * (i % (ROT // 2)) / ROT), freqs)
    for slot in range(4):
        group = order_ref[chip * 4 + slot]
        position = (group * GROUP + lax.broadcasted_iota(jnp.int32, (GROUP, 128), 0)).astype(F32)
        angles = position * freqs
        place = slice(GROUP * slot, GROUP * slot + GROUP)
        cos_ref[place, :] = jnp.cos(angles)
        sin_ref[place, :] = jnp.sin(angles)
        column = lax.broadcasted_iota(jnp.int32, (1, TILE), 1)
        column = group * GROUP + jnp.where(column < GROUP, column, column - GROUP)
        begin = jnp.zeros((1, TILE), jnp.int32)
        for doc in range(1, DOCS):
            before = jnp.sum(jnp.where(ids_ref[...] < doc, 1, 0), axis=0, keepdims=True)
            before = jnp.sum(before, axis=1, keepdims=True)
            begin = jnp.where(before <= column, before, begin)
        begin_ref[slot] = begin

    def find(group, carry):
        place = 0
        for slot in range(1, GROUPS):
            apart = order_ref[slot] - group
            place = place + slot * (1 - jnp.minimum(apart * apart, 1))
        slot_of[group] = jnp.minimum(place, GROUPS - 1)
        return carry

    lax.fori_loop(0, GROUPS, find, 0)

    x_steps.finish()
    gain, shift = x_all[rows : rows + 1, :].astype(F32), x_all[rows + 1 : rows + 2, :].astype(F32)

    def exchange(ref, i):
        half = ref.at[core, pl.ds(GROUP * i, GROUP), :]
        return remote(half, half, cs, 2 * (ref is dy_all) + i, partner)

    def norm(i, carry):
        place = chunk_of(i, 32)
        values = x_all[place, :].astype(F32)
        mean = jnp.mean(values, axis=1, keepdims=True)
        centered = values - mean
        inv = lax.rsqrt(jnp.mean(centered * centered, axis=1, keepdims=True) + EPS)
        normed[core, place, :] = (centered * inv * gain + shift).astype(BF16)
        unit_ref[place, :] = (x_all[place, chunk_of(fsdp, width)].astype(F32) - mean) * inv
        inv_ref[place, :] = inv
        return carry

    for i in range(2):
        lax.fori_loop(GROUP // 32 * i, GROUP // 32 * (i + 1), norm, 0)
        exchange(normed, i).start()
    copies.wait(2, 3, 4)
    dy_steps.take(2)

    def project(i, carry):
        slot = lax.rem(2 * core + i, 4)
        place = chunk_of(slot, GROUP)
        pre_rows = dot(normed[lax.div(slot, 2), chunk_of(lax.rem(slot, 2), GROUP), :], qkv_w[...])
        bias = [ref[:, chunk_of(core, 128)].astype(F32) for ref in (bq_ref, bk_ref, bv_ref)]
        cosine, sine = cos_ref[place, :], sin_ref[place, :]
        queries = turned(pre_rows[:, :128] + bias[0], cosine, sine).astype(BF16)
        q_ref[slot] = (queries.astype(F32) * HEAD_DIM ** (-0.5)).astype(BF16)
        kv_all[4 * chip + slot, :, :128] = turned(pre_rows[:, 128:256] + bias[1], cosine, sine).astype(BF16)
        kv_all[4 * chip + slot, :, 128:] = (pre_rows[:, 256:] + bias[2]).astype(BF16)
        return carry

    lax.fori_loop(0, 2, project, 0)
    for i in range(2):
        exchange(normed, i).wait()
    lax.fori_loop(2, 4, project, 0)

    def kv_view(member, a, b):
        return kv_all.at[pl.ds(4 * member + a, b - a)]

    kv_steps = Steps(gather(across, kv_view, ks))
    kv_steps.take()
    dy_steps.take(2)
    copies.wait(5, 6, 7)

    def four_by_four(one):
        def loop(i, carry):
            slot, j = lax.div(i, 4), lax.rem(i, 4)
            one(lax.div(slot, 2), chunk_of(lax.rem(slot, 2), GROUP), chunk_of(slot, GROUP), chunk_of(j, 512))
            return carry

        lax.fori_loop(0, 16, loop, 0)

    inner_bias = bi_ref[:, chunk_of(core, 512)].astype(F32)

    def feed(slot, carry):
        place = chunk_of(slot, GROUP)
        value = dot(normed[lax.div(slot, 2), chunk_of(lax.rem(slot, 2), GROUP), :], i_w[...]) + inner_bias
        inner[place, :] = value
        curve = jnp.tanh(GELU_A * (value + GELU_B * value * value * value))
        act[place, :] = (0.5 * value * (1.0 + curve)).astype(BF16)
        return carry

    lax.fori_loop(0, 4, feed, 0)
    dy_steps.take(2)
    kv_steps.take(3)

    def feed_out(of, part, place, columns):
        ff[of, part, columns] = dot(act[place, :], u_w[:, columns]).astype(BF16)

    four_by_four(feed_out)
    dy_steps.finish()
    for i in range(2):
        exchange(dy_all, i).start()
    kv_steps.take(2)
    inner_sum[...] = jnp.zeros_like(inner_sum)

    def gradients(i, carry):
        slot = lax.rem(2 * core + i, 4)
        place = chunk_of(slot, GROUP)
        dy_rows = dy_all[lax.div(slot, 2), chunk_of(lax.rem(slot, 2), GROUP), :]
        cotangent_ref[slot] = dot(dy_rows, o_w[...], NT).astype(BF16)
        value = inner[place, :]
        square = value * value
        curve = jnp.tanh(GELU_A * (value + GELU_B * square * value))
        slope = 0.5 * (1.0 + curve) + 0.5 * value * (1.0 - curve * curve) * (GELU_A * (1.0 + 3.0 * GELU_B * square))
        out = (dot(dy_rows, u_w[...], NT) * slope).astype(BF16)
        grad[place, :] = out
        inner_sum[...] += jnp.sum(out.astype(F32), axis=0, keepdims=True)
        return carry

    lax.fori_loop(0, 2, gradients, 0)
    for i in range(2):
        exchange(dy_all, i).wait()
    lax.fori_loop(2, 4, gradients, 0)
    kv_steps.take(2)

    def outer_weights(i, carry):
        block = chunk_of(i, 256)
        outer_part[:, block] = dot(act[...], dy_all[:, :, block].reshape(2 * rows, 256), TN).astype(BF16)
        return carry

    lax.fori_loop(0, 8, outer_weights, 0)
    outer_program = reduce_one(across, outer_part, lambda c: outer_out.at[c], outer_hold, sems_for(7))
    inner_program = reduce_one(across, inner_part, lambda c: inner_out.at[:, chunk_of(c, 512)], inner_hold, sems_for(7))
    kv_steps.take(2)

    def inner_weights(i, carry):
        block = chunk_of(i, 256)
        inner_part[block, :] = dot(normed[:, :, block].reshape(2 * rows, 256), grad[...], TN).astype(BF16)
        return carry

    lax.fori_loop(0, 8, inner_weights, 0)
    kv_steps.take(2)

    def feed_back(of, part, place, columns):
        ffn[of, part, columns] = dot(grad[place, :], i_w[columns, :], NT).astype(BF16)

    four_by_four(feed_back)
    kv_steps.finish()
    weights_steps = Steps(outer_program, inner_program)
    weights_steps.take()

    def bit(number):
        return jnp.minimum(jnp.maximum(number, 0), 1)

    def pair_facts(p):
        g0, g1 = order_ref[4 * chip + 2 * p], order_ref[4 * chip + 2 * p + 1]
        low, high = jnp.minimum(g0, g1), jnp.maximum(g0, g1)
        return low, high, bit(g0 - g1), lax.div(low, 2) + 1

    key_row = lax.broadcasted_iota(jnp.int32, (TILE, TILE), 0)
    column = lax.broadcasted_iota(jnp.int32, (1, TILE), 1)
    query_row = jnp.where(column < GROUP, column, column - GROUP)

    def item_facts(p, j):
        low, high, low_slot, count = pair_facts(p)
        second = bit(j - count + 1)
        tile = second * TILES + (1 - second) * (count - 1) - j
        slot = 2 * p + second * (1 - low_slot) + (1 - second) * low_slot
        position = (second * high + (1 - second) * low) * GROUP
        last = query_row + (position - tile * TILE)
        begin = begin_ref[slot] - tile * TILE
        allowed = (key_row <= last) & (key_row >= begin)
        keep = bit(j * (j - count) * (j - count)).astype(F32)
        return tile, slot, allowed, keep

    def keys_of(tile, lanes):
        return jnp.concatenate([kv_all[slot_of[2 * tile], :, lanes], kv_all[slot_of[2 * tile + 1], :, lanes]], axis=0)

    def stacked(rows):
        zero = jnp.zeros_like(rows)
        return jnp.concatenate([jnp.where(left, rows, zero), jnp.where(left, zero, rows)], axis=0)

    def unstacked(columns):
        rows = columns.T
        return jnp.where(left, rows[:GROUP], rows[GROUP:])

    def final_item(p, i):
        low, high, low_slot, count = pair_facts(p)
        is_low = low_slot if i else 1 - low_slot
        return count * is_low + 10 * (1 - is_low)

    for p in range(2):
        state_max[p, 0] = jnp.full((1, TILE), FLOOR, F32)
        state_sum[p, 0] = jnp.zeros((1, TILE), F32)
        state_acc[p, 0] = jnp.zeros((128, TILE), F32)

    def forward(j, carry):
        weights_steps.at(j, FORWARD_PLAN)
        now, after = state_of(j), state_of(j + 1)
        for p in range(2):
            tile, slot, allowed, keep = item_facts(p, j)
            scores = jnp.where(allowed, dot(keys_of(tile, KEYS), stacked(q_ref[slot]), NT), MASKED)
            old_max = state_max[p, now] * keep + FLOOR * (1.0 - keep)
            new_max = jnp.maximum(old_max, jnp.max(scores, axis=0, keepdims=True))
            weights = jnp.exp(scores - new_max)
            factor = jnp.exp(old_max - new_max)
            state_max[p, after] = new_max
            state_sum[p, after] = state_sum[p, now] * factor + jnp.sum(weights, axis=0, keepdims=True)
            state_acc[p, after] = state_acc[p, now] * factor + dot(keys_of(tile, VALUES), weights.astype(BF16), TN)
        return carry

    lax.fori_loop(0, ITEMS, forward, 0)

    for p in range(2):
        for i in range(2):
            item = final_item(p, i)
            slot = 2 * p + i
            total = state_sum[p, item]
            out = state_acc[p, item] / total
            lse_ref[slot] = state_max[p, item] + jnp.log(total)
            cotangent = stacked(cotangent_ref[slot].astype(F32)).T
            delta_ref[slot] = jnp.sum(cotangent * out, axis=0, keepdims=True)
            att_ref[slot] = unstacked(out).astype(BF16)

    def branches(of, part, place, columns):
        attended = att_ref[2 * of + lax.div(place.start - of * rows, GROUP)]
        ff[of, part, columns] = (ff[of, part, columns].astype(F32) + dot(attended, o_w[:, columns])).astype(BF16)

    four_by_four(branches)
    branch_steps = Steps(rows_scatter(along, ff, sum_ref, arriving, branch_hold, sems_for(4)))
    branch_steps.take()

    for p in range(2):
        state_acc[p, 0] = jnp.zeros((128, TILE), F32)

    def backward(j, carry):
        weights_steps.at(j, BACKWARD_PLAN)
        branch_steps.at(j, BRANCH_PLAN)
        now, after = state_of(j), state_of(j + 1)
        for p in range(2):
            tile, slot, allowed, keep = item_facts(p, j)
            queries, cotangent = stacked(q_ref[slot]), stacked(cotangent_ref[slot])
            scores = dot(keys_of(tile, KEYS), queries, NT)
            probs = jnp.where(allowed, jnp.exp(scores - lse_ref[slot]), 0.0)
            prob_grad = dot(keys_of(tile, VALUES), cotangent, NT)
            score_grad = (probs * (prob_grad - delta_ref[slot])).astype(BF16)
            state_acc[p, after] = state_acc[p, now] * keep + dot(keys_of(tile, KEYS), score_grad, TN)
            key_grad = dot(score_grad, queries).astype(BF16)
            value_grad = dot(probs.astype(BF16), cotangent).astype(BF16)
            for half in range(2):
                rows = slice(GROUP * half, GROUP * half + GROUP)
                dkv_items[p, j, half, :, :128] = key_grad[rows]
                dkv_items[p, j, half, :, 128:] = value_grad[rows]
        return carry

    lax.fori_loop(0, ITEMS, backward, 0)

    for p in range(2):
        for i in range(2):
            dq_ref[2 * p + i] = unstacked(state_acc[p, final_item(p, i)])

    counts = [pair_facts(p)[3] for p in range(2)]

    def collect(s, carry):
        group = order_ref[s]
        tile, half = lax.div(group, 2), lax.rem(group, 2)
        total = jnp.zeros((GROUP, 256), F32)
        for p in range(2):
            low_item = dkv_items[p, jnp.maximum(counts[p] - 1 - tile, 0), half].astype(F32)
            high_item = dkv_items[p, jnp.maximum(TILES - tile, counts[p]), half].astype(F32)
            total = total + low_item * bit(counts[p] - tile).astype(F32)
            total = total + high_item * bit(TILES - tile - counts[p] + 1).astype(F32)
        kv_all[s] = total.astype(BF16)
        return carry

    lax.fori_loop(0, GROUPS, collect, 0)

    def part(step, flip, a, b):
        return kv_all.at[pl.ds(4 * across.member(step, flip) + a, b - a)]

    def cut_groups(ref, a, b):
        return ref.at[pl.ds(a, b - a)]

    def result(a, b, refs):
        own[a:b] = total_of(refs)

    keys_steps = Steps(scatter(across, part, cut_groups, keys_hold, result, sems_for(2)))
    keys_steps.take()
    branch_steps.finish()
    layer_sum = x_all[:rows, chunk_of(fsdp, width)].astype(F32) + sum_ref[...]
    layer_out[...] = (layer_sum + bo_ref[...].astype(F32) + bu_ref[...].astype(F32)).astype(BF16)
    for slot in range(4):
        place = slice(GROUP * slot, GROUP * slot + GROUP)
        turned_back = turned(dq_ref[slot] * HEAD_DIM ** (-0.5), cos_ref[place, :], -sin_ref[place, :])
        pre[place, :128] = turned_back.astype(BF16)
    weights_steps.finish()
    q_part, kv_part = inner_part.at[:, pl.ds(0, 128)], inner_part.at[:, pl.ds(128, 256)]
    out_part = outer_part.at[pl.ds(0, 128), :]

    def query_weights(i, carry):
        block = chunk_of(i, 256)
        q_part[block, :] = dot(normed[:, :, block].reshape(2 * rows, 256), pre[:, :128], TN).astype(BF16)
        return carry

    lax.fori_loop(0, 8, query_weights, 0)

    def out_weights(i, carry):
        block = chunk_of(i, 256)
        attended = att_ref[...].reshape(2 * rows, 128)
        out_part[:, block] = dot(attended, dy_all[:, :, block].reshape(2 * rows, 256), TN).astype(BF16)
        return carry

    lax.fori_loop(0, 8, out_weights, 0)
    keys_steps.finish()
    for slot in range(4):
        place = slice(GROUP * slot, GROUP * slot + GROUP)
        turned_back = turned(own[slot, :, :128], cos_ref[place, :], -sin_ref[place, :])
        pre[place, 128:256] = turned_back.astype(BF16)
        pre[place, 256:] = own[slot, :, 128:].astype(BF16)

    def key_weights(i, carry):
        block = chunk_of(i, 256)
        kv_part[block, :] = dot(normed[:, :, block].reshape(2 * rows, 256), pre[:, 128:], TN).astype(BF16)
        return carry

    lax.fori_loop(0, 8, key_weights, 0)
    last_steps = Steps(
        reduce_one(across, kv_part, lambda c: kv_out.at[c], kv_hold, sems_for(7)),
        reduce_one(across, q_part, lambda c: q_out.at[c], q_hold, sems_for(7)),
        reduce_one(across, out_part, lambda c: out_out.at[c], out_hold, sems_for(7)),
    )
    last_steps.take()

    def normed_grad(of):
        def one(i, carry):
            part_rows, columns = chunk_of(lax.div(i, 4), GROUP), chunk_of(lax.rem(i, 4), 512)
            from_rows = chunk_of(2 * of + lax.div(i, 4), GROUP)
            total = ffn[of, part_rows, columns].astype(F32) + dot(pre[from_rows, :], qkv_w[columns, :], NT)
            ffn[of, part_rows, columns] = total.astype(BF16)
            return carry

        lax.fori_loop(0, 8, one, 0)

    normed_grad(1 - core)
    rows_steps = Steps(rows_scatter(along, ffn, local_ref, arriving_back, back_hold, sems_for(4)))
    rows_steps.take()
    normed_grad(core)
    for count in (1, 2, 1, 2, 2):
        rows_steps.take()
        last_steps.take(count)
    rows_steps.finish()

    whole = local_ref[...]
    unit = unit_ref[...]
    scaled = whole * gain_ref[...].astype(F32)
    lane = lax.broadcasted_iota(jnp.int32, (1, 128), 1)
    first = jnp.sum(scaled, axis=1, keepdims=True)
    second = jnp.sum(scaled * unit, axis=1, keepdims=True)
    stats[...] = jnp.where(lane == 0, first, jnp.where(lane == 1, second, 0.0)).T[:8]
    stats_steps = Steps(sum_small(stats, stats_sum, stats_hold, sems_for(2), peers("fsdp")))
    stats_steps.take()
    cotangent = dy_all[core, :, chunk_of(fsdp, width)].astype(F32)
    vec[...] = jnp.zeros_like(vec)
    vec[0:1, :] = jnp.sum(whole * unit, axis=0, keepdims=True)
    vec[1:2, :] = jnp.sum(whole, axis=0, keepdims=True)
    vec[2:3, :] = jnp.sum(cotangent, axis=0, keepdims=True)
    for i in range(3):
        vec[3 + i : 4 + i, chunk_of(core, 128)] = jnp.sum(pre[:, 128 * i : 128 * i + 128].astype(F32), axis=0, keepdims=True)
    for i in range(2):
        vec[pl.ds(6 + 2 * core + i, 1), :] = inner_sum[:, 256 * i : 256 * i + 256]
    vec_steps = Steps(sum_small(vec, vec_out, vec_hold, sems_for(2), peers("ctx")))
    vec_steps.take()
    last_steps.take(2)
    stats_steps.finish()
    back = jnp.concatenate([stats_sum[...], jnp.zeros((120, rows), F32)], axis=0).T * (1.0 / 2048)
    input_out[...] = cotangent + inv_ref[...] * (scaled - back[:, 0:1] - unit * back[:, 1:2])
    vec_steps.finish()
    last_steps.finish()
    assert not sems


def layer(order, ids, x, dy, vectors, weights):
    rows, width = dy.shape
    wide, both = weights[0].shape[0], 2 * rows

    def bf(*shape):
        return pltpu.VMEM(shape, BF16)

    def f32(*shape):
        return pltpu.VMEM(shape, F32)

    def of(kind, *shape):
        return jax.ShapeDtypeStruct(shape, kind)

    return pl.pallas_call(
        layer_kernel,
        out_shape=[
            of(BF16, rows, width),
            of(F32, rows, width),
            of(F32, 16, width),
            of(BF16, 2, wide, 128),
            of(BF16, 2, wide, 256),
            of(BF16, 2, 128, wide),
            of(BF16, wide, 1024),
            of(BF16, 2, 512, wide),
        ],
        in_specs=[SMEM, VMEM, ANY, ANY] + [VMEM] * len(vectors) + [ANY] * len(weights),
        out_specs=[VMEM] * 3 + [ANY] * 5,
        scratch_shapes=[
            bf(rows + 16, wide),
            bf(2, rows, wide),
            bf(2, rows, wide),
            bf(wide, 384),
            bf(128, wide),
            bf(wide, 512),
            bf(512, wide),
            bf(GROUPS, GROUP, 256),
            f32(both, 512),
            bf(both, 512),
            bf(both, 512),
            bf(2, rows, wide),
            bf(2, rows, wide),
            bf(wide, 512),
            bf(512, wide),
            f32(both, 128),
            f32(both, 128),
            bf(4, GROUP, 128),
            bf(4, GROUP, 128),
            pltpu.VMEM((4, 1, TILE), jnp.int32),
            f32(rows, width),
            f32(rows, 1),
            f32(1, 512),
            pltpu.SMEM((GROUPS,), jnp.int32),
            f32(2, STATES, 1, TILE),
            f32(2, STATES, 1, TILE),
            f32(2, STATES, 128, TILE),
            bf(2, ITEMS, 2, GROUP, 256),
            f32(4, 1, TILE),
            f32(4, 1, TILE),
            bf(4, GROUP, 128),
            f32(4, GROUP, 128),
            bf(rows, wide),
            bf(HOLD, rows, width),
            f32(rows, width),
            bf(rows, wide),
            bf(HOLD, rows, width),
            f32(rows, width),
            reduce_scratch((wide, 512)),
            reduce_scratch((512, wide)),
            reduce_scratch((wide, 128)),
            reduce_scratch((wide, 256)),
            reduce_scratch((128, wide)),
            bf(HOLD, 4, GROUP, 256),
            f32(4, GROUP, 256),
            bf(both, 384),
            f32(8, rows),
            f32(7, 8, rows),
            f32(8, rows),
            f32(16, width),
            f32(15, 16, width),
        ]
        + pairs(GATHER_SLOTS) * 3
        + pairs(4)
        + [pltpu.SemaphoreType.DMA((8,))]
        + reduce_sems() * 2
        + pairs(1)
        + pairs(SCATTER_SLOTS)
        + pairs(SCATTER_SLOTS)
        + reduce_sems() * 3
        + pairs(1)
        + pairs(SCATTER_SLOTS)
        + pairs(7)
        + pairs(15),
        compiler_params=params(0, 63),
        name="layer",
    )(order, ids, x, dy, *vectors, *weights)


def body(
    layer_input,
    norm_gain,
    norm_bias,
    query_weight,
    query_bias,
    key_weight,
    key_bias,
    value_weight,
    value_bias,
    out_weight,
    out_bias,
    inner_weight,
    inner_bias,
    outer_weight,
    outer_bias,
    output_grad,
    group_order,
    sequence_ids,
):
    def row(vector):
        return vector.reshape(1, -1)

    layer_output, input_grad, vectors, query_grad, kv_grad, out_grad, inner_w_grad, outer_w_grad = layer(
        group_order,
        sequence_ids.reshape(-1, 128),
        layer_input,
        output_grad,
        [row(v) for v in (norm_gain, norm_bias, query_bias, key_bias, value_bias, out_bias, inner_bias, outer_bias)],
        [query_weight, key_weight, value_weight, out_weight, inner_weight, outer_weight],
    )

    def side_by_side(array):
        return jnp.concatenate([array[0], array[1]], axis=1).astype(F32)

    return (
        layer_output,
        input_grad,
        vectors[0],
        vectors[1],
        side_by_side(query_grad),
        vectors[3],
        side_by_side(kv_grad[:, :, :128]),
        vectors[4],
        side_by_side(kv_grad[:, :, 128:]),
        vectors[5],
        out_grad.reshape(256, 2048).astype(F32),
        vectors[2],
        inner_w_grad.astype(F32),
        vectors[6:10].reshape(1024),
        outer_w_grad.reshape(1024, 2048).astype(F32),
        vectors[2],
    )


def solution(mesh):
    in_specs = (
        P("ctx", "fsdp"),
        P("fsdp"),
        P("fsdp"),
        P(None, "fsdp"),
        P("fsdp"),
        P(None, "fsdp"),
        P("fsdp"),
        P(None, "fsdp"),
        P("fsdp"),
        P("fsdp", None),
        P("fsdp"),
        P(None, "fsdp"),
        P("fsdp"),
        P("fsdp", None),
        P("fsdp"),
        P("ctx", "fsdp"),
        P(),
        P(),
    )
    out_specs = (
        P("ctx", "fsdp"),
        P("ctx", "fsdp"),
        P("fsdp"),
        P("fsdp"),
        P(None, "fsdp"),
        P("fsdp"),
        P(None, "fsdp"),
        P("fsdp"),
        P(None, "fsdp"),
        P("fsdp"),
        P("fsdp", None),
        P("fsdp"),
        P(None, "fsdp"),
        P("fsdp"),
        P("fsdp", None),
        P("fsdp"),
    )
    return jax.shard_map(body, mesh=mesh, in_specs=in_specs, out_specs=out_specs, check_vma=False)
```

```python
from functools import partial

import jax
import jax.numpy as jnp
from jax import lax
from jax.experimental import pallas as pl
from jax.experimental.pallas import tpu as pltpu
from jax.sharding import PartitionSpec as P

HEAD_DIM = 64
ROT = 32
GROUP = 192
GROUPS = 32
SEQ_LEN = 6144
DOCS = 5
EPS = 1e-05
MASKED = -1e30
FLOOR = -1e29
GELU_A = 0.7978845608028654
GELU_B = 0.044715
MESH = pl.DeviceIdType.MESH
BF16 = jnp.bfloat16
F32 = jnp.float32
ANY = pl.BlockSpec(memory_space=pl.ANY)
VMEM = pl.BlockSpec(memory_space=pltpu.VMEM)
SMEM = pl.BlockSpec(memory_space=pltpu.SMEM)
MIB = 2**20


class Group:
    def __init__(self, axis):
        ctx, fsdp = lax.axis_index("ctx"), lax.axis_index("fsdp")
        self.axis, self.ctx, self.fsdp = axis, ctx, fsdp
        self.core = lax.rem(ctx, 2)
        self.me = lax.div(ctx, 2) if axis == "ctx" else fsdp
        self.ring, self.pair = lax.rem(self.me, 4), lax.div(self.me, 4)

    def member(self, step, flip):
        pair = 1 - self.pair if flip else self.pair
        return pair * 4 + lax.rem(self.ring + (step + 4), 4)

    def device(self, step, flip):
        member = self.member(step, flip)
        if self.axis == "ctx":
            return (member * 2 + self.core, self.fsdp)
        return (self.ctx, member)

    def neighbours(self):
        return [self.device(1, 0), self.device(-1, 0), self.device(0, 1)]


def other_core(group):
    return (group.ctx + 1 - 2 * group.core, group.fsdp)


def barrier(devices):
    semaphore = pltpu.get_barrier_semaphore()
    for device in devices:
        pl.semaphore_signal(semaphore, inc=1, device_id=device, device_id_type=MESH)
    pl.semaphore_wait(semaphore, len(devices))


def remote(source, target, sems, slot, device):
    return pltpu.make_async_remote_copy(
        src_ref=source,
        dst_ref=target,
        send_sem=sems[0].at[slot],
        recv_sem=sems[1].at[slot],
        device_id=device,
        device_id_type=MESH,
    )


GATHER = (
    (1, 0, (0, 0), 0, 2, None),
    (-1, 0, (0, 0), 0, 2, None),
    (0, 1, (0, 0), 2, 4, None),
    (1, 0, (0, 0), 2, 4, None),
    (-1, 0, (0, 0), 2, 4, None),
    (0, 1, (0, 0), 0, 2, None),
    (1, 0, (-1, 0), 0, 1, 0),
    (-1, 0, (1, 0), 1, 2, 1),
    (0, 1, (-1, 0), 0, 2, 0),
    (0, 1, (1, 0), 0, 2, 1),
    (0, 1, (2, 0), 0, 1, 6),
    (0, 1, (2, 0), 1, 2, 7),
    (1, 0, (0, 1), 2, 4, 2),
    (-1, 0, (0, 1), 2, 4, 2),
    (1, 0, (-1, 0), 2, 3, 3),
    (-1, 0, (1, 0), 3, 4, 4),
    (1, 0, (-1, 1), 2, 3, 12),
    (-1, 0, (1, 1), 3, 4, 13),
)
GATHER_ORDER = (0, 1, 2, 3, 4, 6, 7, 12, 13, 5, 8, 14, 15, 9, 10, 16, 17, 11)
GATHER_SLOTS = len(GATHER)


def gather(group, view, sems, arrived=None, own=None):
    started = []

    def start(slot):
        step, flip, block, a, b, _ = GATHER[slot]

        def copy():
            ref = view(group.member(*block), a, b)
            source = own(a, b) if own and block == (0, 0) else ref
            return remote(source, ref, sems, slot, group.device(step, flip))

        copy().start()
        started.append(copy)

    for slot in range(GATHER_SLOTS):
        if GATHER[slot][5] is None:
            start(slot)
    if arrived:
        arrived((0, 0), 0, 4)
    for slot in GATHER_ORDER:
        step, flip, block, a, b, _ = GATHER[slot]
        yield
        source = (block[0] - step, block[1] ^ flip)
        ref = view(group.member(*source), a, b)
        remote(ref, ref, sems, slot, group.device(step, flip)).wait_recv()
        for later in range(GATHER_SLOTS):
            if GATHER[later][5] == slot:
                start(later)
        if arrived:
            arrived(source, a, b)
    for copy in started:
        copy().wait_send()


SCATTER_SLOTS = 23
HOLD = 7


def add_into(target, *sources):
    total = target[...].astype(F32)
    for source in sources:
        total = total + source[...].astype(F32)
    target[...] = total.astype(target.dtype)


def scatter(group, part, quarters, hold, result, sems, pair_first=True):
    started = []

    def held(k, a, b):
        return quarters(hold.at[k], a, b)

    def start(slot, source, step, flip, k, a, b):
        def copy():
            return remote(source(), held(k, a, b), sems, slot, group.device(step, flip))

        copy().start()
        started.append(copy)

    def send_part(slot, block, step, flip, k, a, b):
        start(slot, lambda: part(*block, a, b), step, flip, k, a, b)

    def send_held(slot, source, step, flip, k, a, b):
        start(slot, lambda: held(source, a, b), step, flip, k, a, b)

    def wait(slot, k, a, b):
        ref = held(k, a, b)
        remote(ref, ref, sems, slot, group.device(0, 1)).wait_recv()

    if pair_first:
        send_part(0, (2, 1), 0, 1, 0, 0, 2)
    send_part(10, (2, 1), 1, 0, 0, 2, 3)
    send_part(11, (2, 1), -1, 0, 0, 3, 4)
    if pair_first:
        send_part(1, (1, 1), 0, 1, 1, 0, 2)
        send_part(2, (-1, 1), 0, 1, 2, 0, 2)
    send_part(16, (2, 0), 1, 0, 3, 2, 3)
    send_part(17, (2, 0), -1, 0, 3, 3, 4)
    send_part(12, (1, 1), 1, 0, 1, 3, 4)
    send_part(13, (-1, 1), -1, 0, 2, 2, 3)
    send_part(18, (1, 0), 1, 0, 4, 3, 4)
    send_part(19, (-1, 0), -1, 0, 5, 2, 3)
    if pair_first:
        send_part(3, (0, 1), 0, 1, 3, 0, 2)
    yield
    wait(10, 0, 2, 3)
    add_into(held(0, 2, 3), part(1, 1, 2, 3))
    send_held(14, 0, 1, 0, 1, 2, 3)
    wait(11, 0, 3, 4)
    add_into(held(0, 3, 4), part(-1, 1, 3, 4))
    send_held(15, 0, -1, 0, 2, 3, 4)
    if pair_first:
        yield
        wait(0, 0, 0, 2)
        add_into(held(0, 0, 2), part(2, 0, 0, 2))
        send_held(4, 0, 1, 0, 4, 0, 1)
        send_held(5, 0, -1, 0, 4, 1, 2)
    yield
    wait(16, 3, 2, 3)
    add_into(held(3, 2, 3), part(1, 0, 2, 3))
    send_held(20, 3, 1, 0, 4, 2, 3)
    wait(17, 3, 3, 4)
    add_into(held(3, 3, 4), part(-1, 0, 3, 4))
    send_held(21, 3, -1, 0, 5, 3, 4)
    if pair_first:
        yield
        wait(1, 1, 0, 2)
        add_into(held(1, 0, 2), part(1, 0, 0, 2))
        send_held(6, 1, 1, 0, 5, 1, 2)
    yield
    wait(12, 1, 3, 4)
    wait(14, 1, 2, 3)
    wait(13, 2, 2, 3)
    wait(15, 2, 3, 4)
    add_into(held(1, 2, 4), held(2, 2, 4), part(0, 1, 2, 4))
    send_held(22, 1, 0, 1, 6, 2, 4)
    if pair_first:
        yield
        wait(2, 2, 0, 2)
        add_into(held(2, 0, 2), part(-1, 0, 0, 2))
        send_held(8, 2, -1, 0, 6, 0, 1)
        yield
        wait(4, 4, 0, 1)
        add_into(held(1, 0, 1), held(4, 0, 1))
        send_held(7, 1, 1, 0, 5, 0, 1)
        wait(5, 4, 1, 2)
        add_into(held(2, 1, 2), held(4, 1, 2))
        send_held(9, 2, -1, 0, 6, 1, 2)
        yield
        wait(3, 3, 0, 2)
        wait(6, 5, 1, 2)
        wait(8, 6, 0, 1)
        wait(7, 5, 0, 1)
        wait(9, 6, 1, 2)
        result(0, 2, [part(0, 0, 0, 2), held(3, 0, 2), held(5, 0, 2), held(6, 0, 2)])
    yield
    wait(18, 4, 3, 4)
    wait(20, 4, 2, 3)
    wait(19, 5, 2, 3)
    wait(21, 5, 3, 4)
    wait(22, 6, 2, 4)
    result(2, 4, [part(0, 0, 2, 4), held(4, 2, 4), held(5, 2, 4), held(6, 2, 4)])
    for copy in started:
        copy().wait_send()


def total_of(refs):
    total = refs[0][...].astype(F32)
    for ref in refs[1:]:
        total = total + ref[...].astype(F32)
    return total


def drain(*programs):
    programs = list(programs)
    while programs:
        programs = [p for p in programs if next(p, "end") != "end"]


def pairs(count):
    return [pltpu.SemaphoreType.DMA((count,)), pltpu.SemaphoreType.DMA((count,))]


def params(collective_id, mib):
    return pltpu.CompilerParams(
        collective_id=collective_id, has_side_effects=True, vmem_limit_bytes=mib * MIB
    )


ROW_CUTS = (0, 96, 192, 288, 400)


TILE = 2 * GROUP
TILES = SEQ_LEN // TILE
ITEMS = TILES + 1
KEYS, VALUES = slice(0, 128), slice(128, 256)
NT = (((1,), (1,)), ((), ()))
TN = (((0,), (0,)), ((), ()))


def dot(a, b, dims=(((1,), (0,)), ((), ()))):
    return lax.dot_general(a, b, dims, preferred_element_type=F32)


class Steps:
    def __init__(self, *programs):
        self.programs = list(programs)

    def take(self, count=1):
        for _ in range(count):
            self.programs = [p for p in self.programs if next(p, "end") != "end"]

    def at(self, j, plan):
        for iteration, count in plan:
            pl.when(j == iteration)(partial(self.take, count))

    def finish(self):
        drain(*self.programs)


class Copies:
    def __init__(self, sems):
        self.sems, self.made = sems, []

    def start(self, source, target):
        slot = len(self.made)

        def copy():
            return pltpu.make_async_copy(source(), target(), self.sems.at[slot])

        copy().start()
        self.made.append(copy)
        return slot

    def wait(self, *slots):
        for slot in slots:
            self.made[slot]().wait()
            self.made[slot] = None

    def finish(self):
        self.wait(*[slot for slot, copy in enumerate(self.made) if copy])


def chunk_of(i, size):
    return pl.ds(pl.multiple_of(i * size, size), size)


def turned(values, cosine, sine):
    lane = lax.rem(lax.broadcasted_iota(jnp.int32, (1, 128), 1), HEAD_DIM)
    swapped = jnp.where(lane < ROT // 2, -pltpu.roll(values, 128 - ROT // 2, 1), pltpu.roll(values, ROT // 2, 1))
    return values * cosine + swapped * sine


def cut_rows(ref, a, b):
    step = ref.shape[0] // 4
    return ref.at[pl.ds(step * a, step * (b - a)), :]


def rows_scatter(group, part_ref, out, arriving, hold, sems):
    cs, cr, send, recv = sems
    core, partner = group.core, other_core(group)

    def exchange():
        return remote(part_ref.at[1 - core], arriving, (cs, cr), 0, partner)

    exchange().start()
    yield
    exchange().wait()

    def one(i, carry):
        rows = pl.ds(pl.multiple_of(i * 32, 32), 32)
        arriving[rows, :] = (arriving[rows, :].astype(F32) + part_ref[core, rows, :].astype(F32)).astype(BF16)
        return carry

    lax.fori_loop(0, arriving.shape[0] // 32, one, 0)
    width, size = out.shape[1], out.shape[0] // 2

    def cut(ref, a, b):
        return ref.at[pl.ds(size * (a - 2), size * (b - a)), :]

    def part(step, flip, a, b):
        columns = pl.ds(pl.multiple_of(group.member(step, flip) * width, width), width)
        return arriving.at[pl.ds(size * (a - 2), size * (b - a)), columns]

    def result(a, b, refs):
        target = cut(out, a, b)
        target[...] = total_of(refs)

    yield from scatter(group, part, cut, hold, result, (send, recv), pair_first=False)


def peers(axis):
    ctx, fsdp = lax.axis_index("ctx"), lax.axis_index("fsdp")
    count = lax.axis_size(axis)
    if axis == "ctx":
        return [(lax.rem(ctx + offset, count), fsdp) for offset in range(1, count)]
    return [(ctx, lax.rem(fsdp + offset, count)) for offset in range(1, count)]


def sum_small(x_ref, out, hold, sems, devices):
    def copy(i):
        return remote(x_ref, hold.at[i], sems, i, devices[i])

    for i in range(len(devices)):
        copy(i).start()
    yield
    total = x_ref[...]
    for i in range(len(devices)):
        copy(i).wait_recv()
        total = total + hold[i]
    out[...] = total
    for i in range(len(devices)):
        copy(i).wait_send()


def reduce_one(group, source, target, hold, sems):
    rs, rr, gs, gr, cs, cr, ls = sems
    core, partner = group.core, other_core(group)
    rows, width = source.shape[0] // 8, source.shape[1]
    by_rows = rows % 64 == 0

    def quarters(ref, a, b):
        if by_rows:
            return ref.at[pl.ds(rows // 4 * a, rows // 4 * (b - a)), :]
        return ref.at[:, pl.ds(width // 4 * a, width // 4 * (b - a))]

    def part(step, flip, a, b):
        return quarters(source.at[chunk_of(group.member(step, flip), rows), :], a, b)

    def view(member, a, b):
        return quarters(target(core).at[chunk_of(member, rows), :], a, b)

    def own(a, b):
        return quarters(hold.at[HOLD - 1], a, b)

    def result(a, b, terms):
        place = own(a, b)
        place[...] = total_of(terms).astype(BF16)

    def keep():
        return pltpu.make_async_copy(own(0, 4), view(group.me, 0, 4), ls.at[0])

    copies = []

    def arrived(block, a, b):
        slot = len(copies)

        def copy():
            ref = view(group.member(*block), a, b)
            return remote(own(a, b) if block == (0, 0) else ref, ref, (cs, cr), slot, partner)

        copy().start()
        copies.append(copy)

    yield from scatter(group, part, quarters, hold, result, (rs, rr))
    keep().start()
    yield from gather(group, view, (gs, gr), arrived, own=own)
    yield
    keep().wait()
    for copy in copies:
        copy().wait()


def reduce_scratch(shape):
    return pltpu.VMEM((HOLD, shape[0] // 8, shape[1]), BF16)


def reduce_sems():
    return pairs(SCATTER_SLOTS) + pairs(GATHER_SLOTS) + pairs(GATHER_SLOTS + 1) + [pltpu.SemaphoreType.DMA((1,))]


STATES = 11


def state_of(j):
    late = lax.div(j + 7, 16)
    return j * (1 - late) + (9 + lax.rem(j, 2)) * late


FORWARD_PLAN = ((1, 1), (3, 1), (4, 1), (8, 1), (11, 1), (13, 1), (14, 1))
BACKWARD_PLAN = ((0, 1), (2, 1), (8, 3), (12, 2), (14, 2), (16, 2))
BRANCH_PLAN = ((2, 1), (5, 1), (8, 1), (12, 1))
OUT_PLAN = ((4, 2), (6, 2), (9, 2), (11, 1), (13, 2), (15, 5))
ROWS, LAST, EARLY, WEIGHTS, OUT = range(5)
TAIL_PLAN = (
    (ROWS, 1), (EARLY, 3), (EARLY, 2), (LAST, 3), (EARLY, 2), (LAST, 1), (ROWS, 1), (LAST, 1), (EARLY, 1), (LAST, 2), (ROWS, 1), (EARLY, 1),
    (LAST, 2), (ROWS, 1), (EARLY, 5), (LAST, 5), (EARLY, 4), (LAST, 4), (ROWS, 1),
)


def layer_kernel(
    order_ref, ids_ref, x_ref, dy_ref, vectors_ref, wq, wk, wv, wo, wi, wu,
    layer_out, input_out, vec_out, q_out, k_out, v_out, out_out, inner_out, outer_out,
    x_all, dy_all, normed, qkv_w, o_w, i_w, u_w, kv_all, inner, act, act_t, grad, ff, ffn, inner_part, outer_part, out_part,
    cos_ref, sin_ref, q_ref, cotangent_ref, begin_ref, unit_ref, inv_ref, inner_sum, slot_of,
    state_max, state_sum, state_acc, dkv_items, lse_ref, delta_ref, att_ref, dq_ref,
    arriving, branch_hold, sum_ref, arriving_back, back_hold, local_ref, inner_hold, outer_hold, q_hold, k_hold, v_hold, out_hold, keys_hold, own, pre,
    stats, stats_hold, stats_sum, vec, vec_hold,
    *sems,
):
    across, along = Group("ctx"), Group("fsdp")
    core, chip, fsdp, partner = across.core, across.me, along.me, other_core(across)
    rows, width = dy_ref.shape
    sems = list(sems)

    def sems_for(count):
        taken = sems[:count]
        del sems[:count]
        return taken

    xs, ds, ks, cs = sems_for(2), sems_for(2), sems_for(2), sems_for(2)
    copies = Copies(sems_for(1)[0])
    x_cuts = (0, 96, 192, 288, x_all.shape[0])

    def x_view(member, a, b):
        return x_all.at[pl.ds(x_cuts[a], x_cuts[b] - x_cuts[a]), chunk_of(member, width)]

    def dy_view(member, a, b):
        return dy_all.at[core, pl.ds(rows // 4 * a, rows // 4 * (b - a)), chunk_of(member, width)]

    copies.start(lambda: x_ref, lambda: x_all.at[pl.ds(0, rows), chunk_of(fsdp, width)])
    copies.start(lambda: dy_ref, lambda: dy_view(fsdp, 0, 4))
    for i, ref in enumerate((wq, wk, wv)):
        copies.start(lambda ref=ref: ref.at[:, chunk_of(core, 128)], lambda i=i: qkv_w.at[:, pl.ds(128 * i, 128)])
    copies.start(lambda: wi.at[:, chunk_of(core, 512)], lambda: i_w)
    copies.start(lambda: wu.at[chunk_of(core, 512), :], lambda: u_w)
    copies.start(lambda: wo.at[chunk_of(core, 128), :], lambda: o_w)
    def vector(i):
        return vectors_ref[:, 256 * i : 256 * i + 256]

    extra = jnp.concatenate([vector(0), vector(1), jnp.zeros((14, width), F32)], axis=0)
    x_all[rows:, chunk_of(fsdp, width)] = extra.astype(BF16)
    barrier(peers("ctx") + peers("fsdp"))
    copies.wait(0, 1)
    x_steps = Steps(gather(along, x_view, xs))
    x_steps.take()
    dy_steps = Steps(gather(along, dy_view, ds))

    lane = lax.rem(lax.broadcasted_iota(jnp.int32, (1, 128), 1), HEAD_DIM)
    left = lax.broadcasted_iota(jnp.int32, (1, 128), 1) < HEAD_DIM
    freqs = jnp.zeros((1, 128), F32)
    for i in range(ROT):
        freqs = jnp.where(lane == i, 10000.0 ** (-2.0 * (i % (ROT // 2)) / ROT), freqs)
    for slot in range(4):
        group = order_ref[chip * 4 + slot]
        position = (group * GROUP + lax.broadcasted_iota(jnp.int32, (GROUP, 128), 0)).astype(F32)
        angles = position * freqs
        place = slice(GROUP * slot, GROUP * slot + GROUP)
        cos_ref[place, :] = jnp.cos(angles)
        sin_ref[place, :] = jnp.sin(angles)
        column = lax.broadcasted_iota(jnp.int32, (1, TILE), 1)
        column = group * GROUP + jnp.where(column < GROUP, column, column - GROUP)
        begin = jnp.zeros((1, TILE), jnp.int32)
        for doc in range(1, DOCS):
            before = jnp.sum(jnp.where(ids_ref[...] < doc, 1, 0), axis=0, keepdims=True)
            before = jnp.sum(before, axis=1, keepdims=True)
            begin = jnp.where(before <= column, before, begin)
        begin_ref[slot] = begin

    def find(group, carry):
        place = 0
        for slot in range(1, GROUPS):
            apart = order_ref[slot] - group
            place = place + slot * (1 - jnp.minimum(apart * apart, 1))
        slot_of[group] = jnp.minimum(place, GROUPS - 1)
        return carry

    lax.fori_loop(0, GROUPS, find, 0)

    x_steps.take(9)
    dy_steps.take()
    x_steps.finish()
    gain, shift = x_all[rows : rows + 1, :].astype(F32), x_all[rows + 1 : rows + 2, :].astype(F32)

    def exchange(ref, i):
        half = ref.at[core, pl.ds(GROUP * i, GROUP), :]
        return remote(half, half, cs, 2 * (ref is dy_all) + i, partner)

    def norm(i, carry):
        place = chunk_of(i, 32)
        values = x_all[place, :].astype(F32)
        mean = jnp.mean(values, axis=1, keepdims=True)
        centered = values - mean
        inv = lax.rsqrt(jnp.mean(centered * centered, axis=1, keepdims=True) + EPS)
        normed[core, place, :] = (centered * inv * gain + shift).astype(BF16)
        unit_ref[place, :] = (x_all[place, chunk_of(fsdp, width)].astype(F32) - mean) * inv
        inv_ref[place, :] = inv
        return carry

    for i in range(2):
        lax.fori_loop(GROUP // 32 * i, GROUP // 32 * (i + 1), norm, 0)
        exchange(normed, i).start()
    copies.wait(2, 3, 4)
    dy_steps.take(3)

    def project(of):
        pre_rows = dot(normed[of], qkv_w[...])
        bias = [vectors_ref[:, pl.ds(pl.multiple_of(512 + 256 * i + 128 * core, 128), 128)] for i in range(3)]
        for half in range(2):
            slot, part_rows = 2 * of + half, slice(GROUP * half, GROUP * half + GROUP)
            cosine, sine = cos_ref[chunk_of(slot, GROUP), :], sin_ref[chunk_of(slot, GROUP), :]
            queries = turned(pre_rows[part_rows, :128] + bias[0], cosine, sine).astype(BF16)
            q_ref[slot] = (queries.astype(F32) * HEAD_DIM ** (-0.5)).astype(BF16)
            kv_all[4 * chip + slot, :, :128] = turned(pre_rows[part_rows, 128:256] + bias[1], cosine, sine).astype(BF16)
            kv_all[4 * chip + slot, :, 128:] = (pre_rows[part_rows, 256:] + bias[2]).astype(BF16)

    def both_cores(one, ref):
        def here():
            for i in range(2):
                exchange(ref, i).wait()

        def loop(i, carry):
            pl.when(i == 1)(here)
            one(lax.rem(core + i, 2))
            return carry

        lax.fori_loop(0, 2, loop, 0)

    both_cores(project, normed)

    def kv_view(member, a, b):
        return kv_all.at[pl.ds(4 * member + a, b - a)]

    kv_steps = Steps(gather(across, kv_view, ks))
    kv_steps.take()
    dy_steps.take(6)
    copies.wait(5, 6, 7)

    inner_bias = vectors_ref[:, pl.ds(pl.multiple_of(1792 + 512 * core, 128), 512)]

    def feed(of, carry):
        value = dot(normed[of], i_w[...]) + inner_bias
        inner[chunk_of(of, rows), :] = value
        curve = jnp.tanh(GELU_A * (value + GELU_B * value * value * value))
        act[chunk_of(of, rows), :] = (0.5 * value * (1.0 + curve)).astype(BF16)
        return carry

    lax.fori_loop(0, 2, feed, 0)
    dy_steps.take(4)
    kv_steps.take(3)

    def feed_out(i, carry):
        block = chunk_of(i, 256)
        ff[:, :, block] = dot(act[...], u_w[:, block]).astype(BF16).reshape(2, rows, 256)
        return carry

    lax.fori_loop(0, 8, feed_out, 0)
    act_t[...] = act[...].T
    dy_steps.finish()
    for i in range(2):
        exchange(dy_all, i).start()
    kv_steps.take(2)
    inner_sum[...] = jnp.zeros_like(inner_sum)

    def gradients(of):
        dy_rows = dy_all[of]
        ag = dot(dy_rows, o_w[...], NT).astype(BF16)
        cotangent_ref[2 * of], cotangent_ref[2 * of + 1] = ag[:GROUP], ag[GROUP:]
        value = inner[chunk_of(of, rows), :]
        square = value * value
        curve = jnp.tanh(GELU_A * (value + GELU_B * square * value))
        slope = 0.5 * (1.0 + curve) + 0.5 * value * (1.0 - curve * curve) * (GELU_A * (1.0 + 3.0 * GELU_B * square))
        out = (dot(dy_rows, u_w[...], NT) * slope).astype(BF16)
        grad[chunk_of(of, rows), :] = out
        inner_sum[...] += jnp.sum(out.astype(F32), axis=0, keepdims=True)

    both_cores(gradients, dy_all)
    kv_steps.take(2)

    def outer_weights(i, carry):
        block = chunk_of(i, 256)
        outer_part[:, block] = dot(act_t[...], dy_all[:, :, block].reshape(2 * rows, 256)).astype(BF16)
        return carry

    lax.fori_loop(0, 8, outer_weights, 0)
    outer_program = reduce_one(across, outer_part, lambda c: outer_out.at[c], outer_hold, sems_for(7))
    inner_program = reduce_one(across, inner_part, lambda c: inner_out.at[:, chunk_of(c, 512)], inner_hold, sems_for(7))
    kv_steps.take(2)
    next(outer_program)

    def inner_weights(i, carry):
        block = chunk_of(i, 256)
        inner_part[block, :] = dot(normed[:, :, block].reshape(2 * rows, 256), grad[...], TN).astype(BF16)
        return carry

    lax.fori_loop(0, 8, inner_weights, 0)
    kv_steps.take(2)
    next(inner_program)

    kv_steps.finish()
    weights_steps = Steps(outer_program, inner_program)

    def bit(number):
        return jnp.minimum(jnp.maximum(number, 0), 1)

    def pair_facts(p):
        g0, g1 = order_ref[4 * chip + 2 * p], order_ref[4 * chip + 2 * p + 1]
        low, high = jnp.minimum(g0, g1), jnp.maximum(g0, g1)
        return low, high, bit(g0 - g1), lax.div(low, 2) + 1

    key_row = lax.broadcasted_iota(jnp.int32, (TILE, TILE), 0)
    column = lax.broadcasted_iota(jnp.int32, (1, TILE), 1)
    query_row = jnp.where(column < GROUP, column, column - GROUP)

    def item_facts(p, j):
        low, high, low_slot, count = pair_facts(p)
        second = bit(j - count + 1)
        tile = second * TILES + (1 - second) * (count - 1) - j
        slot = 2 * p + second * (1 - low_slot) + (1 - second) * low_slot
        position = (second * high + (1 - second) * low) * GROUP
        last = query_row + (position - tile * TILE)
        begin = begin_ref[slot] - tile * TILE
        allowed = (key_row <= last) & (key_row >= begin)
        keep = bit(j * (j - count) * (j - count)).astype(F32)
        return tile, slot, allowed, keep

    def keys_of(tile, lanes):
        return jnp.concatenate([kv_all[slot_of[2 * tile], :, lanes], kv_all[slot_of[2 * tile + 1], :, lanes]], axis=0)

    def stacked(rows):
        zero = jnp.zeros_like(rows)
        return jnp.concatenate([jnp.where(left, rows, zero), jnp.where(left, zero, rows)], axis=0)

    def unstacked(columns):
        rows = columns.T
        return jnp.where(left, rows[:GROUP], rows[GROUP:])

    def final_item(p, i):
        low, high, low_slot, count = pair_facts(p)
        is_low = low_slot if i else 1 - low_slot
        return count * is_low + 10 * (1 - is_low)

    for p in range(2):
        state_max[p, 0] = jnp.full((1, TILE), FLOOR, F32)
        state_sum[p, 0] = jnp.zeros((1, TILE), F32)
        state_acc[p, 0] = jnp.zeros((128, TILE), F32)

    def forward(j, carry):
        weights_steps.at(j, FORWARD_PLAN)
        now, after = state_of(j), state_of(j + 1)
        for p in range(2):
            tile, slot, allowed, keep = item_facts(p, j)
            scores = jnp.where(allowed, dot(keys_of(tile, KEYS), stacked(q_ref[slot]), NT), MASKED)
            old_max = state_max[p, now] * keep + FLOOR * (1.0 - keep)
            new_max = jnp.maximum(old_max, jnp.max(scores, axis=0, keepdims=True))
            weights = jnp.exp(scores - new_max)
            factor = jnp.exp(old_max - new_max)
            state_max[p, after] = new_max
            state_sum[p, after] = state_sum[p, now] * factor + jnp.sum(weights, axis=0, keepdims=True)
            state_acc[p, after] = state_acc[p, now] * factor + dot(keys_of(tile, VALUES), weights.astype(BF16), TN)
        return carry

    lax.fori_loop(0, ITEMS, forward, 0)

    for p in range(2):
        for i in range(2):
            item = final_item(p, i)
            slot = 2 * p + i
            total = state_sum[p, item]
            out = state_acc[p, item] / total
            lse_ref[slot] = state_max[p, item] + jnp.log(total)
            cotangent = stacked(cotangent_ref[slot].astype(F32)).T
            delta_ref[slot] = jnp.sum(cotangent * out, axis=0, keepdims=True)
            att_ref[slot] = unstacked(out).astype(BF16)

    def branches(i, carry):
        block = chunk_of(i, 256)
        attended = dot(att_ref[...].reshape(2 * rows, 128), o_w[:, block]).reshape(2, rows, 256)
        ff[:, :, block] = (ff[:, :, block].astype(F32) + attended).astype(BF16)
        return carry

    lax.fori_loop(0, 8, branches, 0)
    branch_steps = Steps(rows_scatter(along, ff, sum_ref, arriving, branch_hold, sems_for(4)))
    branch_steps.take()

    def out_weights(i, carry):
        block = chunk_of(i, 256)
        out_part[:, block] = dot(att_ref[...].reshape(2 * rows, 128), dy_all[:, :, block].reshape(2 * rows, 256), TN).astype(BF16)
        return carry

    lax.fori_loop(0, 8, out_weights, 0)
    out_steps = Steps(reduce_one(across, out_part, lambda c: out_out.at[c], out_hold, sems_for(7)))
    out_steps.take()

    for p in range(2):
        state_acc[p, 0] = jnp.zeros((128, TILE), F32)

    def backward(j, carry):
        weights_steps.at(j, BACKWARD_PLAN)
        branch_steps.at(j, BRANCH_PLAN)
        out_steps.at(j, OUT_PLAN)
        now, after = state_of(j), state_of(j + 1)
        for p in range(2):
            tile, slot, allowed, keep = item_facts(p, j)
            queries, cotangent = stacked(q_ref[slot]), stacked(cotangent_ref[slot])
            scores = dot(keys_of(tile, KEYS), queries, NT)
            probs = jnp.where(allowed, jnp.exp(scores - lse_ref[slot]), 0.0)
            prob_grad = dot(keys_of(tile, VALUES), cotangent, NT)
            score_grad = (probs * (prob_grad - delta_ref[slot])).astype(BF16)
            state_acc[p, after] = state_acc[p, now] * keep + dot(keys_of(tile, KEYS), score_grad, TN)
            key_grad = dot(score_grad, queries).astype(BF16)
            value_grad = dot(probs.astype(BF16), cotangent).astype(BF16)
            for half in range(2):
                rows = slice(GROUP * half, GROUP * half + GROUP)
                dkv_items[p, j, half, :, :128] = key_grad[rows]
                dkv_items[p, j, half, :, 128:] = value_grad[rows]
        return carry

    lax.fori_loop(0, ITEMS, backward, 0)

    for p in range(2):
        for i in range(2):
            dq_ref[2 * p + i] = unstacked(state_acc[p, final_item(p, i)])

    counts = [pair_facts(p)[3] for p in range(2)]

    def collect(s, carry):
        group = order_ref[s]
        tile, half = lax.div(group, 2), lax.rem(group, 2)
        total = jnp.zeros((GROUP, 256), F32)
        for p in range(2):
            low_item = dkv_items[p, jnp.maximum(counts[p] - 1 - tile, 0), half].astype(F32)
            high_item = dkv_items[p, jnp.maximum(TILES - tile, counts[p]), half].astype(F32)
            total = total + low_item * bit(counts[p] - tile).astype(F32)
            total = total + high_item * bit(TILES - tile - counts[p] + 1).astype(F32)
        kv_all[s] = total.astype(BF16)
        return carry

    lax.fori_loop(0, GROUPS, collect, 0)

    def part(step, flip, a, b):
        return kv_all.at[pl.ds(4 * across.member(step, flip) + a, b - a)]

    def cut_groups(ref, a, b):
        return ref.at[pl.ds(a, b - a)]

    def result(a, b, refs):
        own[a:b] = total_of(refs)

    keys_steps = Steps(scatter(across, part, cut_groups, keys_hold, result, sems_for(2)))
    keys_steps.take()
    branch_steps.finish()
    layer_sum = x_all[:rows, chunk_of(fsdp, width)].astype(F32) + sum_ref[...]
    layer_out[...] = (layer_sum + vector(5) + vector(6)).astype(BF16)
    for slot in range(4):
        place = slice(GROUP * slot, GROUP * slot + GROUP)
        turned_back = turned(dq_ref[slot] * HEAD_DIM ** (-0.5), cos_ref[place, :], -sin_ref[place, :])
        pre[place, :128] = turned_back.astype(BF16)
    q_part, k_part, v_part = [inner_part.at[:, pl.ds(128 * i, 128)] for i in range(3)]

    def query_weights(i, carry):
        block = chunk_of(i, 256)
        q_part[block, :] = dot(normed[:, :, block].reshape(2 * rows, 256), pre[:, :128], TN).astype(BF16)
        return carry

    lax.fori_loop(0, 8, query_weights, 0)
    keys_steps.take()

    early_steps = Steps(reduce_one(across, q_part, lambda c: q_out.at[:, chunk_of(c, 128)], q_hold, sems_for(7)))
    keys_steps.take()
    early_steps.take()
    def feed_back(i, carry):
        block = chunk_of(i, 256)
        ffn[:, :, block] = dot(grad[...], i_w[block, :], NT).astype(BF16).reshape(2, rows, 256)
        return carry

    lax.fori_loop(0, 8, feed_back, 0)
    weights_steps.take(2)
    keys_steps.take(2)
    weights_steps.take(2)
    keys_steps.take(2)
    weights_steps.take(2)
    keys_steps.finish()
    for slot in range(4):
        place = slice(GROUP * slot, GROUP * slot + GROUP)
        turned_back = turned(own[slot, :, :128], cos_ref[place, :], -sin_ref[place, :])
        pre[place, 128:256] = turned_back.astype(BF16)
        pre[place, 256:] = own[slot, :, 128:].astype(BF16)

    def key_weights(i, carry):
        block = chunk_of(i, 256)
        total = dot(normed[:, :, block].reshape(2 * rows, 256), pre[:, 128:], TN).astype(BF16)
        k_part[block, :] = total[:, :128]
        v_part[block, :] = total[:, 128:]
        return carry

    def normed_grad(of):
        def one(i, carry):
            part_rows, columns = chunk_of(lax.div(i, 4), GROUP), chunk_of(lax.rem(i, 4), 512)
            from_rows = chunk_of(2 * of + lax.div(i, 4), GROUP)
            total = ffn[of, part_rows, columns].astype(F32) + dot(pre[from_rows, :], qkv_w[columns, :], NT)
            ffn[of, part_rows, columns] = total.astype(BF16)
            return carry

        lax.fori_loop(0, 8, one, 0)

    normed_grad(1 - core)
    rows_steps = Steps(rows_scatter(along, ffn, local_ref, arriving_back, back_hold, sems_for(4)))
    rows_steps.take()
    lax.fori_loop(0, 8, key_weights, 0)
    last_steps = Steps(
        reduce_one(across, k_part, lambda c: k_out.at[:, chunk_of(c, 128)], k_hold, sems_for(7)),
        reduce_one(across, v_part, lambda c: v_out.at[:, chunk_of(c, 128)], v_hold, sems_for(7)),
    )
    last_steps.take()
    normed_grad(core)
    for programs, count in TAIL_PLAN:
        (rows_steps, last_steps, early_steps, weights_steps, out_steps)[programs].take(count)
    rows_steps.finish()

    whole = local_ref[...]
    unit = unit_ref[...]
    scaled = whole * vector(0)
    lane = lax.broadcasted_iota(jnp.int32, (1, 128), 1)
    first = jnp.sum(scaled, axis=1, keepdims=True)
    second = jnp.sum(scaled * unit, axis=1, keepdims=True)
    stats[...] = jnp.where(lane == 0, first, jnp.where(lane == 1, second, 0.0)).T[:8]
    stats_steps = Steps(sum_small(stats, stats_sum, stats_hold, sems_for(2), peers("fsdp")))
    stats_steps.take()
    cotangent = dy_all[core, :, chunk_of(fsdp, width)].astype(F32)
    vec[...] = jnp.zeros_like(vec)
    vec[0:1, :] = jnp.sum(whole * unit, axis=0, keepdims=True)
    vec[1:2, :] = jnp.sum(whole, axis=0, keepdims=True)
    vec[2:3, :] = jnp.sum(cotangent, axis=0, keepdims=True)
    for i in range(3):
        vec[3 + i : 4 + i, chunk_of(core, 128)] = jnp.sum(pre[:, 128 * i : 128 * i + 128].astype(F32), axis=0, keepdims=True)
    for i in range(2):
        vec[pl.ds(6 + 2 * core + i, 1), :] = inner_sum[:, 256 * i : 256 * i + 256]
    vec_steps = Steps(sum_small(vec, vec_out, vec_hold, sems_for(2), peers("ctx")))
    vec_steps.take()
    early_steps.take(9)
    weights_steps.finish()
    out_steps.finish()
    stats_steps.finish()
    back = jnp.concatenate([stats_sum[...], jnp.zeros((120, rows), F32)], axis=0).T * (1.0 / 2048)
    input_out[...] = cotangent + inv_ref[...] * (scaled - back[:, 0:1] - unit * back[:, 1:2])
    vec_steps.finish()
    weights_steps.finish()
    early_steps.finish()
    last_steps.finish()
    assert not sems


def layer(order, ids, x, dy, vectors, weights):
    rows, width = dy.shape
    wide, both = weights[0].shape[0], 2 * rows

    def bf(*shape):
        return pltpu.VMEM(shape, BF16)

    def f32(*shape):
        return pltpu.VMEM(shape, F32)

    def of(kind, *shape):
        return jax.ShapeDtypeStruct(shape, kind)

    return pl.pallas_call(
        layer_kernel,
        out_shape=[
            of(BF16, rows, width),
            of(F32, rows, width),
            of(F32, 16, width),
            of(BF16, wide, width),
            of(BF16, wide, width),
            of(BF16, wide, width),
            of(BF16, 2, 128, wide),
            of(BF16, wide, 1024),
            of(BF16, 2, 512, wide),
        ],
        in_specs=[SMEM, VMEM, ANY, ANY, VMEM] + [ANY] * len(weights),
        out_specs=[VMEM] * 3 + [ANY] * 6,
        scratch_shapes=[
            bf(rows + 16, wide),
            bf(2, rows, wide),
            bf(2, rows, wide),
            bf(wide, 384),
            bf(128, wide),
            bf(wide, 512),
            bf(512, wide),
            bf(GROUPS, GROUP, 256),
            f32(both, 512),
            bf(both, 512),
            bf(512, both),
            bf(both, 512),
            bf(2, rows, wide),
            bf(2, rows, wide),
            bf(wide, 512),
            bf(512, wide),
            bf(128, wide),
            f32(both, 128),
            f32(both, 128),
            bf(4, GROUP, 128),
            bf(4, GROUP, 128),
            pltpu.VMEM((4, 1, TILE), jnp.int32),
            f32(rows, width),
            f32(rows, 1),
            f32(1, 512),
            pltpu.SMEM((GROUPS,), jnp.int32),
            f32(2, STATES, 1, TILE),
            f32(2, STATES, 1, TILE),
            f32(2, STATES, 128, TILE),
            bf(2, ITEMS, 2, GROUP, 256),
            f32(4, 1, TILE),
            f32(4, 1, TILE),
            bf(4, GROUP, 128),
            f32(4, GROUP, 128),
            bf(rows, wide),
            bf(HOLD, rows, width),
            f32(rows, width),
            bf(rows, wide),
            bf(HOLD, rows, width),
            f32(rows, width),
            reduce_scratch((wide, 512)),
            reduce_scratch((512, wide)),
            reduce_scratch((wide, 128)),
            reduce_scratch((wide, 128)),
            reduce_scratch((wide, 128)),
            reduce_scratch((128, wide)),
            bf(HOLD, 4, GROUP, 256),
            f32(4, GROUP, 256),
            bf(both, 384),
            f32(8, rows),
            f32(7, 8, rows),
            f32(8, rows),
            f32(16, width),
            f32(15, 16, width),
        ]
        + pairs(GATHER_SLOTS) * 3
        + pairs(4)
        + [pltpu.SemaphoreType.DMA((8,))]
        + reduce_sems() * 2
        + pairs(1)
        + pairs(SCATTER_SLOTS)
        + reduce_sems()
        + pairs(SCATTER_SLOTS)
        + reduce_sems()
        + pairs(1)
        + pairs(SCATTER_SLOTS)
        + reduce_sems() * 2
        + pairs(7)
        + pairs(15),
        compiler_params=params(0, 63),
        name="layer",
    )(order, ids, x, dy, vectors, *weights)


def body(
    layer_input,
    norm_gain,
    norm_bias,
    query_weight,
    query_bias,
    key_weight,
    key_bias,
    value_weight,
    value_bias,
    out_weight,
    out_bias,
    inner_weight,
    inner_bias,
    outer_weight,
    outer_bias,
    output_grad,
    group_order,
    sequence_ids,
):
    layer_output, input_grad, vectors, query_grad, key_grad, value_grad, out_grad, inner_w_grad, outer_w_grad = layer(
        group_order,
        sequence_ids.reshape(-1, 128),
        layer_input,
        output_grad,
        jnp.concatenate([norm_gain, norm_bias, query_bias, key_bias, value_bias, out_bias, outer_bias, inner_bias]).astype(F32)[None],
        [query_weight, key_weight, value_weight, out_weight, inner_weight, outer_weight],
    )

    return (
        layer_output,
        input_grad,
        vectors[0],
        vectors[1],
        query_grad.astype(F32),
        vectors[3],
        key_grad.astype(F32),
        vectors[4],
        value_grad.astype(F32),
        vectors[5],
        out_grad.reshape(256, 2048).astype(F32),
        vectors[2],
        inner_w_grad.astype(F32),
        vectors[6:10].reshape(1024),
        outer_w_grad.reshape(1024, 2048).astype(F32),
        vectors[2],
    )


def solution(mesh):
    in_specs = (
        P("ctx", "fsdp"),
        P("fsdp"),
        P("fsdp"),
        P(None, "fsdp"),
        P("fsdp"),
        P(None, "fsdp"),
        P("fsdp"),
        P(None, "fsdp"),
        P("fsdp"),
        P("fsdp", None),
        P("fsdp"),
        P(None, "fsdp"),
        P("fsdp"),
        P("fsdp", None),
        P("fsdp"),
        P("ctx", "fsdp"),
        P(),
        P(),
    )
    out_specs = (
        P("ctx", "fsdp"),
        P("ctx", "fsdp"),
        P("fsdp"),
        P("fsdp"),
        P(None, "fsdp"),
        P("fsdp"),
        P(None, "fsdp"),
        P("fsdp"),
        P(None, "fsdp"),
        P("fsdp"),
        P("fsdp", None),
        P("fsdp"),
        P(None, "fsdp"),
        P("fsdp"),
        P("fsdp", None),
        P("fsdp"),
    )
    return jax.shard_map(body, mesh=mesh, in_specs=in_specs, out_specs=out_specs, check_vma=False)
```

```python
from functools import partial

import jax
import jax.numpy as jnp
from jax import lax
from jax.experimental import pallas as pl
from jax.experimental.pallas import tpu as pltpu
from jax.sharding import PartitionSpec as P

HEAD_DIM = 64
ROT = 32
GROUP = 192
GROUPS = 32
SEQ_LEN = 6144
DOCS = 5
EPS = 1e-05
MASKED = -1e30
FLOOR = -1e29
GELU_A = 0.7978845608028654
GELU_B = 0.044715
MESH = pl.DeviceIdType.MESH
BF16 = jnp.bfloat16
F32 = jnp.float32
ANY = pl.BlockSpec(memory_space=pl.ANY)
VMEM = pl.BlockSpec(memory_space=pltpu.VMEM)
SMEM = pl.BlockSpec(memory_space=pltpu.SMEM)
MIB = 2**20


class Group:
    def __init__(self, axis):
        ctx, fsdp = lax.axis_index("ctx"), lax.axis_index("fsdp")
        self.axis, self.ctx, self.fsdp = axis, ctx, fsdp
        self.core = lax.rem(ctx, 2)
        self.me = lax.div(ctx, 2) if axis == "ctx" else fsdp
        self.ring, self.pair = lax.rem(self.me, 4), lax.div(self.me, 4)

    def member(self, step, flip):
        pair = 1 - self.pair if flip else self.pair
        return pair * 4 + lax.rem(self.ring + (step + 4), 4)

    def device(self, step, flip):
        member = self.member(step, flip)
        if self.axis == "ctx":
            return (member * 2 + self.core, self.fsdp)
        return (self.ctx, member)

    def neighbours(self):
        return [self.device(1, 0), self.device(-1, 0), self.device(0, 1)]


def other_core(group):
    return (group.ctx + 1 - 2 * group.core, group.fsdp)


def barrier(devices):
    semaphore = pltpu.get_barrier_semaphore()
    for device in devices:
        pl.semaphore_signal(semaphore, inc=1, device_id=device, device_id_type=MESH)
    pl.semaphore_wait(semaphore, len(devices))


def remote(source, target, sems, slot, device):
    return pltpu.make_async_remote_copy(
        src_ref=source,
        dst_ref=target,
        send_sem=sems[0].at[slot],
        recv_sem=sems[1].at[slot],
        device_id=device,
        device_id_type=MESH,
    )


GATHER = (
    (1, 0, (0, 0), 0, 2, None),
    (-1, 0, (0, 0), 0, 2, None),
    (0, 1, (0, 0), 2, 4, None),
    (1, 0, (0, 0), 2, 4, None),
    (-1, 0, (0, 0), 2, 4, None),
    (0, 1, (0, 0), 0, 2, None),
    (1, 0, (-1, 0), 0, 1, 0),
    (-1, 0, (1, 0), 1, 2, 1),
    (0, 1, (-1, 0), 0, 2, 0),
    (0, 1, (1, 0), 0, 2, 1),
    (0, 1, (2, 0), 0, 1, 6),
    (0, 1, (2, 0), 1, 2, 7),
    (1, 0, (0, 1), 2, 4, 2),
    (-1, 0, (0, 1), 2, 4, 2),
    (1, 0, (-1, 0), 2, 3, 3),
    (-1, 0, (1, 0), 3, 4, 4),
    (1, 0, (-1, 1), 2, 3, 12),
    (-1, 0, (1, 1), 3, 4, 13),
)
GATHER_ORDER = (0, 1, 2, 3, 4, 6, 7, 12, 13, 5, 8, 14, 15, 9, 10, 16, 17, 11)
GATHER_SLOTS = len(GATHER)


def gather(group, view, sems, arrived=None, own=None):
    started = []

    def start(slot):
        step, flip, block, a, b, _ = GATHER[slot]

        def copy():
            ref = view(group.member(*block), a, b)
            source = own(a, b) if own and block == (0, 0) else ref
            return remote(source, ref, sems, slot, group.device(step, flip))

        copy().start()
        started.append(copy)

    for slot in range(GATHER_SLOTS):
        if GATHER[slot][5] is None:
            start(slot)
    if arrived:
        arrived((0, 0), 0, 4)
    for slot in GATHER_ORDER:
        step, flip, block, a, b, _ = GATHER[slot]
        yield
        source = (block[0] - step, block[1] ^ flip)
        ref = view(group.member(*source), a, b)
        remote(ref, ref, sems, slot, group.device(step, flip)).wait_recv()
        for later in range(GATHER_SLOTS):
            if GATHER[later][5] == slot:
                start(later)
        if arrived:
            arrived(source, a, b)
    for copy in started:
        copy().wait_send()


SCATTER_SLOTS = 23
HOLD = 7


def add_into(target, *sources):
    total = target[...].astype(F32)
    for source in sources:
        total = total + source[...].astype(F32)
    target[...] = total.astype(target.dtype)


def scatter(group, part, quarters, hold, result, sems, pair_first=True, prepare=None):
    started = []

    def held(k, a, b):
        return quarters(hold.at[k], a, b)

    def start(slot, source, step, flip, k, a, b):
        def copy():
            return remote(source(), held(k, a, b), sems, slot, group.device(step, flip))

        copy().start()
        started.append(copy)

    prepared = []

    def ready(block):
        if prepare and block not in prepared:
            prepared.append(block)
            prepare(*block)

    def send_part(slot, block, step, flip, k, a, b):
        ready(block)
        start(slot, lambda: part(*block, a, b), step, flip, k, a, b)

    def send_held(slot, source, step, flip, k, a, b):
        start(slot, lambda: held(source, a, b), step, flip, k, a, b)

    def wait(slot, k, a, b):
        ref = held(k, a, b)
        remote(ref, ref, sems, slot, group.device(0, 1)).wait_recv()

    if pair_first:
        send_part(0, (2, 1), 0, 1, 0, 0, 2)
    send_part(10, (2, 1), 1, 0, 0, 2, 3)
    send_part(11, (2, 1), -1, 0, 0, 3, 4)
    if pair_first:
        send_part(1, (1, 1), 0, 1, 1, 0, 2)
        send_part(2, (-1, 1), 0, 1, 2, 0, 2)
    send_part(16, (2, 0), 1, 0, 3, 2, 3)
    send_part(17, (2, 0), -1, 0, 3, 3, 4)
    send_part(12, (1, 1), 1, 0, 1, 3, 4)
    send_part(13, (-1, 1), -1, 0, 2, 2, 3)
    send_part(18, (1, 0), 1, 0, 4, 3, 4)
    send_part(19, (-1, 0), -1, 0, 5, 2, 3)
    if pair_first:
        send_part(3, (0, 1), 0, 1, 3, 0, 2)
    ready((0, 1))
    ready((0, 0))
    yield
    wait(10, 0, 2, 3)
    add_into(held(0, 2, 3), part(1, 1, 2, 3))
    send_held(14, 0, 1, 0, 1, 2, 3)
    wait(11, 0, 3, 4)
    add_into(held(0, 3, 4), part(-1, 1, 3, 4))
    send_held(15, 0, -1, 0, 2, 3, 4)
    if pair_first:
        yield
        wait(0, 0, 0, 2)
        add_into(held(0, 0, 2), part(2, 0, 0, 2))
        send_held(4, 0, 1, 0, 4, 0, 1)
        send_held(5, 0, -1, 0, 4, 1, 2)
    yield
    wait(16, 3, 2, 3)
    add_into(held(3, 2, 3), part(1, 0, 2, 3))
    send_held(20, 3, 1, 0, 4, 2, 3)
    wait(17, 3, 3, 4)
    add_into(held(3, 3, 4), part(-1, 0, 3, 4))
    send_held(21, 3, -1, 0, 5, 3, 4)
    if pair_first:
        yield
        wait(1, 1, 0, 2)
        add_into(held(1, 0, 2), part(1, 0, 0, 2))
        send_held(6, 1, 1, 0, 5, 1, 2)
    yield
    wait(12, 1, 3, 4)
    wait(14, 1, 2, 3)
    wait(13, 2, 2, 3)
    wait(15, 2, 3, 4)
    add_into(held(1, 2, 4), held(2, 2, 4), part(0, 1, 2, 4))
    send_held(22, 1, 0, 1, 6, 2, 4)
    if pair_first:
        yield
        wait(2, 2, 0, 2)
        add_into(held(2, 0, 2), part(-1, 0, 0, 2))
        send_held(8, 2, -1, 0, 6, 0, 1)
        yield
        wait(4, 4, 0, 1)
        add_into(held(1, 0, 1), held(4, 0, 1))
        send_held(7, 1, 1, 0, 5, 0, 1)
        wait(5, 4, 1, 2)
        add_into(held(2, 1, 2), held(4, 1, 2))
        send_held(9, 2, -1, 0, 6, 1, 2)
        yield
        wait(3, 3, 0, 2)
        wait(6, 5, 1, 2)
        wait(8, 6, 0, 1)
        wait(7, 5, 0, 1)
        wait(9, 6, 1, 2)
        result(0, 2, [part(0, 0, 0, 2), held(3, 0, 2), held(5, 0, 2), held(6, 0, 2)])
    yield
    wait(18, 4, 3, 4)
    wait(20, 4, 2, 3)
    wait(19, 5, 2, 3)
    wait(21, 5, 3, 4)
    wait(22, 6, 2, 4)
    result(2, 4, [part(0, 0, 2, 4), held(4, 2, 4), held(5, 2, 4), held(6, 2, 4)])
    for copy in started:
        copy().wait_send()


def total_of(refs):
    total = refs[0][...].astype(F32)
    for ref in refs[1:]:
        total = total + ref[...].astype(F32)
    return total


def drain(*programs):
    programs = list(programs)
    while programs:
        programs = [p for p in programs if next(p, "end") != "end"]


def pairs(count):
    return [pltpu.SemaphoreType.DMA((count,)), pltpu.SemaphoreType.DMA((count,))]


def params(collective_id, mib):
    return pltpu.CompilerParams(
        collective_id=collective_id, has_side_effects=True, vmem_limit_bytes=mib * MIB
    )


ROW_CUTS = (0, 96, 192, 288, 400)


TILE = 2 * GROUP
TILES = SEQ_LEN // TILE
ITEMS = TILES + 1
KEYS, VALUES = slice(0, 128), slice(128, 256)
NT = (((1,), (1,)), ((), ()))
TN = (((0,), (0,)), ((), ()))


def dot(a, b, dims=(((1,), (0,)), ((), ()))):
    return lax.dot_general(a, b, dims, preferred_element_type=F32)


class Steps:
    def __init__(self, *programs):
        self.programs = list(programs)

    def take(self, count=1):
        for _ in range(count):
            self.programs = [p for p in self.programs if next(p, "end") != "end"]

    def at(self, j, plan):
        for iteration, count in plan:
            pl.when(j == iteration)(partial(self.take, count))

    def finish(self):
        drain(*self.programs)


class Copies:
    def __init__(self, sems):
        self.sems, self.made = sems, []

    def start(self, source, target):
        slot = len(self.made)

        def copy():
            return pltpu.make_async_copy(source(), target(), self.sems.at[slot])

        copy().start()
        self.made.append(copy)
        return slot

    def wait(self, *slots):
        for slot in slots:
            self.made[slot]().wait()
            self.made[slot] = None

    def finish(self):
        self.wait(*[slot for slot, copy in enumerate(self.made) if copy])


def chunk_of(i, size):
    return pl.ds(pl.multiple_of(i * size, size), size)


def turned(values, cosine, sine):
    lane = lax.rem(lax.broadcasted_iota(jnp.int32, (1, 128), 1), HEAD_DIM)
    swapped = jnp.where(lane < ROT // 2, -pltpu.roll(values, 128 - ROT // 2, 1), pltpu.roll(values, ROT // 2, 1))
    return values * cosine + swapped * sine


def cut_rows(ref, a, b):
    step = ref.shape[0] // 4
    return ref.at[pl.ds(step * a, step * (b - a)), :]


def rows_scatter(group, part_ref, out, arriving, hold, sems):
    cs, cr, send, recv = sems
    core, partner = group.core, other_core(group)

    def exchange():
        return remote(part_ref.at[1 - core], arriving, (cs, cr), 0, partner)

    exchange().start()
    yield
    exchange().wait()

    def one(i, carry):
        rows = pl.ds(pl.multiple_of(i * 32, 32), 32)
        arriving[rows, :] = (arriving[rows, :].astype(F32) + part_ref[core, rows, :].astype(F32)).astype(BF16)
        return carry

    lax.fori_loop(0, arriving.shape[0] // 32, one, 0)
    width, size = out.shape[1], out.shape[0] // 2

    def cut(ref, a, b):
        return ref.at[pl.ds(size * (a - 2), size * (b - a)), :]

    def part(step, flip, a, b):
        columns = pl.ds(pl.multiple_of(group.member(step, flip) * width, width), width)
        return arriving.at[pl.ds(size * (a - 2), size * (b - a)), columns]

    def result(a, b, refs):
        target = cut(out, a, b)
        target[...] = total_of(refs)

    yield from scatter(group, part, cut, hold, result, (send, recv), pair_first=False)


def peers(axis):
    ctx, fsdp = lax.axis_index("ctx"), lax.axis_index("fsdp")
    count = lax.axis_size(axis)
    if axis == "ctx":
        return [(lax.rem(ctx + offset, count), fsdp) for offset in range(1, count)]
    return [(ctx, lax.rem(fsdp + offset, count)) for offset in range(1, count)]


def sum_small(x_ref, out, hold, sems, devices):
    def copy(i):
        return remote(x_ref, hold.at[i], sems, i, devices[i])

    for i in range(len(devices)):
        copy(i).start()
    yield
    total = x_ref[...]
    for i in range(len(devices)):
        copy(i).wait_recv()
        total = total + hold[i]
    out[...] = total
    for i in range(len(devices)):
        copy(i).wait_send()


def reduce_one(group, source, target, hold, sems):
    rs, rr, gs, gr, cs, cr, ls = sems
    core, partner = group.core, other_core(group)
    rows, width = source.shape[0] // 8, source.shape[1]
    by_rows = rows % 64 == 0

    def quarters(ref, a, b):
        if by_rows:
            return ref.at[pl.ds(rows // 4 * a, rows // 4 * (b - a)), :]
        return ref.at[:, pl.ds(width // 4 * a, width // 4 * (b - a))]

    def part(step, flip, a, b):
        return quarters(source.at[chunk_of(group.member(step, flip), rows), :], a, b)

    def view(member, a, b):
        return quarters(target(core).at[chunk_of(member, rows), :], a, b)

    def own(a, b):
        return quarters(hold.at[HOLD - 1], a, b)

    def result(a, b, terms):
        place = own(a, b)
        place[...] = total_of(terms).astype(BF16)

    def keep():
        return pltpu.make_async_copy(own(0, 4), view(group.me, 0, 4), ls.at[0])

    copies = []

    def arrived(block, a, b):
        slot = len(copies)

        def copy():
            ref = view(group.member(*block), a, b)
            return remote(own(a, b) if block == (0, 0) else ref, ref, (cs, cr), slot, partner)

        copy().start()
        copies.append(copy)

    yield from scatter(group, part, quarters, hold, result, (rs, rr))
    keep().start()
    yield from gather(group, view, (gs, gr), arrived, own=own)
    yield
    keep().wait()
    for copy in copies:
        copy().wait()


def reduce_scratch(shape):
    return pltpu.VMEM((HOLD, shape[0] // 8, shape[1]), BF16)


def reduce_sems():
    return pairs(SCATTER_SLOTS) + pairs(GATHER_SLOTS) + pairs(GATHER_SLOTS + 1) + [pltpu.SemaphoreType.DMA((1,))]


STATES = 11


def state_of(j):
    late = lax.div(j + 7, 16)
    return j * (1 - late) + (9 + lax.rem(j, 2)) * late


FORWARD_PLAN = ((1, 1), (3, 1), (4, 1), (8, 1), (11, 1), (13, 1), (14, 1))
BACKWARD_PLAN = ((0, 1), (2, 1), (8, 3), (12, 2), (14, 2), (16, 2))
BRANCH_PLAN = ((2, 1), (5, 1), (8, 1), (12, 1))
OUT_PLAN = ((4, 2), (6, 2), (9, 2), (11, 1), (13, 2), (15, 5))
ROWS, LAST, EARLY, WEIGHTS, OUT = range(5)
TAIL_PLAN = (
    (ROWS, 1), (EARLY, 3), (EARLY, 2), (LAST, 3), (EARLY, 2), (LAST, 1), (ROWS, 1), (LAST, 1), (EARLY, 1), (LAST, 2), (ROWS, 1), (EARLY, 1),
    (LAST, 2), (ROWS, 1), (EARLY, 5), (LAST, 5), (EARLY, 4), (LAST, 4), (ROWS, 1),
)


def layer_kernel(
    order_ref, ids_ref, x_ref, dy_ref, vectors_ref, wq, wk, wv, wo, wi, wu,
    layer_out, input_out, vec_out, q_out, k_out, v_out, out_out, inner_out, outer_out,
    x_all, dy_all, normed, qkv_w, o_w, i_w, u_w, kv_all, inner, act, act_t, grad, ff, ffn, inner_part, outer_part, out_part,
    cos_ref, sin_ref, q_ref, cotangent_ref, begin_ref, unit_ref, inv_ref, inner_sum, slot_of,
    state_max, state_sum, state_acc, dkv_items, lse_ref, delta_ref, att_ref, dq_ref,
    arriving, branch_hold, sum_ref, arriving_back, back_hold, local_ref, inner_hold, outer_hold, q_hold, k_hold, v_hold, out_hold, keys_hold, own, pre,
    stats, stats_hold, stats_sum, vec, vec_hold,
    *sems,
):
    across, along = Group("ctx"), Group("fsdp")
    core, chip, fsdp, partner = across.core, across.me, along.me, other_core(across)
    rows, width = dy_ref.shape
    sems = list(sems)

    def sems_for(count):
        taken = sems[:count]
        del sems[:count]
        return taken

    xs, ds, ks, cs = sems_for(2), sems_for(2), sems_for(2), sems_for(2)
    copies = Copies(sems_for(1)[0])
    x_cuts = (0, 96, 192, 288, x_all.shape[0])

    def x_view(member, a, b):
        return x_all.at[pl.ds(x_cuts[a], x_cuts[b] - x_cuts[a]), chunk_of(member, width)]

    def dy_view(member, a, b):
        return dy_all.at[core, pl.ds(rows // 4 * a, rows // 4 * (b - a)), chunk_of(member, width)]

    copies.start(lambda: x_ref, lambda: x_all.at[pl.ds(0, rows), chunk_of(fsdp, width)])
    copies.start(lambda: dy_ref, lambda: dy_view(fsdp, 0, 4))
    for i, ref in enumerate((wq, wk, wv)):
        copies.start(lambda ref=ref: ref.at[:, chunk_of(core, 128)], lambda i=i: qkv_w.at[:, pl.ds(128 * i, 128)])
    copies.start(lambda: wi.at[:, chunk_of(core, 512)], lambda: i_w)
    copies.start(lambda: wu.at[chunk_of(core, 512), :], lambda: u_w)
    copies.start(lambda: wo.at[chunk_of(core, 128), :], lambda: o_w)
    def vector(i):
        return vectors_ref[:, 256 * i : 256 * i + 256]

    extra = jnp.concatenate([vector(0), vector(1), jnp.zeros((14, width), F32)], axis=0)
    x_all[rows:, chunk_of(fsdp, width)] = extra.astype(BF16)
    barrier(peers("ctx") + peers("fsdp"))
    copies.wait(0, 1)
    x_steps = Steps(gather(along, x_view, xs))
    x_steps.take()
    dy_steps = Steps(gather(along, dy_view, ds))

    lane = lax.rem(lax.broadcasted_iota(jnp.int32, (1, 128), 1), HEAD_DIM)
    left = lax.broadcasted_iota(jnp.int32, (1, 128), 1) < HEAD_DIM
    freqs = jnp.zeros((1, 128), F32)
    for i in range(ROT):
        freqs = jnp.where(lane == i, 10000.0 ** (-2.0 * (i % (ROT // 2)) / ROT), freqs)
    for slot in range(4):
        group = order_ref[chip * 4 + slot]
        position = (group * GROUP + lax.broadcasted_iota(jnp.int32, (GROUP, 128), 0)).astype(F32)
        angles = position * freqs
        place = slice(GROUP * slot, GROUP * slot + GROUP)
        cos_ref[place, :] = jnp.cos(angles)
        sin_ref[place, :] = jnp.sin(angles)
        column = lax.broadcasted_iota(jnp.int32, (1, TILE), 1)
        column = group * GROUP + jnp.where(column < GROUP, column, column - GROUP)
        begin = jnp.zeros((1, TILE), jnp.int32)
        for doc in range(1, DOCS):
            before = jnp.sum(jnp.where(ids_ref[...] < doc, 1, 0), axis=0, keepdims=True)
            before = jnp.sum(before, axis=1, keepdims=True)
            begin = jnp.where(before <= column, before, begin)
        begin_ref[slot] = begin

    def find(group, carry):
        place = 0
        for slot in range(1, GROUPS):
            apart = order_ref[slot] - group
            place = place + slot * (1 - jnp.minimum(apart * apart, 1))
        slot_of[group] = jnp.minimum(place, GROUPS - 1)
        return carry

    lax.fori_loop(0, GROUPS, find, 0)

    x_steps.take(9)
    dy_steps.take()
    x_steps.finish()
    gain, shift = x_all[rows : rows + 1, :].astype(F32), x_all[rows + 1 : rows + 2, :].astype(F32)

    def exchange(ref, i):
        half = ref.at[core, pl.ds(GROUP * i, GROUP), :]
        return remote(half, half, cs, 2 * (ref is dy_all) + i, partner)

    def norm(i, carry):
        place = chunk_of(i, 32)
        values = x_all[place, :].astype(F32)
        mean = jnp.mean(values, axis=1, keepdims=True)
        centered = values - mean
        inv = lax.rsqrt(jnp.mean(centered * centered, axis=1, keepdims=True) + EPS)
        normed[core, place, :] = (centered * inv * gain + shift).astype(BF16)
        unit_ref[place, :] = (x_all[place, chunk_of(fsdp, width)].astype(F32) - mean) * inv
        inv_ref[place, :] = inv
        return carry

    for i in range(2):
        lax.fori_loop(GROUP // 32 * i, GROUP // 32 * (i + 1), norm, 0)
        exchange(normed, i).start()
    copies.wait(2, 3, 4)
    dy_steps.take(3)

    def project(of):
        pre_rows = dot(normed[of], qkv_w[...])
        bias = [vectors_ref[:, pl.ds(pl.multiple_of(512 + 256 * i + 128 * core, 128), 128)] for i in range(3)]
        for half in range(2):
            slot, part_rows = 2 * of + half, slice(GROUP * half, GROUP * half + GROUP)
            cosine, sine = cos_ref[chunk_of(slot, GROUP), :], sin_ref[chunk_of(slot, GROUP), :]
            queries = turned(pre_rows[part_rows, :128] + bias[0], cosine, sine).astype(BF16)
            q_ref[slot] = (queries.astype(F32) * HEAD_DIM ** (-0.5)).astype(BF16)
            kv_all[4 * chip + slot, :, :128] = turned(pre_rows[part_rows, 128:256] + bias[1], cosine, sine).astype(BF16)
            kv_all[4 * chip + slot, :, 128:] = (pre_rows[part_rows, 256:] + bias[2]).astype(BF16)

    def both_cores(one, ref):
        def here():
            for i in range(2):
                exchange(ref, i).wait()

        def loop(i, carry):
            pl.when(i == 1)(here)
            one(lax.rem(core + i, 2))
            return carry

        lax.fori_loop(0, 2, loop, 0)

    both_cores(project, normed)

    def kv_view(member, a, b):
        return kv_all.at[pl.ds(4 * member + a, b - a)]

    kv_steps = Steps(gather(across, kv_view, ks))
    kv_steps.take()
    dy_steps.take(6)
    copies.wait(5, 6, 7)

    inner_bias = vectors_ref[:, pl.ds(pl.multiple_of(1792 + 512 * core, 128), 512)]

    def feed(of, carry):
        value = dot(normed[of], i_w[...]) + inner_bias
        inner[chunk_of(of, rows), :] = value
        curve = jnp.tanh(GELU_A * (value + GELU_B * value * value * value))
        act[chunk_of(of, rows), :] = (0.5 * value * (1.0 + curve)).astype(BF16)
        return carry

    lax.fori_loop(0, 2, feed, 0)
    dy_steps.take(4)
    kv_steps.take(3)

    def feed_out(i, carry):
        block = chunk_of(i, 256)
        ff[:, :, block] = dot(act[...], u_w[:, block]).astype(BF16).reshape(2, rows, 256)
        return carry

    lax.fori_loop(0, 8, feed_out, 0)
    act_t[...] = act[...].T
    dy_steps.finish()
    for i in range(2):
        exchange(dy_all, i).start()
    kv_steps.take(2)
    inner_sum[...] = jnp.zeros_like(inner_sum)

    def gradients(of):
        dy_rows = dy_all[of]
        ag = dot(dy_rows, o_w[...], NT).astype(BF16)
        cotangent_ref[2 * of], cotangent_ref[2 * of + 1] = ag[:GROUP], ag[GROUP:]
        value = inner[chunk_of(of, rows), :]
        square = value * value
        curve = jnp.tanh(GELU_A * (value + GELU_B * square * value))
        slope = 0.5 * (1.0 + curve) + 0.5 * value * (1.0 - curve * curve) * (GELU_A * (1.0 + 3.0 * GELU_B * square))
        out = (dot(dy_rows, u_w[...], NT) * slope).astype(BF16)
        grad[chunk_of(of, rows), :] = out
        inner_sum[...] += jnp.sum(out.astype(F32), axis=0, keepdims=True)

    both_cores(gradients, dy_all)
    kv_steps.take(2)

    def outer_weights(i, carry):
        block = chunk_of(i, 256)
        outer_part[:, block] = dot(act_t[...], dy_all[:, :, block].reshape(2 * rows, 256)).astype(BF16)
        return carry

    lax.fori_loop(0, 8, outer_weights, 0)
    outer_program = reduce_one(across, outer_part, lambda c: outer_out.at[c], outer_hold, sems_for(7))
    inner_program = reduce_one(across, inner_part, lambda c: inner_out.at[:, chunk_of(c, 512)], inner_hold, sems_for(7))
    kv_steps.take(2)
    next(outer_program)

    def inner_weights(i, carry):
        block = chunk_of(i, 256)
        inner_part[block, :] = dot(normed[:, :, block].reshape(2 * rows, 256), grad[...], TN).astype(BF16)
        return carry

    lax.fori_loop(0, 8, inner_weights, 0)
    kv_steps.take(2)
    next(inner_program)

    kv_steps.finish()
    weights_steps = Steps(outer_program, inner_program)

    def bit(number):
        return jnp.minimum(jnp.maximum(number, 0), 1)

    def pair_facts(p):
        g0, g1 = order_ref[4 * chip + 2 * p], order_ref[4 * chip + 2 * p + 1]
        low, high = jnp.minimum(g0, g1), jnp.maximum(g0, g1)
        return low, high, bit(g0 - g1), lax.div(low, 2) + 1

    key_row = lax.broadcasted_iota(jnp.int32, (TILE, TILE), 0)
    column = lax.broadcasted_iota(jnp.int32, (1, TILE), 1)
    query_row = jnp.where(column < GROUP, column, column - GROUP)

    def item_facts(p, j):
        low, high, low_slot, count = pair_facts(p)
        second = bit(j - count + 1)
        tile = second * TILES + (1 - second) * (count - 1) - j
        slot = 2 * p + second * (1 - low_slot) + (1 - second) * low_slot
        position = (second * high + (1 - second) * low) * GROUP
        last = query_row + (position - tile * TILE)
        begin = begin_ref[slot] - tile * TILE
        allowed = (key_row <= last) & (key_row >= begin)
        keep = bit(j * (j - count) * (j - count)).astype(F32)
        return tile, slot, allowed, keep

    def keys_of(tile, lanes):
        return jnp.concatenate([kv_all[slot_of[2 * tile], :, lanes], kv_all[slot_of[2 * tile + 1], :, lanes]], axis=0)

    def stacked(rows):
        zero = jnp.zeros_like(rows)
        return jnp.concatenate([jnp.where(left, rows, zero), jnp.where(left, zero, rows)], axis=0)

    def unstacked(columns):
        rows = columns.T
        return jnp.where(left, rows[:GROUP], rows[GROUP:])

    def final_item(p, i):
        low, high, low_slot, count = pair_facts(p)
        is_low = low_slot if i else 1 - low_slot
        return count * is_low + 10 * (1 - is_low)

    for p in range(2):
        state_max[p, 0] = jnp.full((1, TILE), FLOOR, F32)
        state_sum[p, 0] = jnp.zeros((1, TILE), F32)
        state_acc[p, 0] = jnp.zeros((128, TILE), F32)

    def forward(j, carry):
        weights_steps.at(j, FORWARD_PLAN)
        now, after = state_of(j), state_of(j + 1)
        for p in range(2):
            tile, slot, allowed, keep = item_facts(p, j)
            scores = jnp.where(allowed, dot(keys_of(tile, KEYS), stacked(q_ref[slot]), NT), MASKED)
            old_max = state_max[p, now] * keep + FLOOR * (1.0 - keep)
            new_max = jnp.maximum(old_max, jnp.max(scores, axis=0, keepdims=True))
            weights = jnp.exp(scores - new_max)
            factor = jnp.exp(old_max - new_max)
            state_max[p, after] = new_max
            state_sum[p, after] = state_sum[p, now] * factor + jnp.sum(weights, axis=0, keepdims=True)
            state_acc[p, after] = state_acc[p, now] * factor + dot(keys_of(tile, VALUES), weights.astype(BF16), TN)
        return carry

    lax.fori_loop(0, ITEMS, forward, 0)

    for p in range(2):
        for i in range(2):
            item = final_item(p, i)
            slot = 2 * p + i
            total = state_sum[p, item]
            out = state_acc[p, item] / total
            lse_ref[slot] = state_max[p, item] + jnp.log(total)
            cotangent = stacked(cotangent_ref[slot].astype(F32)).T
            delta_ref[slot] = jnp.sum(cotangent * out, axis=0, keepdims=True)
            att_ref[slot] = unstacked(out).astype(BF16)

    def branches(i, carry):
        block = chunk_of(i, 256)
        attended = dot(att_ref[...].reshape(2 * rows, 128), o_w[:, block]).reshape(2, rows, 256)
        ff[:, :, block] = (ff[:, :, block].astype(F32) + attended).astype(BF16)
        return carry

    lax.fori_loop(0, 8, branches, 0)
    branch_steps = Steps(rows_scatter(along, ff, sum_ref, arriving, branch_hold, sems_for(4)))
    branch_steps.take()

    def out_weights(i, carry):
        block = chunk_of(i, 256)
        out_part[:, block] = dot(att_ref[...].reshape(2 * rows, 128), dy_all[:, :, block].reshape(2 * rows, 256), TN).astype(BF16)
        return carry

    lax.fori_loop(0, 8, out_weights, 0)
    out_steps = Steps(reduce_one(across, out_part, lambda c: out_out.at[c], out_hold, sems_for(7)))
    out_steps.take()

    for p in range(2):
        state_acc[p, 0] = jnp.zeros((128, TILE), F32)

    def backward(j, carry):
        weights_steps.at(j, BACKWARD_PLAN)
        branch_steps.at(j, BRANCH_PLAN)
        out_steps.at(j, OUT_PLAN)
        now, after = state_of(j), state_of(j + 1)
        for p in range(2):
            tile, slot, allowed, keep = item_facts(p, j)
            queries, cotangent = stacked(q_ref[slot]), stacked(cotangent_ref[slot])
            scores = dot(keys_of(tile, KEYS), queries, NT)
            probs = jnp.where(allowed, jnp.exp(scores - lse_ref[slot]), 0.0)
            prob_grad = dot(keys_of(tile, VALUES), cotangent, NT)
            score_grad = (probs * (prob_grad - delta_ref[slot])).astype(BF16)
            state_acc[p, after] = state_acc[p, now] * keep + dot(keys_of(tile, KEYS), score_grad, TN)
            key_grad = dot(score_grad, queries).astype(BF16)
            value_grad = dot(probs.astype(BF16), cotangent).astype(BF16)
            for half in range(2):
                rows = slice(GROUP * half, GROUP * half + GROUP)
                dkv_items[p, j, half, :, :128] = key_grad[rows]
                dkv_items[p, j, half, :, 128:] = value_grad[rows]
        return carry

    lax.fori_loop(0, ITEMS, backward, 0)

    for p in range(2):
        for i in range(2):
            dq_ref[2 * p + i] = unstacked(state_acc[p, final_item(p, i)])

    counts = [pair_facts(p)[3] for p in range(2)]

    def collect(s, carry):
        group = order_ref[s]
        tile, half = lax.div(group, 2), lax.rem(group, 2)
        total = jnp.zeros((GROUP, 256), F32)
        for p in range(2):
            low_item = dkv_items[p, jnp.maximum(counts[p] - 1 - tile, 0), half].astype(F32)
            high_item = dkv_items[p, jnp.maximum(TILES - tile, counts[p]), half].astype(F32)
            total = total + low_item * bit(counts[p] - tile).astype(F32)
            total = total + high_item * bit(TILES - tile - counts[p] + 1).astype(F32)
        kv_all[s] = total.astype(BF16)
        return carry

    def collect_member(step, flip):
        start = 4 * across.member(step, flip)
        lax.fori_loop(start, start + 4, collect, 0)

    def part(step, flip, a, b):
        return kv_all.at[pl.ds(4 * across.member(step, flip) + a, b - a)]

    def cut_groups(ref, a, b):
        return ref.at[pl.ds(a, b - a)]

    def result(a, b, refs):
        own[a:b] = total_of(refs)

    keys_steps = Steps(scatter(across, part, cut_groups, keys_hold, result, sems_for(2), prepare=collect_member))
    keys_steps.take()
    branch_steps.finish()
    layer_sum = x_all[:rows, chunk_of(fsdp, width)].astype(F32) + sum_ref[...]
    layer_out[...] = (layer_sum + vector(5) + vector(6)).astype(BF16)
    for slot in range(4):
        place = slice(GROUP * slot, GROUP * slot + GROUP)
        turned_back = turned(dq_ref[slot] * HEAD_DIM ** (-0.5), cos_ref[place, :], -sin_ref[place, :])
        pre[place, :128] = turned_back.astype(BF16)
    q_part, k_part, v_part = [inner_part.at[:, pl.ds(128 * i, 128)] for i in range(3)]

    def query_weights(i, carry):
        block = chunk_of(i, 256)
        q_part[block, :] = dot(normed[:, :, block].reshape(2 * rows, 256), pre[:, :128], TN).astype(BF16)
        return carry

    lax.fori_loop(0, 8, query_weights, 0)
    keys_steps.take()

    early_steps = Steps(reduce_one(across, q_part, lambda c: q_out.at[:, chunk_of(c, 128)], q_hold, sems_for(7)))
    keys_steps.take()
    early_steps.take()
    def feed_back(i, carry):
        block = chunk_of(i, 256)
        ffn[:, :, block] = dot(grad[...], i_w[block, :], NT).astype(BF16).reshape(2, rows, 256)
        return carry

    lax.fori_loop(0, 8, feed_back, 0)
    weights_steps.take(2)
    keys_steps.take(2)
    weights_steps.take(2)
    keys_steps.take(2)
    weights_steps.take(2)
    keys_steps.finish()
    for slot in range(4):
        place = slice(GROUP * slot, GROUP * slot + GROUP)
        turned_back = turned(own[slot, :, :128], cos_ref[place, :], -sin_ref[place, :])
        pre[place, 128:256] = turned_back.astype(BF16)
        pre[place, 256:] = own[slot, :, 128:].astype(BF16)

    def key_weights(i, carry):
        block = chunk_of(i, 256)
        total = dot(normed[:, :, block].reshape(2 * rows, 256), pre[:, 128:], TN).astype(BF16)
        k_part[block, :] = total[:, :128]
        v_part[block, :] = total[:, 128:]
        return carry

    def normed_grad(of):
        def one(i, carry):
            part_rows, columns = chunk_of(lax.div(i, 4), GROUP), chunk_of(lax.rem(i, 4), 512)
            from_rows = chunk_of(2 * of + lax.div(i, 4), GROUP)
            total = ffn[of, part_rows, columns].astype(F32) + dot(pre[from_rows, :], qkv_w[columns, :], NT)
            ffn[of, part_rows, columns] = total.astype(BF16)
            return carry

        lax.fori_loop(0, 8, one, 0)

    normed_grad(1 - core)
    rows_steps = Steps(rows_scatter(along, ffn, local_ref, arriving_back, back_hold, sems_for(4)))
    rows_steps.take()
    lax.fori_loop(0, 8, key_weights, 0)
    last_steps = Steps(
        reduce_one(across, k_part, lambda c: k_out.at[:, chunk_of(c, 128)], k_hold, sems_for(7)),
        reduce_one(across, v_part, lambda c: v_out.at[:, chunk_of(c, 128)], v_hold, sems_for(7)),
    )
    last_steps.take()
    normed_grad(core)
    for programs, count in TAIL_PLAN:
        (rows_steps, last_steps, early_steps, weights_steps, out_steps)[programs].take(count)
    rows_steps.finish()

    whole = local_ref[...]
    unit = unit_ref[...]
    scaled = whole * vector(0)
    lane = lax.broadcasted_iota(jnp.int32, (1, 128), 1)
    first = jnp.sum(scaled, axis=1, keepdims=True)
    second = jnp.sum(scaled * unit, axis=1, keepdims=True)
    stats[...] = jnp.where(lane == 0, first, jnp.where(lane == 1, second, 0.0)).T[:8]
    stats_steps = Steps(sum_small(stats, stats_sum, stats_hold, sems_for(2), peers("fsdp")))
    stats_steps.take()
    cotangent = dy_all[core, :, chunk_of(fsdp, width)].astype(F32)
    vec[...] = jnp.zeros_like(vec)
    vec[0:1, :] = jnp.sum(whole * unit, axis=0, keepdims=True)
    vec[1:2, :] = jnp.sum(whole, axis=0, keepdims=True)
    vec[2:3, :] = jnp.sum(cotangent, axis=0, keepdims=True)
    for i in range(3):
        vec[3 + i : 4 + i, chunk_of(core, 128)] = jnp.sum(pre[:, 128 * i : 128 * i + 128].astype(F32), axis=0, keepdims=True)
    for i in range(2):
        vec[pl.ds(6 + 2 * core + i, 1), :] = inner_sum[:, 256 * i : 256 * i + 256]
    vec_steps = Steps(sum_small(vec, vec_out, vec_hold, sems_for(2), peers("ctx")))
    vec_steps.take()
    early_steps.take(9)
    weights_steps.finish()
    out_steps.finish()
    stats_steps.finish()
    back = jnp.concatenate([stats_sum[...], jnp.zeros((120, rows), F32)], axis=0).T * (1.0 / 2048)
    input_out[...] = cotangent + inv_ref[...] * (scaled - back[:, 0:1] - unit * back[:, 1:2])
    vec_steps.finish()
    weights_steps.finish()
    early_steps.finish()
    last_steps.finish()
    assert not sems


def layer(order, ids, x, dy, vectors, weights):
    rows, width = dy.shape
    wide, both = weights[0].shape[0], 2 * rows

    def bf(*shape):
        return pltpu.VMEM(shape, BF16)

    def f32(*shape):
        return pltpu.VMEM(shape, F32)

    def of(kind, *shape):
        return jax.ShapeDtypeStruct(shape, kind)

    return pl.pallas_call(
        layer_kernel,
        out_shape=[
            of(BF16, rows, width),
            of(F32, rows, width),
            of(F32, 16, width),
            of(BF16, wide, width),
            of(BF16, wide, width),
            of(BF16, wide, width),
            of(BF16, 2, 128, wide),
            of(BF16, wide, 1024),
            of(BF16, 2, 512, wide),
        ],
        in_specs=[SMEM, VMEM, ANY, ANY, VMEM] + [ANY] * len(weights),
        out_specs=[VMEM] * 3 + [ANY] * 6,
        scratch_shapes=[
            bf(rows + 16, wide),
            bf(2, rows, wide),
            bf(2, rows, wide),
            bf(wide, 384),
            bf(128, wide),
            bf(wide, 512),
            bf(512, wide),
            bf(GROUPS, GROUP, 256),
            f32(both, 512),
            bf(both, 512),
            bf(512, both),
            bf(both, 512),
            bf(2, rows, wide),
            bf(2, rows, wide),
            bf(wide, 512),
            bf(512, wide),
            bf(128, wide),
            f32(both, 128),
            f32(both, 128),
            bf(4, GROUP, 128),
            bf(4, GROUP, 128),
            pltpu.VMEM((4, 1, TILE), jnp.int32),
            f32(rows, width),
            f32(rows, 1),
            f32(1, 512),
            pltpu.SMEM((GROUPS,), jnp.int32),
            f32(2, STATES, 1, TILE),
            f32(2, STATES, 1, TILE),
            f32(2, STATES, 128, TILE),
            bf(2, ITEMS, 2, GROUP, 256),
            f32(4, 1, TILE),
            f32(4, 1, TILE),
            bf(4, GROUP, 128),
            f32(4, GROUP, 128),
            bf(rows, wide),
            bf(HOLD, rows, width),
            f32(rows, width),
            bf(rows, wide),
            bf(HOLD, rows, width),
            f32(rows, width),
            reduce_scratch((wide, 512)),
            reduce_scratch((512, wide)),
            reduce_scratch((wide, 128)),
            reduce_scratch((wide, 128)),
            reduce_scratch((wide, 128)),
            reduce_scratch((128, wide)),
            bf(HOLD, 4, GROUP, 256),
            f32(4, GROUP, 256),
            bf(both, 384),
            f32(8, rows),
            f32(7, 8, rows),
            f32(8, rows),
            f32(16, width),
            f32(15, 16, width),
        ]
        + pairs(GATHER_SLOTS) * 3
        + pairs(4)
        + [pltpu.SemaphoreType.DMA((8,))]
        + reduce_sems() * 2
        + pairs(1)
        + pairs(SCATTER_SLOTS)
        + reduce_sems()
        + pairs(SCATTER_SLOTS)
        + reduce_sems()
        + pairs(1)
        + pairs(SCATTER_SLOTS)
        + reduce_sems() * 2
        + pairs(7)
        + pairs(15),
        compiler_params=params(0, 63),
        name="layer",
    )(order, ids, x, dy, vectors, *weights)


def body(
    layer_input,
    norm_gain,
    norm_bias,
    query_weight,
    query_bias,
    key_weight,
    key_bias,
    value_weight,
    value_bias,
    out_weight,
    out_bias,
    inner_weight,
    inner_bias,
    outer_weight,
    outer_bias,
    output_grad,
    group_order,
    sequence_ids,
):
    parts = [norm_gain, norm_bias, query_bias, key_bias, value_bias, out_bias, outer_bias, inner_bias]
    ends = [sum(p.shape[0] for p in parts[: i + 1]) for i in range(len(parts))]
    vectors = sum(jnp.pad(p.astype(F32), (end - p.shape[0], ends[-1] - end)) for p, end in zip(parts, ends))
    layer_output, input_grad, vectors, query_grad, key_grad, value_grad, out_grad, inner_w_grad, outer_w_grad = layer(
        group_order,
        sequence_ids.reshape(-1, 128),
        layer_input,
        output_grad,
        vectors[None],
        [query_weight, key_weight, value_weight, out_weight, inner_weight, outer_weight],
    )

    return (
        layer_output,
        input_grad,
        vectors[0],
        vectors[1],
        query_grad.astype(F32),
        vectors[3],
        key_grad.astype(F32),
        vectors[4],
        value_grad.astype(F32),
        vectors[5],
        out_grad.reshape(256, 2048).astype(F32),
        vectors[2],
        inner_w_grad.astype(F32),
        vectors[6:10].reshape(1024),
        outer_w_grad.reshape(1024, 2048).astype(F32),
        vectors[2],
    )


def solution(mesh):
    in_specs = (
        P("ctx", "fsdp"),
        P("fsdp"),
        P("fsdp"),
        P(None, "fsdp"),
        P("fsdp"),
        P(None, "fsdp"),
        P("fsdp"),
        P(None, "fsdp"),
        P("fsdp"),
        P("fsdp", None),
        P("fsdp"),
        P(None, "fsdp"),
        P("fsdp"),
        P("fsdp", None),
        P("fsdp"),
        P("ctx", "fsdp"),
        P(),
        P(),
    )
    out_specs = (
        P("ctx", "fsdp"),
        P("ctx", "fsdp"),
        P("fsdp"),
        P("fsdp"),
        P(None, "fsdp"),
        P("fsdp"),
        P(None, "fsdp"),
        P("fsdp"),
        P(None, "fsdp"),
        P("fsdp"),
        P("fsdp", None),
        P("fsdp"),
        P(None, "fsdp"),
        P("fsdp"),
        P("fsdp", None),
        P("fsdp"),
    )
    return jax.shard_map(body, mesh=mesh, in_specs=in_specs, out_specs=out_specs, check_vma=False)
```

```python
from functools import partial

import jax
import jax.numpy as jnp
from jax import lax
from jax.experimental import pallas as pl
from jax.experimental.pallas import tpu as pltpu
from jax.sharding import PartitionSpec as P

HEAD_DIM = 64
ROT = 32
GROUP = 192
GROUPS = 32
SEQ_LEN = 6144
DOCS = 5
EPS = 1e-05
MASKED = -1e30
FLOOR = -1e29
GELU_A = 0.7978845608028654
GELU_B = 0.044715
MESH = pl.DeviceIdType.MESH
BF16 = jnp.bfloat16
F32 = jnp.float32
ANY = pl.BlockSpec(memory_space=pl.ANY)
VMEM = pl.BlockSpec(memory_space=pltpu.VMEM)
SMEM = pl.BlockSpec(memory_space=pltpu.SMEM)
MIB = 2**20


class Group:
    def __init__(self, axis):
        ctx, fsdp = lax.axis_index("ctx"), lax.axis_index("fsdp")
        self.axis, self.ctx, self.fsdp = axis, ctx, fsdp
        self.core = lax.rem(ctx, 2)
        self.me = lax.div(ctx, 2) if axis == "ctx" else fsdp
        self.ring, self.pair = lax.rem(self.me, 4), lax.div(self.me, 4)

    def member(self, step, flip):
        pair = 1 - self.pair if flip else self.pair
        return pair * 4 + lax.rem(self.ring + (step + 4), 4)

    def device(self, step, flip):
        member = self.member(step, flip)
        if self.axis == "ctx":
            return (member * 2 + self.core, self.fsdp)
        return (self.ctx, member)

    def neighbours(self):
        return [self.device(1, 0), self.device(-1, 0), self.device(0, 1)]


def other_core(group):
    return (group.ctx + 1 - 2 * group.core, group.fsdp)


def barrier(devices):
    semaphore = pltpu.get_barrier_semaphore()
    for device in devices:
        pl.semaphore_signal(semaphore, inc=1, device_id=device, device_id_type=MESH)
    pl.semaphore_wait(semaphore, len(devices))


def remote(source, target, sems, slot, device):
    return pltpu.make_async_remote_copy(
        src_ref=source,
        dst_ref=target,
        send_sem=sems[0].at[slot],
        recv_sem=sems[1].at[slot],
        device_id=device,
        device_id_type=MESH,
    )


GATHER = (
    (1, 0, (0, 0), 0, 2, None),
    (-1, 0, (0, 0), 0, 2, None),
    (0, 1, (0, 0), 2, 4, None),
    (1, 0, (0, 0), 2, 4, None),
    (-1, 0, (0, 0), 2, 4, None),
    (0, 1, (0, 0), 0, 2, None),
    (1, 0, (-1, 0), 0, 1, 0),
    (-1, 0, (1, 0), 1, 2, 1),
    (0, 1, (-1, 0), 0, 2, 0),
    (0, 1, (1, 0), 0, 2, 1),
    (0, 1, (2, 0), 0, 1, 6),
    (0, 1, (2, 0), 1, 2, 7),
    (1, 0, (0, 1), 2, 4, 2),
    (-1, 0, (0, 1), 2, 4, 2),
    (1, 0, (-1, 0), 2, 3, 3),
    (-1, 0, (1, 0), 3, 4, 4),
    (1, 0, (-1, 1), 2, 3, 12),
    (-1, 0, (1, 1), 3, 4, 13),
)
GATHER_ORDER = (0, 1, 2, 3, 4, 6, 7, 12, 13, 5, 8, 14, 15, 9, 10, 16, 17, 11)
GATHER_SLOTS = len(GATHER)


def gather(group, view, sems, arrived=None, own=None, halves=False):
    started = []

    def start(slot):
        step, flip, block, a, b, _ = GATHER[slot]

        def copy():
            ref = view(group.member(*block), a, b)
            source = own(a, b) if own and block == (0, 0) else ref
            return remote(source, ref, sems, slot, group.device(step, flip))

        copy().start()
        started.append(copy)

    if halves:
        for slot in (0, 1, 5):
            start(slot)
        yield
        for slot in (2, 3, 4):
            start(slot)
    else:
        for slot in range(6):
            start(slot)
    if arrived:
        arrived((0, 0), 0, 4)
    for slot in GATHER_ORDER:
        step, flip, block, a, b, _ = GATHER[slot]
        yield
        source = (block[0] - step, block[1] ^ flip)
        ref = view(group.member(*source), a, b)
        remote(ref, ref, sems, slot, group.device(step, flip)).wait_recv()
        for later in range(GATHER_SLOTS):
            if GATHER[later][5] == slot:
                start(later)
        if arrived:
            arrived(source, a, b)
    for copy in started:
        copy().wait_send()


SCATTER_SLOTS = 23
HOLD = 7


def add_into(target, *sources):
    total = target[...].astype(F32)
    for source in sources:
        total = total + source[...].astype(F32)
    target[...] = total.astype(target.dtype)


def scatter(group, part, quarters, hold, result, sems, pair_first=True, prepare=None):
    started = []

    def held(k, a, b):
        return quarters(hold.at[k], a, b)

    def start(slot, source, step, flip, k, a, b):
        def copy():
            return remote(source(), held(k, a, b), sems, slot, group.device(step, flip))

        copy().start()
        started.append(copy)

    prepared = []

    def ready(block):
        if prepare and block not in prepared:
            prepared.append(block)
            prepare(*block)

    def send_part(slot, block, step, flip, k, a, b):
        ready(block)
        start(slot, lambda: part(*block, a, b), step, flip, k, a, b)

    def send_held(slot, source, step, flip, k, a, b):
        start(slot, lambda: held(source, a, b), step, flip, k, a, b)

    def wait(slot, k, a, b):
        ref = held(k, a, b)
        remote(ref, ref, sems, slot, group.device(0, 1)).wait_recv()

    if pair_first:
        send_part(0, (2, 1), 0, 1, 0, 0, 2)
    send_part(10, (2, 1), 1, 0, 0, 2, 3)
    send_part(11, (2, 1), -1, 0, 0, 3, 4)
    if pair_first:
        send_part(1, (1, 1), 0, 1, 1, 0, 2)
        send_part(2, (-1, 1), 0, 1, 2, 0, 2)
    send_part(16, (2, 0), 1, 0, 3, 2, 3)
    send_part(17, (2, 0), -1, 0, 3, 3, 4)
    send_part(12, (1, 1), 1, 0, 1, 3, 4)
    send_part(13, (-1, 1), -1, 0, 2, 2, 3)
    send_part(18, (1, 0), 1, 0, 4, 3, 4)
    send_part(19, (-1, 0), -1, 0, 5, 2, 3)
    if pair_first:
        send_part(3, (0, 1), 0, 1, 3, 0, 2)
    ready((0, 1))
    ready((0, 0))
    yield
    wait(10, 0, 2, 3)
    add_into(held(0, 2, 3), part(1, 1, 2, 3))
    send_held(14, 0, 1, 0, 1, 2, 3)
    wait(11, 0, 3, 4)
    add_into(held(0, 3, 4), part(-1, 1, 3, 4))
    send_held(15, 0, -1, 0, 2, 3, 4)
    if pair_first:
        yield
        wait(0, 0, 0, 2)
        add_into(held(0, 0, 2), part(2, 0, 0, 2))
        send_held(4, 0, 1, 0, 4, 0, 1)
        send_held(5, 0, -1, 0, 4, 1, 2)
    yield
    wait(16, 3, 2, 3)
    add_into(held(3, 2, 3), part(1, 0, 2, 3))
    send_held(20, 3, 1, 0, 4, 2, 3)
    wait(17, 3, 3, 4)
    add_into(held(3, 3, 4), part(-1, 0, 3, 4))
    send_held(21, 3, -1, 0, 5, 3, 4)
    if pair_first:
        yield
        wait(1, 1, 0, 2)
        add_into(held(1, 0, 2), part(1, 0, 0, 2))
        send_held(6, 1, 1, 0, 5, 1, 2)
    yield
    wait(12, 1, 3, 4)
    wait(14, 1, 2, 3)
    wait(13, 2, 2, 3)
    wait(15, 2, 3, 4)
    add_into(held(1, 2, 4), held(2, 2, 4), part(0, 1, 2, 4))
    send_held(22, 1, 0, 1, 6, 2, 4)
    if pair_first:
        yield
        wait(2, 2, 0, 2)
        add_into(held(2, 0, 2), part(-1, 0, 0, 2))
        send_held(8, 2, -1, 0, 6, 0, 1)
        yield
        wait(4, 4, 0, 1)
        add_into(held(1, 0, 1), held(4, 0, 1))
        send_held(7, 1, 1, 0, 5, 0, 1)
        wait(5, 4, 1, 2)
        add_into(held(2, 1, 2), held(4, 1, 2))
        send_held(9, 2, -1, 0, 6, 1, 2)
        yield
        wait(3, 3, 0, 2)
        wait(6, 5, 1, 2)
        wait(8, 6, 0, 1)
        wait(7, 5, 0, 1)
        wait(9, 6, 1, 2)
        result(0, 2, [part(0, 0, 0, 2), held(3, 0, 2), held(5, 0, 2), held(6, 0, 2)])
    yield
    wait(18, 4, 3, 4)
    wait(20, 4, 2, 3)
    wait(19, 5, 2, 3)
    wait(21, 5, 3, 4)
    wait(22, 6, 2, 4)
    result(2, 4, [part(0, 0, 2, 4), held(4, 2, 4), held(5, 2, 4), held(6, 2, 4)])
    for copy in started:
        copy().wait_send()


def total_of(refs):
    total = refs[0][...].astype(F32)
    for ref in refs[1:]:
        total = total + ref[...].astype(F32)
    return total


def drain(*programs):
    programs = list(programs)
    while programs:
        programs = [p for p in programs if next(p, "end") != "end"]


def pairs(count):
    return [pltpu.SemaphoreType.DMA((count,)), pltpu.SemaphoreType.DMA((count,))]


def params(collective_id, mib):
    return pltpu.CompilerParams(
        collective_id=collective_id, has_side_effects=True, vmem_limit_bytes=mib * MIB
    )


ROW_CUTS = (0, 96, 192, 288, 400)


TILE = 2 * GROUP
TILES = SEQ_LEN // TILE
ITEMS = TILES + 1
KEYS, VALUES = slice(0, 128), slice(128, 256)
NT = (((1,), (1,)), ((), ()))
TN = (((0,), (0,)), ((), ()))


def dot(a, b, dims=(((1,), (0,)), ((), ()))):
    return lax.dot_general(a, b, dims, preferred_element_type=F32)


class Steps:
    def __init__(self, *programs):
        self.programs = list(programs)

    def take(self, count=1):
        for _ in range(count):
            self.programs = [p for p in self.programs if next(p, "end") != "end"]

    def at(self, j, plan):
        for iteration, count in plan:
            pl.when(j == iteration)(partial(self.take, count))

    def finish(self):
        drain(*self.programs)


class Copies:
    def __init__(self, sems):
        self.sems, self.made = sems, []

    def start(self, source, target):
        slot = len(self.made)

        def copy():
            return pltpu.make_async_copy(source(), target(), self.sems.at[slot])

        copy().start()
        self.made.append(copy)
        return slot

    def wait(self, *slots):
        for slot in slots:
            self.made[slot]().wait()
            self.made[slot] = None

    def finish(self):
        self.wait(*[slot for slot, copy in enumerate(self.made) if copy])


def chunk_of(i, size):
    return pl.ds(pl.multiple_of(i * size, size), size)


def turned(values, cosine, sine):
    lane = lax.rem(lax.broadcasted_iota(jnp.int32, (1, 128), 1), HEAD_DIM)
    swapped = jnp.where(lane < ROT // 2, -pltpu.roll(values, 128 - ROT // 2, 1), pltpu.roll(values, ROT // 2, 1))
    return values * cosine + swapped * sine


def cut_rows(ref, a, b):
    step = ref.shape[0] // 4
    return ref.at[pl.ds(step * a, step * (b - a)), :]


def rows_scatter(group, part_ref, out, arriving, hold, sems):
    cs, cr, send, recv = sems
    core, partner = group.core, other_core(group)

    def exchange():
        return remote(part_ref.at[1 - core], arriving, (cs, cr), 0, partner)

    exchange().start()
    yield
    exchange().wait()

    def one(i, carry):
        rows = pl.ds(pl.multiple_of(i * 32, 32), 32)
        arriving[rows, :] = (arriving[rows, :].astype(F32) + part_ref[core, rows, :].astype(F32)).astype(BF16)
        return carry

    lax.fori_loop(0, arriving.shape[0] // 32, one, 0)
    width, size = out.shape[1], out.shape[0] // 2

    def cut(ref, a, b):
        return ref.at[pl.ds(size * (a - 2), size * (b - a)), :]

    def part(step, flip, a, b):
        columns = pl.ds(pl.multiple_of(group.member(step, flip) * width, width), width)
        return arriving.at[pl.ds(size * (a - 2), size * (b - a)), columns]

    def result(a, b, refs):
        target = cut(out, a, b)
        target[...] = total_of(refs)

    yield from scatter(group, part, cut, hold, result, (send, recv), pair_first=False)


def peers(axis):
    ctx, fsdp = lax.axis_index("ctx"), lax.axis_index("fsdp")
    count = lax.axis_size(axis)
    if axis == "ctx":
        return [(lax.rem(ctx + offset, count), fsdp) for offset in range(1, count)]
    return [(ctx, lax.rem(fsdp + offset, count)) for offset in range(1, count)]


def sum_small(x_ref, out, hold, sems, devices):
    def copy(i):
        return remote(x_ref, hold.at[i], sems, i, devices[i])

    for i in range(len(devices)):
        copy(i).start()
    yield
    total = x_ref[...]
    for i in range(len(devices)):
        copy(i).wait_recv()
        total = total + hold[i]
    out[...] = total
    for i in range(len(devices)):
        copy(i).wait_send()


def reduce_one(group, source, target, hold, sems):
    rs, rr, gs, gr, cs, cr, ls = sems
    core, partner = group.core, other_core(group)
    rows, width = source.shape[0] // 8, source.shape[1]
    by_rows = rows % 64 == 0

    def quarters(ref, a, b):
        if by_rows:
            return ref.at[pl.ds(rows // 4 * a, rows // 4 * (b - a)), :]
        return ref.at[:, pl.ds(width // 4 * a, width // 4 * (b - a))]

    def part(step, flip, a, b):
        return quarters(source.at[chunk_of(group.member(step, flip), rows), :], a, b)

    def view(member, a, b):
        return quarters(target(core).at[chunk_of(member, rows), :], a, b)

    def own(a, b):
        return quarters(hold.at[HOLD - 1], a, b)

    def result(a, b, terms):
        place = own(a, b)
        place[...] = total_of(terms).astype(BF16)

    def keep():
        return pltpu.make_async_copy(own(0, 4), view(group.me, 0, 4), ls.at[0])

    copies = []

    def arrived(block, a, b):
        slot = len(copies)

        def copy():
            ref = view(group.member(*block), a, b)
            return remote(own(a, b) if block == (0, 0) else ref, ref, (cs, cr), slot, partner)

        copy().start()
        copies.append(copy)

    yield from scatter(group, part, quarters, hold, result, (rs, rr))
    keep().start()
    yield from gather(group, view, (gs, gr), arrived, own=own)
    yield
    keep().wait()
    for copy in copies:
        copy().wait()


def reduce_scratch(shape):
    return pltpu.VMEM((HOLD, shape[0] // 8, shape[1]), BF16)


def reduce_sems():
    return pairs(SCATTER_SLOTS) + pairs(GATHER_SLOTS) + pairs(GATHER_SLOTS + 1) + [pltpu.SemaphoreType.DMA((1,))]


STATES = 11


def state_of(j):
    late = lax.div(j + 7, 16)
    return j * (1 - late) + (9 + lax.rem(j, 2)) * late


FORWARD_PLAN = ((1, 1), (3, 1), (4, 1), (8, 1), (11, 1), (13, 1), (14, 1))
BACKWARD_PLAN = ((0, 1), (2, 1), (8, 3), (12, 2), (14, 2), (16, 2))
BRANCH_PLAN = ((2, 1), (5, 1), (8, 1), (12, 1))
OUT_PLAN = ((4, 2), (6, 2), (9, 2), (11, 1), (13, 2), (15, 5))
ROWS, LAST, EARLY, WEIGHTS, OUT = range(5)
TAIL_PLAN = (
    (ROWS, 1), (EARLY, 3), (EARLY, 2), (LAST, 3), (EARLY, 2), (LAST, 1), (ROWS, 1), (LAST, 1), (EARLY, 1), (LAST, 2), (ROWS, 1), (EARLY, 1),
    (LAST, 2), (ROWS, 1), (EARLY, 5), (LAST, 5), (EARLY, 4), (LAST, 4), (ROWS, 1),
)


def layer_kernel(
    order_ref, ids_ref, x_ref, dy_ref, vectors_ref, wq, wk, wv, wo, wi, wu,
    layer_out, input_out, vec_out, q_out, k_out, v_out, out_out, inner_out, outer_out,
    x_all, dy_all, normed, qkv_w, o_w, i_w, u_w, kv_all, inner, act, act_t, grad, ff, ffn, inner_part, outer_part, out_part,
    cos_ref, sin_ref, q_ref, cotangent_ref, begin_ref, unit_ref, inv_ref, inner_sum, slot_of,
    state_max, state_sum, state_acc, dkv_items, lse_ref, delta_ref, att_ref, dq_ref,
    arriving, branch_hold, sum_ref, arriving_back, back_hold, local_ref, inner_hold, outer_hold, q_hold, k_hold, v_hold, out_hold, keys_hold, own, pre,
    stats, stats_hold, stats_sum, vec, vec_hold,
    *sems,
):
    across, along = Group("ctx"), Group("fsdp")
    core, chip, fsdp, partner = across.core, across.me, along.me, other_core(across)
    rows, width = dy_ref.shape
    sems = list(sems)

    def sems_for(count):
        taken = sems[:count]
        del sems[:count]
        return taken

    xs, ds, ks, cs = sems_for(2), sems_for(2), sems_for(2), sems_for(2)
    copies = Copies(sems_for(1)[0])
    x_cuts = (0, 96, 192, 288, x_all.shape[0])

    def x_view(member, a, b):
        return x_all.at[pl.ds(x_cuts[a], x_cuts[b] - x_cuts[a]), chunk_of(member, width)]

    def dy_view(member, a, b):
        return dy_all.at[core, pl.ds(rows // 4 * a, rows // 4 * (b - a)), chunk_of(member, width)]

    copies.start(lambda: x_ref, lambda: x_all.at[pl.ds(0, rows), chunk_of(fsdp, width)])
    copies.start(lambda: dy_ref, lambda: dy_view(fsdp, 0, 4))
    for i, ref in enumerate((wq, wk, wv)):
        copies.start(lambda ref=ref: ref.at[:, chunk_of(core, 128)], lambda i=i: qkv_w.at[:, pl.ds(128 * i, 128)])
    copies.start(lambda: wi.at[:, chunk_of(core, 512)], lambda: i_w)
    copies.start(lambda: wu.at[chunk_of(core, 512), :], lambda: u_w)
    copies.start(lambda: wo.at[chunk_of(core, 128), :], lambda: o_w)
    def vector(i):
        return vectors_ref[:, 256 * i : 256 * i + 256]

    extra = jnp.concatenate([vector(0), vector(1), jnp.zeros((14, width), F32)], axis=0)
    x_all[rows:, chunk_of(fsdp, width)] = extra.astype(BF16)
    barrier(peers("ctx") + peers("fsdp"))
    copies.wait(0, 1)
    x_steps = Steps(gather(along, x_view, xs))
    x_steps.take()
    dy_steps = Steps(gather(along, dy_view, ds))

    lane = lax.rem(lax.broadcasted_iota(jnp.int32, (1, 128), 1), HEAD_DIM)
    left = lax.broadcasted_iota(jnp.int32, (1, 128), 1) < HEAD_DIM
    freqs = jnp.zeros((1, 128), F32)
    for i in range(ROT):
        freqs = jnp.where(lane == i, 10000.0 ** (-2.0 * (i % (ROT // 2)) / ROT), freqs)
    for slot in range(4):
        group = order_ref[chip * 4 + slot]
        position = (group * GROUP + lax.broadcasted_iota(jnp.int32, (GROUP, 128), 0)).astype(F32)
        angles = position * freqs
        place = slice(GROUP * slot, GROUP * slot + GROUP)
        cos_ref[place, :] = jnp.cos(angles)
        sin_ref[place, :] = jnp.sin(angles)
        column = lax.broadcasted_iota(jnp.int32, (1, TILE), 1)
        column = group * GROUP + jnp.where(column < GROUP, column, column - GROUP)
        begin = jnp.zeros((1, TILE), jnp.int32)
        for doc in range(1, DOCS):
            before = jnp.sum(jnp.where(ids_ref[...] < doc, 1, 0), axis=0, keepdims=True)
            before = jnp.sum(before, axis=1, keepdims=True)
            begin = jnp.where(before <= column, before, begin)
        begin_ref[slot] = begin

    def find(group, carry):
        place = 0
        for slot in range(1, GROUPS):
            apart = order_ref[slot] - group
            place = place + slot * (1 - jnp.minimum(apart * apart, 1))
        slot_of[group] = jnp.minimum(place, GROUPS - 1)
        return carry

    lax.fori_loop(0, GROUPS, find, 0)

    x_steps.take(9)
    dy_steps.take()
    x_steps.finish()
    gain, shift = x_all[rows : rows + 1, :].astype(F32), x_all[rows + 1 : rows + 2, :].astype(F32)

    def exchange(ref, i):
        half = ref.at[core, pl.ds(GROUP * i, GROUP), :]
        return remote(half, half, cs, 2 * (ref is dy_all) + i, partner)

    def norm(i, carry):
        place = chunk_of(i, 32)
        values = x_all[place, :].astype(F32)
        mean = jnp.mean(values, axis=1, keepdims=True)
        centered = values - mean
        inv = lax.rsqrt(jnp.mean(centered * centered, axis=1, keepdims=True) + EPS)
        normed[core, place, :] = (centered * inv * gain + shift).astype(BF16)
        unit_ref[place, :] = (x_all[place, chunk_of(fsdp, width)].astype(F32) - mean) * inv
        inv_ref[place, :] = inv
        return carry

    for i in range(2):
        lax.fori_loop(GROUP // 32 * i, GROUP // 32 * (i + 1), norm, 0)
        exchange(normed, i).start()
    copies.wait(2, 3, 4)
    dy_steps.take(3)

    def project(of):
        pre_rows = dot(normed[of], qkv_w[...])
        bias = [vectors_ref[:, pl.ds(pl.multiple_of(512 + 256 * i + 128 * core, 128), 128)] for i in range(3)]
        for half in range(2):
            slot, part_rows = 2 * of + half, slice(GROUP * half, GROUP * half + GROUP)
            cosine, sine = cos_ref[chunk_of(slot, GROUP), :], sin_ref[chunk_of(slot, GROUP), :]
            queries = turned(pre_rows[part_rows, :128] + bias[0], cosine, sine).astype(BF16)
            q_ref[slot] = (queries.astype(F32) * HEAD_DIM ** (-0.5)).astype(BF16)
            kv_all[4 * chip + slot, :, :128] = turned(pre_rows[part_rows, 128:256] + bias[1], cosine, sine).astype(BF16)
            kv_all[4 * chip + slot, :, 128:] = (pre_rows[part_rows, 256:] + bias[2]).astype(BF16)

    def both_cores(one, ref, between=None):
        def here():
            if between:
                between()
            for i in range(2):
                exchange(ref, i).wait()

        def loop(i, carry):
            pl.when(i == 1)(here)
            one(lax.rem(core + i, 2))
            return carry

        lax.fori_loop(0, 2, loop, 0)

    def kv_view(member, a, b):
        return kv_all.at[pl.ds(4 * member + lax.rem(a + 2 * core, 4), b - a)]

    kv_steps = Steps(gather(across, kv_view, ks, halves=True))
    both_cores(project, normed, kv_steps.take)
    kv_steps.take()
    dy_steps.take(6)
    copies.wait(5, 6, 7)

    inner_bias = vectors_ref[:, pl.ds(pl.multiple_of(1792 + 512 * core, 128), 512)]

    def feed(of, carry):
        value = dot(normed[of], i_w[...]) + inner_bias
        inner[chunk_of(of, rows), :] = value
        curve = jnp.tanh(GELU_A * (value + GELU_B * value * value * value))
        act[chunk_of(of, rows), :] = (0.5 * value * (1.0 + curve)).astype(BF16)
        return carry

    lax.fori_loop(0, 2, feed, 0)
    dy_steps.take(4)
    kv_steps.take(3)

    def feed_out(i, carry):
        block = chunk_of(i, 256)
        ff[:, :, block] = dot(act[...], u_w[:, block]).astype(BF16).reshape(2, rows, 256)
        return carry

    lax.fori_loop(0, 8, feed_out, 0)
    act_t[...] = act[...].T
    dy_steps.finish()
    for i in range(2):
        exchange(dy_all, i).start()
    kv_steps.take(2)
    inner_sum[...] = jnp.zeros_like(inner_sum)

    def gradients(of):
        dy_rows = dy_all[of]
        ag = dot(dy_rows, o_w[...], NT).astype(BF16)
        cotangent_ref[2 * of], cotangent_ref[2 * of + 1] = ag[:GROUP], ag[GROUP:]
        value = inner[chunk_of(of, rows), :]
        square = value * value
        curve = jnp.tanh(GELU_A * (value + GELU_B * square * value))
        slope = 0.5 * (1.0 + curve) + 0.5 * value * (1.0 - curve * curve) * (GELU_A * (1.0 + 3.0 * GELU_B * square))
        out = (dot(dy_rows, u_w[...], NT) * slope).astype(BF16)
        grad[chunk_of(of, rows), :] = out
        inner_sum[...] += jnp.sum(out.astype(F32), axis=0, keepdims=True)

    both_cores(gradients, dy_all)
    kv_steps.take(2)

    def outer_weights(i, carry):
        block = chunk_of(i, 256)
        outer_part[:, block] = dot(act_t[...], dy_all[:, :, block].reshape(2 * rows, 256)).astype(BF16)
        return carry

    lax.fori_loop(0, 8, outer_weights, 0)
    outer_program = reduce_one(across, outer_part, lambda c: outer_out.at[c], outer_hold, sems_for(7))
    inner_program = reduce_one(across, inner_part, lambda c: inner_out.at[:, chunk_of(c, 512)], inner_hold, sems_for(7))
    kv_steps.take(2)
    next(outer_program)

    def inner_weights(i, carry):
        block = chunk_of(i, 256)
        inner_part[block, :] = dot(normed[:, :, block].reshape(2 * rows, 256), grad[...], TN).astype(BF16)
        return carry

    lax.fori_loop(0, 8, inner_weights, 0)
    kv_steps.take(2)
    next(inner_program)

    kv_steps.finish()
    weights_steps = Steps(outer_program, inner_program)

    def bit(number):
        return jnp.minimum(jnp.maximum(number, 0), 1)

    def pair_facts(p):
        g0, g1 = order_ref[4 * chip + 2 * p], order_ref[4 * chip + 2 * p + 1]
        low, high = jnp.minimum(g0, g1), jnp.maximum(g0, g1)
        return low, high, bit(g0 - g1), lax.div(low, 2) + 1

    key_row = lax.broadcasted_iota(jnp.int32, (TILE, TILE), 0)
    column = lax.broadcasted_iota(jnp.int32, (1, TILE), 1)
    query_row = jnp.where(column < GROUP, column, column - GROUP)

    def item_facts(p, j):
        low, high, low_slot, count = pair_facts(p)
        second = bit(j - count + 1)
        tile = second * TILES + (1 - second) * (count - 1) - j
        slot = 2 * p + second * (1 - low_slot) + (1 - second) * low_slot
        position = (second * high + (1 - second) * low) * GROUP
        last = query_row + (position - tile * TILE)
        begin = begin_ref[slot] - tile * TILE
        allowed = (key_row <= last) & (key_row >= begin)
        keep = bit(j * (j - count) * (j - count)).astype(F32)
        return tile, slot, allowed, keep

    def keys_of(tile, lanes):
        return jnp.concatenate([kv_all[slot_of[2 * tile], :, lanes], kv_all[slot_of[2 * tile + 1], :, lanes]], axis=0)

    def stacked(rows):
        zero = jnp.zeros_like(rows)
        return jnp.concatenate([jnp.where(left, rows, zero), jnp.where(left, zero, rows)], axis=0)

    def unstacked(columns):
        rows = columns.T
        return jnp.where(left, rows[:GROUP], rows[GROUP:])

    def final_item(p, i):
        low, high, low_slot, count = pair_facts(p)
        is_low = low_slot if i else 1 - low_slot
        return count * is_low + 10 * (1 - is_low)

    for p in range(2):
        state_max[p, 0] = jnp.full((1, TILE), FLOOR, F32)
        state_sum[p, 0] = jnp.zeros((1, TILE), F32)
        state_acc[p, 0] = jnp.zeros((128, TILE), F32)

    def forward(j, carry):
        weights_steps.at(j, FORWARD_PLAN)
        now, after = state_of(j), state_of(j + 1)
        for p in range(2):
            tile, slot, allowed, keep = item_facts(p, j)
            scores = jnp.where(allowed, dot(keys_of(tile, KEYS), stacked(q_ref[slot]), NT), MASKED)
            old_max = state_max[p, now] * keep + FLOOR * (1.0 - keep)
            new_max = jnp.maximum(old_max, jnp.max(scores, axis=0, keepdims=True))
            weights = jnp.exp(scores - new_max)
            factor = jnp.exp(old_max - new_max)
            state_max[p, after] = new_max
            state_sum[p, after] = state_sum[p, now] * factor + jnp.sum(weights, axis=0, keepdims=True)
            state_acc[p, after] = state_acc[p, now] * factor + dot(keys_of(tile, VALUES), weights.astype(BF16), TN)
        return carry

    lax.fori_loop(0, ITEMS, forward, 0)

    for p in range(2):
        for i in range(2):
            item = final_item(p, i)
            slot = 2 * p + i
            total = state_sum[p, item]
            out = state_acc[p, item] / total
            lse_ref[slot] = state_max[p, item] + jnp.log(total)
            cotangent = stacked(cotangent_ref[slot].astype(F32)).T
            delta_ref[slot] = jnp.sum(cotangent * out, axis=0, keepdims=True)
            att_ref[slot] = unstacked(out).astype(BF16)

    def branches(i, carry):
        block = chunk_of(i, 256)
        attended = dot(att_ref[...].reshape(2 * rows, 128), o_w[:, block]).reshape(2, rows, 256)
        ff[:, :, block] = (ff[:, :, block].astype(F32) + attended).astype(BF16)
        return carry

    lax.fori_loop(0, 8, branches, 0)
    branch_steps = Steps(rows_scatter(along, ff, sum_ref, arriving, branch_hold, sems_for(4)))
    branch_steps.take()

    def out_weights(i, carry):
        block = chunk_of(i, 256)
        out_part[:, block] = dot(att_ref[...].reshape(2 * rows, 128), dy_all[:, :, block].reshape(2 * rows, 256), TN).astype(BF16)
        return carry

    lax.fori_loop(0, 8, out_weights, 0)
    out_steps = Steps(reduce_one(across, out_part, lambda c: out_out.at[c], out_hold, sems_for(7)))
    out_steps.take()

    for p in range(2):
        state_acc[p, 0] = jnp.zeros((128, TILE), F32)

    def backward(j, carry):
        weights_steps.at(j, BACKWARD_PLAN)
        branch_steps.at(j, BRANCH_PLAN)
        out_steps.at(j, OUT_PLAN)
        now, after = state_of(j), state_of(j + 1)
        for p in range(2):
            tile, slot, allowed, keep = item_facts(p, j)
            queries, cotangent = stacked(q_ref[slot]), stacked(cotangent_ref[slot])
            scores = dot(keys_of(tile, KEYS), queries, NT)
            probs = jnp.where(allowed, jnp.exp(scores - lse_ref[slot]), 0.0)
            prob_grad = dot(keys_of(tile, VALUES), cotangent, NT)
            score_grad = (probs * (prob_grad - delta_ref[slot])).astype(BF16)
            state_acc[p, after] = state_acc[p, now] * keep + dot(keys_of(tile, KEYS), score_grad, TN)
            key_grad = dot(score_grad, queries).astype(BF16)
            value_grad = dot(probs.astype(BF16), cotangent).astype(BF16)
            for half in range(2):
                rows = slice(GROUP * half, GROUP * half + GROUP)
                dkv_items[p, j, half, :, :128] = key_grad[rows]
                dkv_items[p, j, half, :, 128:] = value_grad[rows]
        return carry

    lax.fori_loop(0, ITEMS, backward, 0)

    for p in range(2):
        for i in range(2):
            dq_ref[2 * p + i] = unstacked(state_acc[p, final_item(p, i)])

    counts = [pair_facts(p)[3] for p in range(2)]

    def collect(s, carry):
        group = order_ref[s]
        tile, half = lax.div(group, 2), lax.rem(group, 2)
        total = jnp.zeros((GROUP, 256), F32)
        for p in range(2):
            low_item = dkv_items[p, jnp.maximum(counts[p] - 1 - tile, 0), half].astype(F32)
            high_item = dkv_items[p, jnp.maximum(TILES - tile, counts[p]), half].astype(F32)
            total = total + low_item * bit(counts[p] - tile).astype(F32)
            total = total + high_item * bit(TILES - tile - counts[p] + 1).astype(F32)
        kv_all[s] = total.astype(BF16)
        return carry

    def collect_member(step, flip):
        start = 4 * across.member(step, flip)
        lax.fori_loop(start, start + 4, collect, 0)

    def part(step, flip, a, b):
        return kv_all.at[pl.ds(4 * across.member(step, flip) + a, b - a)]

    def cut_groups(ref, a, b):
        return ref.at[pl.ds(a, b - a)]

    def result(a, b, refs):
        own[a:b] = total_of(refs)

    keys_steps = Steps(scatter(across, part, cut_groups, keys_hold, result, sems_for(2), prepare=collect_member))
    keys_steps.take()
    branch_steps.finish()
    layer_sum = x_all[:rows, chunk_of(fsdp, width)].astype(F32) + sum_ref[...]
    layer_out[...] = (layer_sum + vector(5) + vector(6)).astype(BF16)
    for slot in range(4):
        place = slice(GROUP * slot, GROUP * slot + GROUP)
        turned_back = turned(dq_ref[slot] * HEAD_DIM ** (-0.5), cos_ref[place, :], -sin_ref[place, :])
        pre[place, :128] = turned_back.astype(BF16)
    q_part, k_part, v_part = [inner_part.at[:, pl.ds(128 * i, 128)] for i in range(3)]

    def query_weights(i, carry):
        block = chunk_of(i, 256)
        q_part[block, :] = dot(normed[:, :, block].reshape(2 * rows, 256), pre[:, :128], TN).astype(BF16)
        return carry

    lax.fori_loop(0, 8, query_weights, 0)
    keys_steps.take()

    early_steps = Steps(reduce_one(across, q_part, lambda c: q_out.at[:, chunk_of(c, 128)], q_hold, sems_for(7)))
    keys_steps.take()
    early_steps.take()
    def feed_back(i, carry):
        block = chunk_of(i, 256)
        ffn[:, :, block] = dot(grad[...], i_w[block, :], NT).astype(BF16).reshape(2, rows, 256)
        return carry

    lax.fori_loop(0, 8, feed_back, 0)
    weights_steps.take(2)
    keys_steps.take(2)
    weights_steps.take(2)
    keys_steps.take(2)
    weights_steps.take(2)
    keys_steps.finish()
    for slot in range(4):
        place = slice(GROUP * slot, GROUP * slot + GROUP)
        turned_back = turned(own[slot, :, :128], cos_ref[place, :], -sin_ref[place, :])
        pre[place, 128:256] = turned_back.astype(BF16)
        pre[place, 256:] = own[slot, :, 128:].astype(BF16)

    def key_weights(i, carry):
        block = chunk_of(i, 256)
        total = dot(normed[:, :, block].reshape(2 * rows, 256), pre[:, 128:], TN).astype(BF16)
        k_part[block, :] = total[:, :128]
        v_part[block, :] = total[:, 128:]
        return carry

    def normed_grad(of):
        def one(i, carry):
            part_rows, columns = chunk_of(lax.div(i, 4), GROUP), chunk_of(lax.rem(i, 4), 512)
            from_rows = chunk_of(2 * of + lax.div(i, 4), GROUP)
            total = ffn[of, part_rows, columns].astype(F32) + dot(pre[from_rows, :], qkv_w[columns, :], NT)
            ffn[of, part_rows, columns] = total.astype(BF16)
            return carry

        lax.fori_loop(0, 8, one, 0)

    normed_grad(1 - core)
    rows_steps = Steps(rows_scatter(along, ffn, local_ref, arriving_back, back_hold, sems_for(4)))
    rows_steps.take()
    lax.fori_loop(0, 8, key_weights, 0)
    last_steps = Steps(
        reduce_one(across, k_part, lambda c: k_out.at[:, chunk_of(c, 128)], k_hold, sems_for(7)),
        reduce_one(across, v_part, lambda c: v_out.at[:, chunk_of(c, 128)], v_hold, sems_for(7)),
    )
    last_steps.take()
    normed_grad(core)
    for programs, count in TAIL_PLAN:
        (rows_steps, last_steps, early_steps, weights_steps, out_steps)[programs].take(count)
    rows_steps.finish()

    whole = local_ref[...]
    unit = unit_ref[...]
    scaled = whole * vector(0)
    lane = lax.broadcasted_iota(jnp.int32, (1, 128), 1)
    first = jnp.sum(scaled, axis=1, keepdims=True)
    second = jnp.sum(scaled * unit, axis=1, keepdims=True)
    stats[...] = jnp.where(lane == 0, first, jnp.where(lane == 1, second, 0.0)).T[:8]
    stats_steps = Steps(sum_small(stats, stats_sum, stats_hold, sems_for(2), peers("fsdp")))
    stats_steps.take()
    cotangent = dy_all[core, :, chunk_of(fsdp, width)].astype(F32)
    vec[...] = jnp.zeros_like(vec)
    vec[0:1, :] = jnp.sum(whole * unit, axis=0, keepdims=True)
    vec[1:2, :] = jnp.sum(whole, axis=0, keepdims=True)
    vec[2:3, :] = jnp.sum(cotangent, axis=0, keepdims=True)
    for i in range(3):
        vec[3 + i : 4 + i, chunk_of(core, 128)] = jnp.sum(pre[:, 128 * i : 128 * i + 128].astype(F32), axis=0, keepdims=True)
    for i in range(2):
        vec[pl.ds(6 + 2 * core + i, 1), :] = inner_sum[:, 256 * i : 256 * i + 256]
    vec_steps = Steps(sum_small(vec, vec_out, vec_hold, sems_for(2), peers("ctx")))
    vec_steps.take()
    early_steps.take(9)
    weights_steps.finish()
    out_steps.finish()
    stats_steps.finish()
    back = jnp.concatenate([stats_sum[...], jnp.zeros((120, rows), F32)], axis=0).T * (1.0 / 2048)
    input_out[...] = cotangent + inv_ref[...] * (scaled - back[:, 0:1] - unit * back[:, 1:2])
    vec_steps.finish()
    weights_steps.finish()
    early_steps.finish()
    last_steps.finish()
    assert not sems


def layer(order, ids, x, dy, vectors, weights):
    rows, width = dy.shape
    wide, both = weights[0].shape[0], 2 * rows

    def bf(*shape):
        return pltpu.VMEM(shape, BF16)

    def f32(*shape):
        return pltpu.VMEM(shape, F32)

    def of(kind, *shape):
        return jax.ShapeDtypeStruct(shape, kind)

    return pl.pallas_call(
        layer_kernel,
        out_shape=[
            of(BF16, rows, width),
            of(F32, rows, width),
            of(F32, 16, width),
            of(BF16, wide, width),
            of(BF16, wide, width),
            of(BF16, wide, width),
            of(BF16, 2, 128, wide),
            of(BF16, wide, 1024),
            of(BF16, 2, 512, wide),
        ],
        in_specs=[SMEM, VMEM, ANY, ANY, VMEM] + [ANY] * len(weights),
        out_specs=[VMEM] * 3 + [ANY] * 6,
        scratch_shapes=[
            bf(rows + 16, wide),
            bf(2, rows, wide),
            bf(2, rows, wide),
            bf(wide, 384),
            bf(128, wide),
            bf(wide, 512),
            bf(512, wide),
            bf(GROUPS, GROUP, 256),
            f32(both, 512),
            bf(both, 512),
            bf(512, both),
            bf(both, 512),
            bf(2, rows, wide),
            bf(2, rows, wide),
            bf(wide, 512),
            bf(512, wide),
            bf(128, wide),
            f32(both, 128),
            f32(both, 128),
            bf(4, GROUP, 128),
            bf(4, GROUP, 128),
            pltpu.VMEM((4, 1, TILE), jnp.int32),
            f32(rows, width),
            f32(rows, 1),
            f32(1, 512),
            pltpu.SMEM((GROUPS,), jnp.int32),
            f32(2, STATES, 1, TILE),
            f32(2, STATES, 1, TILE),
            f32(2, STATES, 128, TILE),
            bf(2, ITEMS, 2, GROUP, 256),
            f32(4, 1, TILE),
            f32(4, 1, TILE),
            bf(4, GROUP, 128),
            f32(4, GROUP, 128),
            bf(rows, wide),
            bf(HOLD, rows, width),
            f32(rows, width),
            bf(rows, wide),
            bf(HOLD, rows, width),
            f32(rows, width),
            reduce_scratch((wide, 512)),
            reduce_scratch((512, wide)),
            reduce_scratch((wide, 128)),
            reduce_scratch((wide, 128)),
            reduce_scratch((wide, 128)),
            reduce_scratch((128, wide)),
            bf(HOLD, 4, GROUP, 256),
            f32(4, GROUP, 256),
            bf(both, 384),
            f32(8, rows),
            f32(7, 8, rows),
            f32(8, rows),
            f32(16, width),
            f32(15, 16, width),
        ]
        + pairs(GATHER_SLOTS) * 3
        + pairs(4)
        + [pltpu.SemaphoreType.DMA((8,))]
        + reduce_sems() * 2
        + pairs(1)
        + pairs(SCATTER_SLOTS)
        + reduce_sems()
        + pairs(SCATTER_SLOTS)
        + reduce_sems()
        + pairs(1)
        + pairs(SCATTER_SLOTS)
        + reduce_sems() * 2
        + pairs(7)
        + pairs(15),
        compiler_params=params(0, 63),
        name="layer",
    )(order, ids, x, dy, vectors, *weights)


def body(
    layer_input,
    norm_gain,
    norm_bias,
    query_weight,
    query_bias,
    key_weight,
    key_bias,
    value_weight,
    value_bias,
    out_weight,
    out_bias,
    inner_weight,
    inner_bias,
    outer_weight,
    outer_bias,
    output_grad,
    group_order,
    sequence_ids,
):
    parts = [norm_gain, norm_bias, query_bias, key_bias, value_bias, out_bias, outer_bias, inner_bias]
    ends = [sum(p.shape[0] for p in parts[: i + 1]) for i in range(len(parts))]
    vectors = sum(jnp.pad(p.astype(F32), (end - p.shape[0], ends[-1] - end)) for p, end in zip(parts, ends))
    layer_output, input_grad, vectors, query_grad, key_grad, value_grad, out_grad, inner_w_grad, outer_w_grad = layer(
        group_order,
        sequence_ids.reshape(-1, 128),
        layer_input,
        output_grad,
        vectors[None],
        [query_weight, key_weight, value_weight, out_weight, inner_weight, outer_weight],
    )

    return (
        layer_output,
        input_grad,
        vectors[0],
        vectors[1],
        query_grad.astype(F32),
        vectors[3],
        key_grad.astype(F32),
        vectors[4],
        value_grad.astype(F32),
        vectors[5],
        out_grad.reshape(256, 2048).astype(F32),
        vectors[2],
        inner_w_grad.astype(F32),
        vectors[6:10].reshape(1024),
        outer_w_grad.reshape(1024, 2048).astype(F32),
        vectors[2],
    )


def solution(mesh):
    in_specs = (
        P("ctx", "fsdp"),
        P("fsdp"),
        P("fsdp"),
        P(None, "fsdp"),
        P("fsdp"),
        P(None, "fsdp"),
        P("fsdp"),
        P(None, "fsdp"),
        P("fsdp"),
        P("fsdp", None),
        P("fsdp"),
        P(None, "fsdp"),
        P("fsdp"),
        P("fsdp", None),
        P("fsdp"),
        P("ctx", "fsdp"),
        P(),
        P(),
    )
    out_specs = (
        P("ctx", "fsdp"),
        P("ctx", "fsdp"),
        P("fsdp"),
        P("fsdp"),
        P(None, "fsdp"),
        P("fsdp"),
        P(None, "fsdp"),
        P("fsdp"),
        P(None, "fsdp"),
        P("fsdp"),
        P("fsdp", None),
        P("fsdp"),
        P(None, "fsdp"),
        P("fsdp"),
        P("fsdp", None),
        P("fsdp"),
    )
    return jax.shard_map(body, mesh=mesh, in_specs=in_specs, out_specs=out_specs, check_vma=False)
```
